256 devices in a mesh: dom: 64 (over z, x, core), feat: 4 (over y).
Axes of the slice: x: 4, y: 4, z: 8, core: 2. Of those that a mesh axis runs over, the one named last changes fastest.
Arguments:
- feats: bfloat16 [16384, 1024], P('dom', 'feat'), may hold values from -16 to 16
- weight: bfloat16 [1024, 1024], P('feat', 'dom'), may hold values from -0.1875 to 0.1875
- bias: float32 [1024], P('feat'), may hold values from -3 to 3
- tile_values: bfloat16 [8192, 128, 128], P('dom'), may hold values from 0 to 10, as said below
- tile_rows: int32 [8192], P('dom'), may hold values from 0 to 1
- tile_cols: int32 [8192], P('dom'), may hold values from 0 to 127
- tile_live: int32 [64], P('dom'), may hold values from 0 to 128, as said below
- cotangent: bfloat16 [16384, 1024], P('dom', 'feat'), may hold values from -6 to 6
Outputs:
- output: bfloat16 [16384, 1024], P('dom', 'feat')
- feats_grad: bfloat16 [16384, 1024], P('dom', 'feat')
- weight_grad: float32 [1024, 1024], P('feat', 'dom')
- bias_grad: float32 [1024], P('feat')
The draws below stay inside these ranges and needn't reach their ends.
Inputs may be any that keep to these rules, and one draw needn't show every extreme that they name: `tile_live`: device d and device d + 32 have at most 128 live slots together. Live slots are a device's first ones. `tile_values`: nonnegative edge weights.
All inputs are finite; a program needn't handle non-finite values.
Results may differ from the reference program's by a relative error of at most 0.0061.
Values may be sent and summed in bfloat16 or wider, within the bound.
No kernel may reach another device: no remote copies, remote signals or barrier semaphores. Data moves between devices by JAX's collectives and lax.ppermute only.
A program may use at most 128 MiB of HBM per device.

```python
import jax
import jax.numpy as jnp
from jax import lax

HID = 1024
BLK = 128
RB_DEV = 2
TILE_CAP = 128
N_ROWBLK = 128
NODES = 16384
TILES = 8192
N_DOM = 64


def draw_tile_values(key, part):
    key = jax.random.fold_in(key, 7)
    mask_key, value_key = jax.random.split(key, 2)
    shape = (TILES, BLK, BLK)
    present = jax.random.uniform(mask_key, shape, dtype=jnp.float32) < 1.5 / BLK
    values = jax.random.uniform(value_key, shape, dtype=jnp.float32, minval=0.25, maxval=1.0)
    return jnp.where(present, values, 0.0).astype(jnp.bfloat16)


def draw_tile_live(key, part):
    key = jax.random.fold_in(key, 11)
    heavy_key, light_key, flip_key = jax.random.split(key, 3)
    pair_count = N_DOM // 2
    heavy = jax.random.randint(heavy_key, (pair_count,), TILE_CAP // 2, TILE_CAP + 1)
    heavy = jnp.where(jnp.arange(pair_count) == 0, TILE_CAP, heavy)
    light = jax.random.randint(light_key, (pair_count,), 0, TILE_CAP - heavy + 1)
    flip = jax.random.randint(flip_key, (pair_count,), 0, 2)
    first_half = jnp.where(flip == 1, heavy, light)
    second_half = jnp.where(flip == 1, light, heavy)
    return jnp.concatenate([first_half, second_half]).astype(jnp.int32)


def plant(result, own_key, smallest, largest):
    place = [jax.random.randint(jax.random.fold_in(own_key, axis), (), 0, length) for axis, length in enumerate(result.shape)]
    widest = result.shape.index(max(result.shape))
    next_to = place[:widest] + [(place[widest] + 1) % result.shape[widest]] + place[widest + 1:]
    return result.at[tuple(place)].set(smallest).at[tuple(next_to)].set(largest)


def shard_levels(key, shape, shards, least, high):
    def one(axis_at, parts):
        draws = jax.random.uniform(jax.random.fold_in(jax.random.fold_in(key, 6), axis_at), (parts,), jnp.float32, least / len(shards), high / len(shards))
        return jnp.repeat(jnp.exp(draws), shape[axis_at] // parts).reshape((-1,) + (1,) * (len(shape) - axis_at - 1))

    gain = one(*shards[0])
    for cut in shards[1:]:
        gain = gain * one(*cut)
    return gain


def gaussian(rng, shape, width, reach, pieces=(), held_as=jnp.bfloat16):
    result = jax.random.normal(rng, shape, jnp.float32) * width
    if len(pieces) > 0:
        result = shard_levels(rng, shape, pieces, -0.22, 0.18) * result
    return jnp.clip(result, min=-reach, max=reach).astype(held_as)


def setup_inputs(seed: int = 0) -> dict:
    streams_of = jax.random.split(jax.random.key(seed), 9)
    feats = gaussian(streams_of[0], (NODES, HID), 4.0, 16.0, ((0, 64), (1, 4)))
    weight = gaussian(streams_of[1], (HID, HID), HID ** -0.5, 0.1875, ((0, 4), (1, 64)))
    bias = gaussian(streams_of[2], (HID,), 0.5, 3.0, ((0, 4),), jnp.float32)
    tile_values = draw_tile_values(jax.random.fold_in(streams_of[8], 71), 0)
    tile_rows = plant(jax.random.randint(streams_of[4], (TILES,), 0, RB_DEV), jax.random.fold_in(streams_of[4], 1), 0, RB_DEV - 1).astype(jnp.int32)
    tile_cols = plant(jax.random.randint(streams_of[5], (TILES,), 0, N_ROWBLK), jax.random.fold_in(streams_of[5], 1), 0, N_ROWBLK - 1).astype(jnp.int32)
    tile_live = draw_tile_live(jax.random.fold_in(streams_of[8], 71), 0)
    cotangent = gaussian(streams_of[7], (NODES, HID), 1.0, 6.0, ((0, 64), (1, 4)))
    return dict(feats=feats, weight=weight, bias=bias, tile_values=tile_values, tile_rows=tile_rows, tile_cols=tile_cols, tile_live=tile_live, cotangent=cotangent)


def silu_parts(hidden):
    gate_value = jax.nn.sigmoid(hidden)
    return hidden * gate_value, gate_value * (1.0 + hidden * (1.0 - gate_value))


def reference(feats, weight, bias, tile_values, tile_rows, tile_cols, tile_live, cotangent):
    slot_index = jnp.arange(TILES, dtype=jnp.int32)
    owner = slot_index // TILE_CAP
    live = (slot_index % TILE_CAP) < tile_live[owner]
    row_block = (owner * RB_DEV + tile_rows).astype(jnp.int32)
    row_ids = jnp.where(live, row_block, N_ROWBLK).astype(jnp.int32)
    col_ids = jnp.where(live, tile_cols, N_ROWBLK).astype(jnp.int32)
    owners = jnp.arange(N_DOM, dtype=jnp.int32)
    feat_blocks = feats.astype(jnp.float32).reshape(N_ROWBLK, BLK, HID)

    def forward_step(carry, owner_id):
        sums, degs = carry
        first = (owner_id * TILE_CAP).astype(jnp.int32)
        values = lax.dynamic_slice_in_dim(tile_values, first, TILE_CAP, 0).astype(jnp.float32)
        columns = lax.dynamic_slice_in_dim(tile_cols, first, TILE_CAP, 0)
        segment_ids = lax.dynamic_slice_in_dim(row_ids, first, TILE_CAP, 0)
        picked = jnp.take(feat_blocks, columns, axis=0)
        terms = jnp.einsum("sij,sjf->sif", values, picked)
        sums = sums + jax.ops.segment_sum(terms, segment_ids, num_segments=N_ROWBLK)
        degs = degs + jax.ops.segment_sum(jnp.sum(values, axis=2), segment_ids, num_segments=N_ROWBLK)
        return (sums, degs), None

    start_carry = (jnp.zeros((N_ROWBLK, BLK, HID), jnp.float32), jnp.zeros((N_ROWBLK, BLK), jnp.float32))
    (sums, degs), _ = lax.scan(forward_step, start_carry, owners)
    degree = 1.0 + degs.reshape(NODES, 1)
    mixed = ((feats.astype(jnp.float32) + sums.reshape(NODES, HID)) / degree).astype(jnp.bfloat16)
    hidden = jnp.dot(mixed, weight, preferred_element_type=jnp.float32) + bias
    activated, slope = silu_parts(hidden)
    output = activated.astype(jnp.bfloat16)
    dz_full = cotangent.astype(jnp.float32) * slope
    bias_grad = jnp.sum(dz_full, axis=0)
    dz = dz_full.astype(jnp.bfloat16)
    weight_grad = jnp.dot(mixed.T, dz, preferred_element_type=jnp.float32)
    dmixed = jnp.dot(dz, weight.T, preferred_element_type=jnp.float32)
    scaled = (dmixed / degree).astype(jnp.bfloat16)
    steady = lax.optimization_barrier(scaled)
    grad_blocks = steady.astype(jnp.float32).reshape(N_ROWBLK, BLK, HID)

    def backward_step(total, owner_id):
        first = (owner_id * TILE_CAP).astype(jnp.int32)
        values = lax.dynamic_slice_in_dim(tile_values, first, TILE_CAP, 0).astype(jnp.float32)
        sources = lax.dynamic_slice_in_dim(row_block, first, TILE_CAP, 0)
        segment_ids = lax.dynamic_slice_in_dim(col_ids, first, TILE_CAP, 0)
        picked = jnp.take(grad_blocks, sources, axis=0)
        terms = jnp.einsum("sji,sjf->sif", values, picked)
        return total + jax.ops.segment_sum(terms, segment_ids, num_segments=N_ROWBLK), None

    column_sum, _ = lax.scan(backward_step, jnp.zeros((N_ROWBLK, BLK, HID), jnp.float32), owners)
    feats_grad = (steady.astype(jnp.float32) + column_sum.reshape(NODES, HID)).astype(jnp.bfloat16)
    return output, feats_grad, weight_grad, bias_grad
```

```python
import functools

import jax
import jax.numpy as jnp
from jax import lax
from jax.experimental import pallas as pl
from jax.experimental.pallas import tpu as pltpu
from jax.sharding import PartitionSpec as P

F32 = jnp.float32
BF16 = jnp.bfloat16
NZ, NX, NY = 8, 4, 4
BLK = 128
SLOTS = 128
WIDTH = 256
W_ROWS = 16
UNROLL = 4
AG_GROUPS = ((0, 1, 7, 2), (6, 3, 5, 4))
RS_GROUPS = ((4, 5, 3, 6), (2, 7, 1, 0))
AGB_GROUPS = ((0, 1), (3, 2))
RSB_GROUPS = ((2, 1), (3, 0))
MIB = 1 << 20


def chip_shift(value, dz=0, dx=0):
    pairs = []
    for z in range(NZ):
        for x in range(NX):
            for c in range(2):
                target = ((z + dz) % NZ * NX + (x + dx) % NX) * 2 + c
                pairs.append(((z * NX + x) * 2 + c, target))
    return lax.ppermute(value, "dom", pairs)


def swap(value, bit):
    return lax.ppermute(value, "dom", [(i, i ^ bit) for i in range(NZ * NX * 2)])


def y_shift(value, dy):
    return lax.ppermute(value, "feat", [(y, (y + dy) % NY) for y in range(NY)])


def smem():
    return pl.BlockSpec(memory_space=pltpu.SMEM)


def vmem():
    return pl.BlockSpec(memory_space=pltpu.VMEM)


def anywhere():
    return pl.BlockSpec(memory_space=pl.ANY)


def list_kernel(own, sib, place, count, slots, spots):
    core, x, z = place[0], place[1], place[2]
    for group in range(8):
        count[group] = 0

    def scan(meta, first_row, first_slot):
        def step(s, carry):
            column = meta[1, s]
            owner = column // 2
            group = (column % 2) * 4 + first_row + meta[0, s]

            @pl.when(owner % 2 == core)
            def _():
                chip = owner // 2
                at = count[group]
                slots[group, at] = first_slot + s
                spots[group, at] = ((x - chip % NX) & (NX - 1)) * NZ + ((z - chip // NX) & (NZ - 1))
                count[group] = at + 1

            return carry

        lax.fori_loop(0, meta[2, 0], step, 0)

    scan(own, 0, 0)
    scan(sib, 2, SLOTS)


def make_lists(own, sib, place):
    return pl.pallas_call(
        list_kernel,
        out_shape=(
            jax.ShapeDtypeStruct((8,), jnp.int32),
            jax.ShapeDtypeStruct((8, 2 * SLOTS), jnp.int32),
            jax.ShapeDtypeStruct((8, 2 * SLOTS), jnp.int32),
        ),
        in_specs=[smem()] * 3,
        out_specs=(smem(),) * 3,
    )(own, sib, place)


def forward_kernel(stream, spread, keep_weight, count, slots, spots, place, tiles, start, *rest):
    chunks = rest[: len(spread)]
    rest = rest[len(spread) :]
    if keep_weight:
        sums, weight_out, blocks, sem = rest
    else:
        sums, blocks, sem = rest
    copies = []
    for chunk, places in zip(chunks, spread):
        for i, spot in enumerate(places):
            copies.append(pltpu.make_async_copy(chunk.at[i], blocks.at[spot], sem.at[spot]))
    for copy in copies:
        copy.start()
    for copy in copies:
        copy.wait()
    for row in range(4):
        group = stream * 4 + row
        number = count[group]

        def step(it, total):
            lefts, rights = [], []
            for u in range(UNROLL):
                at = it * UNROLL + u
                held = jnp.minimum(at, number - 1)
                slot = jnp.where(at < number, slots[group, held], 2 * SLOTS)
                lefts.append(tiles[slot])
                rights.append(blocks[spots[group, held], 0:BLK, :])
            return total + jnp.dot(
                jnp.concatenate(lefts, axis=1),
                jnp.concatenate(rights, axis=0),
                preferred_element_type=F32,
            )

        steps = lax.div(number + (UNROLL - 1), UNROLL)
        sums[row] = lax.fori_loop(0, steps, step, start[row])
    if keep_weight:
        x, z, y = place[1], place[2], place[3]
        for k in range(NX):
            for j in range(NZ):
                column = (x - k) & (NX - 1)
                level = (z - j) & (NZ - 1)
                part = (level // 2 - y) & (NY - 1)
                weight_out[part, (level & 1) * NX + column] = blocks[k * NZ + j, BLK : BLK + W_ROWS, :]


def forward(stream, chunks, spread, lists, place, tiles, start, keep_weight):
    rows = chunks[0].shape[1]
    out_shape = [jax.ShapeDtypeStruct((4, BLK, WIDTH), F32)]
    if keep_weight:
        out_shape.append(jax.ShapeDtypeStruct((NY, 2 * NX, W_ROWS, WIDTH), BF16))
    result = pl.pallas_call(
        functools.partial(forward_kernel, stream, spread, keep_weight),
        out_shape=tuple(out_shape),
        in_specs=[smem()] * 4 + [vmem()] * 2 + [anywhere()] * len(chunks),
        out_specs=(vmem(),) * len(out_shape),
        scratch_shapes=[
            pltpu.VMEM((NX * NZ, rows, WIDTH), BF16),
            pltpu.SemaphoreType.DMA((NX * NZ,)),
        ],
        compiler_params=pltpu.CompilerParams(vmem_limit_bytes=20 * MIB),
        cost_estimate=pl.CostEstimate(flops=64 * 2 * BLK * BLK * WIDTH, bytes_accessed=11 * MIB, transcendentals=0),
    )(*lists, place, tiles, start, *chunks)
    return result if keep_weight else result[0]


def backward_kernel(stream, spread, with_weight, count, slots, spots, place, tiles, scaled, *rest):
    if with_weight:
        weight_sums = rest[0]
        rest = rest[1:]
    outs, total = rest[:-1], rest[-1]
    total[...] = jnp.zeros_like(total)
    for row in range(4):
        group = stream * 4 + row
        number = count[group]
        right = scaled[row]

        def step(it, carry):
            lefts, at_spots = [], []
            for u in range(UNROLL):
                at = it * UNROLL + u
                held = jnp.minimum(at, number - 1)
                slot = jnp.where(at < number, slots[group, held], 2 * SLOTS)
                lefts.append(tiles[slot])
                at_spots.append(spots[group, held])
            terms = lax.dot_general(
                jnp.concatenate(lefts, axis=1), right, (((0,), (0,)), ((), ())), preferred_element_type=F32
            )
            for u in range(UNROLL):
                total[at_spots[u]] += terms[u * BLK : (u + 1) * BLK]
            return carry

        lax.fori_loop(0, lax.div(number + (UNROLL - 1), UNROLL), step, 0)
    x, z, y = place[1], place[2], place[3]
    for out, places in zip(outs, spread):
        for i, (dx, dz) in enumerate(places):
            spot = (-dx) % NX * NZ + (-dz) % NZ
            out[i, 0:BLK, :] = total[spot].astype(BF16)
            if with_weight:
                column = (x + dx) & (NX - 1)
                level = (z + dz) & (NZ - 1)
                part = (level // 2 - y) & (NY - 1)
                out[i, BLK : BLK + W_ROWS, :] = weight_sums[part, (level & 1) * NX + column]


def backward(stream, spread, lists, place, tiles, scaled, weight_sums=None):
    with_weight = weight_sums is not None
    rows = BLK + W_ROWS if with_weight else BLK
    extra = [weight_sums] if with_weight else []
    return pl.pallas_call(
        functools.partial(backward_kernel, stream, spread, with_weight),
        out_shape=tuple(jax.ShapeDtypeStruct((len(places), rows, WIDTH), BF16) for places in spread),
        in_specs=[smem()] * 4 + [vmem()] * (2 + len(extra)),
        out_specs=(vmem(),) * len(spread),
        scratch_shapes=[pltpu.VMEM((NX * NZ, BLK, WIDTH), F32)],
        compiler_params=pltpu.CompilerParams(vmem_limit_bytes=24 * MIB),
        cost_estimate=pl.CostEstimate(flops=64 * 2 * BLK * BLK * WIDTH, bytes_accessed=11 * MIB, transcendentals=0),
    )(*lists, place, tiles, scaled, *extra)


def gather_a(block):
    at_z = {0: block}
    up = down = block
    for step in range(1, 5):
        up = chip_shift(up, dz=1)
        at_z[step] = up
        if step < 4:
            down = chip_shift(down, dz=-1)
            at_z[NZ - step] = down
    chunks, spread = [], []
    for number, group in enumerate(AG_GROUPS):
        held = jnp.stack([at_z[j] for j in group])
        one = chip_shift(held, dx=1)
        three = chip_shift(held, dx=-1)
        two = chip_shift(one, dx=1) if number == 0 else chip_shift(three, dx=-1)
        for k, chunk in enumerate((held, one, two, three)):
            chunks.append(chunk)
            spread.append(tuple(k * NZ + j for j in group))
    return chunks, tuple(spread)


def gather_b(block):
    at_x = {0: block, 1: chip_shift(block, dx=1), 3: chip_shift(block, dx=-1), 2: chip_shift(block, dx=2)}
    chunks, spread = [], []
    for number, group in enumerate(AGB_GROUPS):
        held = jnp.stack([at_x[k] for k in group])
        at_z = {0: held}
        up = down = held
        for step in range(1, 5):
            if step < 4 or number == 0:
                up = chip_shift(up, dz=1)
                at_z[step] = up
            if step < 4 or number == 1:
                down = chip_shift(down, dz=-1)
                at_z[NZ - step] = down
        for j in range(NZ):
            chunks.append(at_z[j])
            spread.append(tuple(k * NZ + j for k in group))
    return chunks, tuple(spread)


def add(*values):
    total = values[0].astype(F32)
    for value in values[1:]:
        total = total + value.astype(F32)
    return total


RS_A_SPREAD = tuple(tuple((dx, dz) for dz in group) for dx in range(NX) for group in RS_GROUPS)
RS_B_SPREAD = tuple(tuple((dx, dz) for dx in group) for dz in range(NZ) for group in RSB_GROUPS)


def scatter_a(parts):
    part = {(dx, g): parts[dx * 2 + g] for dx in range(NX) for g in range(2)}
    one = {
        0: chip_shift(add(part[1, 0], chip_shift(part[2, 0], dx=1)).astype(BF16), dx=1),
        1: chip_shift(part[1, 1], dx=1),
    }
    three = {
        0: chip_shift(part[3, 0], dx=-1),
        1: chip_shift(add(part[3, 1], chip_shift(part[2, 1], dx=-1)).astype(BF16), dx=-1),
    }
    at_z = {}
    for g, group in enumerate(RS_GROUPS):
        for i, dz in enumerate(group):
            at_z[dz] = add(part[0, g][i], one[g][i], three[g][i])
    up = at_z[4]
    for dz in (3, 2, 1, 0):
        up = chip_shift(up.astype(BF16), dz=1)
        if dz:
            up = add(at_z[dz], up)
    down = at_z[5]
    for dz in (6, 7, 0):
        down = chip_shift(down.astype(BF16), dz=-1)
        if dz:
            down = add(at_z[dz], down)
    return add(at_z[0], up, down)


def scatter_b(parts):
    sums = []
    for e in range(2):
        part = {dz: parts[dz * 2 + e] for dz in range(NZ)}
        first = 4 if e == 0 else 3
        up = part[first]
        for dz in range(first - 1, -1, -1):
            up = chip_shift(up, dz=1)
            if dz:
                up = add(part[dz], up).astype(BF16)
        first = 5 if e == 0 else 4
        down = part[first]
        for dz in range(first + 1, NZ + 1):
            down = chip_shift(down, dz=-1)
            if dz < NZ:
                down = add(part[dz], down).astype(BF16)
        sums.append(add(part[0], up, down))
    two, one = sums[0][0], sums[0][1]
    three, zero = sums[1][0], sums[1][1]
    return add(
        zero,
        chip_shift(one.astype(BF16), dx=1),
        chip_shift(three.astype(BF16), dx=-1),
        chip_shift(two.astype(BF16), dx=2),
    )


def silu_parts(hidden):
    gate_value = jax.nn.sigmoid(hidden)
    return (hidden * gate_value, gate_value * (1.0 + hidden * (1.0 - gate_value)))


def on_device(feats, weight, bias, tile_values, tile_rows, tile_cols, tile_live, cotangent):
    dom = lax.axis_index("dom")
    y = lax.axis_index("feat")
    core = dom % 2
    x = (dom // 2) % NX
    z = dom // (2 * NX)
    place = jnp.stack([core, x, z, y]).astype(jnp.int32)

    chunks_b, spread_b = gather_b(feats[BLK:])
    chunks_a, spread_a = gather_a(jnp.concatenate([feats[:BLK], weight.T], axis=0))

    meta = jnp.stack([tile_rows, tile_cols, jnp.broadcast_to(tile_live, (SLOTS,))])
    other_meta = swap(meta, 1)
    tiles = jnp.concatenate(
        [tile_values, swap(tile_values, 1), jnp.zeros((1, BLK, BLK), BF16)], axis=0
    )
    lists = make_lists(meta, other_meta, place)

    own_live = jnp.arange(SLOTS, dtype=jnp.int32) < tile_live[0]
    row_sums = jnp.sum(tile_values, axis=2, dtype=F32)
    degree = 1.0 + jnp.concatenate(
        [
            jnp.sum(jnp.where((own_live & (tile_rows == row))[:, None], row_sums, 0.0), axis=0)
            for row in range(2)
        ]
    ).reshape(2 * BLK, 1)

    start = jnp.zeros((4, BLK, WIDTH), F32)
    sums, weight_lane = forward(0, chunks_a, spread_a, lists, place, tiles, start, True)
    weight_other = swap(weight_lane, 1)
    sums = forward(1, chunks_b, spread_b, lists, place, tiles, sums, False)
    neighbour_sum = (sums[:2] + swap(sums[2:], 1)).reshape(2 * BLK, WIDTH)
    mixed = ((feats.astype(F32) + neighbour_sum) / degree).astype(BF16)

    first = jnp.where(core == 0, weight_lane, weight_other)
    second = jnp.where(core == 0, weight_other, weight_lane)
    weight_t = jnp.stack([first, second], axis=2).reshape(NY, WIDTH, WIDTH)

    def hidden_part(dy):
        return lax.dot_general(mixed, weight_t[dy], (((1,), (1,)), ((), ())), preferred_element_type=F32)

    hidden = add(
        hidden_part(0),
        y_shift(hidden_part(1).astype(BF16), 1),
        y_shift(hidden_part(2).astype(BF16), 2),
        y_shift(hidden_part(3).astype(BF16), 3),
    ) + bias
    activated, slope = silu_parts(hidden)
    output = activated.astype(BF16)
    dz_full = cotangent.astype(F32) * slope
    bias_grad = jnp.sum(dz_full, axis=0, keepdims=True)
    for bit in (1, 2, 4, 8, 16, 32):
        bias_grad = bias_grad + swap(bias_grad, bit)
    dz_own = dz_full.astype(BF16)
    dz_parts = [dz_own] + [y_shift(dz_own, NY - dy) for dy in range(1, NY)]

    dmixed = sum(jnp.dot(dz_parts[dy], weight_t[dy], preferred_element_type=F32) for dy in range(NY))
    scaled = (dmixed / degree).astype(BF16)
    scaled_blocks = jnp.concatenate([scaled, swap(scaled, 1)], axis=0).reshape(4, BLK, WIDTH)

    parts_b = backward(1, RS_B_SPREAD, lists, place, tiles, scaled_blocks)

    weight_part = jnp.stack(
        [
            lax.dot_general(dz_parts[dy], mixed, (((0,), (0,)), ((), ())), preferred_element_type=F32)
            for dy in range(NY)
        ]
    ).reshape(NY, 2 * NX, 2, W_ROWS, WIDTH)
    mine = jnp.where(core == 0, weight_part[:, :, 0], weight_part[:, :, 1])
    others = jnp.where(core == 0, weight_part[:, :, 1], weight_part[:, :, 0])
    weight_sums = (mine + swap(others, 1)).astype(BF16)

    parts_a = backward(0, RS_A_SPREAD, lists, place, tiles, scaled_blocks, weight_sums)
    sum_b = scatter_b(parts_b)
    sum_a = scatter_a(parts_a)

    column_sum = jnp.concatenate([sum_a[:BLK], sum_b], axis=0)
    feats_grad = (scaled.astype(F32) + column_sum).astype(BF16)
    weight_grad = sum_a[BLK:].T
    return (output, feats_grad, weight_grad, bias_grad.reshape(WIDTH))


def solution(mesh):
    return jax.shard_map(
        on_device,
        mesh=mesh,
        in_specs=(
            P("dom", "feat"),
            P("feat", "dom"),
            P("feat"),
            P("dom", None, None),
            P("dom"),
            P("dom"),
            P("dom"),
            P("dom", "feat"),
        ),
        out_specs=(P("dom", "feat"), P("dom", "feat"), P("feat", "dom"), P("feat")),
        check_vma=False,
    )
```

```python
import functools

import jax
import jax.numpy as jnp
from jax import lax
from jax.experimental import pallas as pl
from jax.experimental.pallas import tpu as pltpu
from jax.sharding import PartitionSpec as P

F32 = jnp.float32
BF16 = jnp.bfloat16
NZ, NX, NY = 8, 4, 4
BLK = 128
SLOTS = 128
WIDTH = 256
NODES = 2 * BLK
W_ROWS = 16
ROWS = NODES + W_ROWS
UNROLL = 4
FETCH = 16
MIB = 1 << 20

LOW, HIGH, ACROSS = (0, 1, 7, 2), (6, 3, 5, 4), (0, 1, 3, 2)
GATHER_0 = tuple(
    tuple(k * NZ + j for j in group)
    for k, group in ((0, LOW), (1, LOW), (3, LOW), (2, LOW), (1, HIGH), (3, HIGH), (2, HIGH), (0, HIGH))
)
GATHER_1 = tuple(tuple(k * NZ + j for k in ACROSS) for j in (0, 1, 7, 2, 6, 3, 5, 4))
FAR, NEAR = (4, 5, 3, 6), (2, 7, 1, 0)
SCATTER_0 = tuple(
    tuple((dx, dz) for dz in group)
    for dx, group in ((2, FAR), (2, NEAR), (1, FAR), (3, NEAR), (1, NEAR), (3, FAR), (0, NEAR), (0, FAR))
)
SCATTER_1 = tuple(tuple((dx, dz) for dx in ACROSS) for dz in (4, 5, 3, 6, 2, 7, 1, 0))


def shift(value, core_0=None, core_1=None):
    pairs = []
    for z in range(NZ):
        for x in range(NX):
            for core, step in enumerate((core_0, core_1)):
                if step is not None:
                    target = ((z + step[0]) % NZ * NX + (x + step[1]) % NX) * 2 + core
                    pairs.append(((z * NX + x) * 2 + core, target))
    return lax.ppermute(value, "dom", pairs)


Z_UP, Z_DOWN, X_UP, X_DOWN, X_TWO = (1, 0), (-1, 0), (0, 1), (0, -1), (0, 2)


def swap(value, bit):
    return lax.ppermute(value, "dom", [(i, i ^ bit) for i in range(NZ * NX * 2)])


def y_shift(value, dy):
    return lax.ppermute(value, "feat", [(y, (y + dy) % NY) for y in range(NY)])


def smem():
    return pl.BlockSpec(memory_space=pltpu.SMEM)


def vmem():
    return pl.BlockSpec(memory_space=pltpu.VMEM)


def anywhere():
    return pl.BlockSpec(memory_space=pl.ANY)


def list_kernel(own, sib, place, count, slots, spots):
    core, x, z = place[0], place[1], place[2]
    for row in range(4):
        count[row] = 0

    def scan(meta, first_row, first_slot):
        def step(s, carry):
            column = meta[1, s]
            owner = column // 2
            row = first_row + meta[0, s]

            @pl.when(owner % 2 == core)
            def _():
                chip = owner // 2
                at = count[row]
                slots[row, at] = first_slot + s
                spot = ((x - chip % NX) & (NX - 1)) * NZ + ((z - chip // NX) & (NZ - 1))
                spots[row, at] = spot * 2 + column % 2
                count[row] = at + 1

            return carry

        lax.fori_loop(0, meta[2, 0], step, 0)

    scan(own, 0, 0)
    scan(sib, 2, SLOTS)


def make_lists(own, sib, place):
    return pl.pallas_call(
        list_kernel,
        out_shape=(
            jax.ShapeDtypeStruct((4,), jnp.int32),
            jax.ShapeDtypeStruct((4, 2 * SLOTS), jnp.int32),
            jax.ShapeDtypeStruct((4, 2 * SLOTS), jnp.int32),
        ),
        in_specs=[smem()] * 3,
        out_specs=(smem(),) * 3,
    )(own, sib, place)


def live_tiles(place, own, sib, tiles, sem):
    copies = []
    for which, source in enumerate((own, sib)):
        for step in range(SLOTS // FETCH):
            first = step * FETCH
            copy = pltpu.make_async_copy(
                source.at[pl.ds(first, FETCH)],
                tiles.at[pl.ds(which * SLOTS + first, FETCH)],
                sem.at[which * (SLOTS // FETCH) + step],
            )
            copies.append((first < place[4 + which], copy))
    return copies


def run_if(conditions_and_calls):
    for condition, call in conditions_and_calls:
        if condition is None:
            call()
        else:
            pl.when(condition)(call)


def picked_tiles(it, row, number, slots, spots, tiles):
    lefts, at_spots = [], []
    for u in range(UNROLL):
        at = it * UNROLL + u
        held = jnp.minimum(at, number - 1)
        slot = jnp.where(at < number, slots[row, held], 2 * SLOTS)
        lefts.append(tiles[slot])
        at_spots.append(spots[row, held])
    return jnp.concatenate(lefts, axis=1), at_spots


def forward_kernel(count, slots, spots, place, own, sib, *rest):
    chunks, rest = rest[:9], rest[9:]
    sums, weight_out, blocks, tiles, sem, tile_sem = rest
    core, x, z, y = place[0], place[1], place[2], place[3]
    copies = live_tiles(place, own, sib, tiles, tile_sem)
    for n, chunk in enumerate(chunks):
        row = min(n, 7)
        condition = None if n < 7 else core == n - 7
        for i in range(4):
            spot = jnp.where(core == 0, GATHER_0[row][i], GATHER_1[row][i])
            copies.append((condition, pltpu.make_async_copy(chunk.at[i], blocks.at[spot], sem.at[n * 4 + i])))
    run_if((condition, copy.start) for condition, copy in copies)
    tiles[2 * SLOTS] = jnp.zeros((BLK, BLK), BF16)
    run_if((condition, copy.wait) for condition, copy in copies)
    for row in range(4):
        number = count[row]

        def step(it, total):
            left, at_spots = picked_tiles(it, row, number, slots, spots, tiles)
            rights = []
            for at in at_spots:
                first = pl.multiple_of((at & 1) * BLK, BLK)
                rights.append(blocks[at >> 1, pl.ds(first, BLK), :])
            return total + jnp.dot(left, jnp.concatenate(rights, axis=0), preferred_element_type=F32)

        steps = lax.div(number + (UNROLL - 1), UNROLL)
        sums[row] = lax.fori_loop(0, steps, step, jnp.zeros((BLK, WIDTH), F32))
    for k in range(NX):
        for j in range(NZ):
            column = (x - k) & (NX - 1)
            level = (z - j) & (NZ - 1)
            part = (level // 2 - y) & (NY - 1)
            weight_out[part, (level & 1) * NX + column] = blocks[k * NZ + j, NODES:ROWS, :]


def forward(lists, place, own, sib, chunks):
    return pl.pallas_call(
        forward_kernel,
        out_shape=(
            jax.ShapeDtypeStruct((4, BLK, WIDTH), F32),
            jax.ShapeDtypeStruct((NY, 2 * NX, W_ROWS, WIDTH), BF16),
        ),
        in_specs=[smem()] * 4 + [anywhere()] * (2 + len(chunks)),
        out_specs=(vmem(),) * 2,
        scratch_shapes=[
            pltpu.VMEM((NX * NZ, ROWS, WIDTH), BF16),
            pltpu.VMEM((2 * SLOTS + 1, BLK, BLK), BF16),
            pltpu.SemaphoreType.DMA((36,)),
            pltpu.SemaphoreType.DMA((2 * SLOTS // FETCH,)),
        ],
        compiler_params=pltpu.CompilerParams(vmem_limit_bytes=20 * MIB),
        cost_estimate=pl.CostEstimate(flops=128 * 2 * BLK * BLK * WIDTH, bytes_accessed=9 * MIB, transcendentals=0),
    )(*lists, place, own, sib, *chunks)


def backward_kernel(count, slots, spots, place, own, sib, scaled, weight_sums, *rest):
    outs, rest = rest[:8], rest[8:]
    total, tiles, tile_sem = rest
    core, x, z, y = place[0], place[1], place[2], place[3]
    copies = live_tiles(place, own, sib, tiles, tile_sem)
    run_if((condition, copy.start) for condition, copy in copies)
    total[...] = jnp.zeros_like(total)
    tiles[2 * SLOTS] = jnp.zeros((BLK, BLK), BF16)
    run_if((condition, copy.wait) for condition, copy in copies)
    for row in range(4):
        number = count[row]
        right = scaled[row]

        def step(it, carry):
            left, at_spots = picked_tiles(it, row, number, slots, spots, tiles)
            terms = lax.dot_general(left, right, (((0,), (0,)), ((), ())), preferred_element_type=F32)
            for u in range(UNROLL):
                total[at_spots[u]] += terms[u * BLK : (u + 1) * BLK]
            return carry

        lax.fori_loop(0, lax.div(number + (UNROLL - 1), UNROLL), step, 0)
    for n, out in enumerate(outs):
        for i in range(4):
            dx = jnp.where(core == 0, SCATTER_0[n][i][0], SCATTER_1[n][i][0])
            dz = jnp.where(core == 0, SCATTER_0[n][i][1], SCATTER_1[n][i][1])
            spot = (-dx & (NX - 1)) * NZ + (-dz & (NZ - 1))
            out[i, 0:BLK, :] = total[spot * 2].astype(BF16)
            out[i, BLK:NODES, :] = total[spot * 2 + 1].astype(BF16)
            column = (x + dx) & (NX - 1)
            level = (z + dz) & (NZ - 1)
            part = (level // 2 - y) & (NY - 1)
            out[i, NODES:ROWS, :] = weight_sums[part, (level & 1) * NX + column]


def backward(lists, place, own, sib, scaled, weight_sums):
    return pl.pallas_call(
        backward_kernel,
        out_shape=(jax.ShapeDtypeStruct((4, ROWS, WIDTH), BF16),) * 8,
        in_specs=[smem()] * 4 + [anywhere()] * 2 + [vmem()] * 2,
        out_specs=(vmem(),) * 8,
        scratch_shapes=[
            pltpu.VMEM((2 * NX * NZ, BLK, WIDTH), F32),
            pltpu.VMEM((2 * SLOTS + 1, BLK, BLK), BF16),
            pltpu.SemaphoreType.DMA((2 * SLOTS // FETCH,)),
        ],
        compiler_params=pltpu.CompilerParams(vmem_limit_bytes=28 * MIB),
        cost_estimate=pl.CostEstimate(flops=128 * 2 * BLK * BLK * WIDTH, bytes_accessed=9 * MIB, transcendentals=0),
    )(*lists, place, own, sib, scaled, weight_sums)


def gather(block, core):
    p1 = shift(block, Z_UP, X_UP)
    p2 = shift(block, Z_DOWN, X_DOWN)
    p3 = shift(jnp.where(core == 0, p1, block), Z_UP, X_TWO)
    low = jnp.stack([block, p1, p2, p3])
    c1 = shift(low, X_UP, Z_UP)
    c2 = shift(low, X_DOWN, Z_DOWN)
    p4 = shift(p2, Z_DOWN)
    p5 = shift(p3, Z_UP)
    p6 = shift(p4, Z_DOWN)
    p7 = shift(p6, Z_DOWN)
    high = jnp.stack([p4, p5, p6, p7])
    c3 = shift(c1, X_UP, Z_UP)
    c4 = shift(jnp.where(core == 0, high, c2), X_UP, Z_DOWN)
    c5 = shift(jnp.where(core == 0, high, c3), X_DOWN, Z_UP)
    c6 = shift(jnp.where(core == 0, c5, c4), X_DOWN, Z_DOWN)
    c7 = shift(c5, None, Z_UP)
    return [low, c1, c2, c3, c4, c5, c6, high, c7]


def add(*values):
    total = values[0].astype(F32)
    for value in values[1:]:
        total = total + value.astype(F32)
    return total


def scatter(parts, core, watch):
    a, b, c, d, e, f, g, h = parts
    zero = jnp.zeros((), BF16)
    j1 = shift(a, X_UP, Z_UP)
    j2 = shift(b, X_DOWN, Z_DOWN)
    j3 = shift(add(c, j1).astype(BF16), X_UP, Z_UP)
    j4 = shift(add(d, j2).astype(BF16), X_DOWN, Z_DOWN)
    j5 = shift(add(e, jnp.where(core == 0, zero, j3)).astype(BF16), X_UP, Z_UP)
    j6 = shift(add(f, jnp.where(core == 0, zero, j4)).astype(BF16), X_DOWN, Z_DOWN)
    j7 = shift(add(g, j5).astype(BF16), None, Z_UP)
    watch.extend([j1, j2, j3, j4, j5])

    def far(i):
        return add(h[i], j3[i], j6[i])

    def near(i):
        return add(g[i], j4[i], j5[i])

    def across(i):
        return add(h[i], j6[i], j7[i])

    r1 = shift(jnp.where(core == 0, far(0), across(1)).astype(BF16), Z_UP, X_UP)
    r2 = shift(jnp.where(core == 0, far(1), across(2)).astype(BF16), Z_DOWN, X_DOWN)
    r3 = shift(jnp.where(core == 0, add(far(2), r1), across(3)).astype(BF16), Z_UP, X_TWO)
    r4 = shift(add(far(3), r2).astype(BF16), Z_DOWN)
    r5 = shift(add(near(0), r3).astype(BF16), Z_UP)
    r6 = shift(add(near(1), r4).astype(BF16), Z_DOWN)
    r7 = shift(add(near(2), r5).astype(BF16), Z_UP)
    return jnp.where(core == 0, add(near(3), r6, r7), add(across(0), r1, r2, r3))


def after(value, other):
    return value + jnp.minimum(jnp.abs(other[0, 0, :1].astype(F32)), 0.0)


def silu_parts(hidden):
    gate_value = jax.nn.sigmoid(hidden)
    return (hidden * gate_value, gate_value * (1.0 + hidden * (1.0 - gate_value)))


def on_device(feats, weight, bias, tile_values, tile_rows, tile_cols, tile_live, cotangent):
    dom = lax.axis_index("dom")
    y = lax.axis_index("feat")
    core = dom % 2
    x = (dom // 2) % NX
    z = dom // (2 * NX)

    chunks = gather(jnp.concatenate([feats, weight.T], axis=0), core)

    meta = jnp.stack([tile_rows, tile_cols, jnp.broadcast_to(tile_live, (SLOTS,))])
    other_meta = swap(meta, 1)
    other_tiles = swap(tile_values, 1)
    place = jnp.stack([core, x, z, y, tile_live[0], other_meta[2, 0]]).astype(jnp.int32)
    lists = make_lists(meta, other_meta, place)

    own_live = jnp.arange(SLOTS, dtype=jnp.int32) < tile_live[0]
    row_sums = jnp.sum(tile_values, axis=2, dtype=F32)
    degree = 1.0 + jnp.concatenate(
        [
            jnp.sum(jnp.where((own_live & (tile_rows == row))[:, None], row_sums, 0.0), axis=0)
            for row in range(2)
        ]
    ).reshape(NODES, 1)

    sums, weight_lane = forward(lists, place, tile_values, other_tiles, chunks)
    neighbour_sum = (sums[:2] + swap(sums[2:], 1)).reshape(NODES, WIDTH)
    weight_other = swap(weight_lane, 1)
    mixed = ((feats.astype(F32) + neighbour_sum) / degree).astype(BF16)

    first = jnp.where(core == 0, weight_lane, weight_other)
    second = jnp.where(core == 0, weight_other, weight_lane)
    weight_t = jnp.stack([first, second], axis=2).reshape(NY, WIDTH, WIDTH)

    def hidden_part(dy):
        return lax.dot_general(mixed, weight_t[dy], (((1,), (1,)), ((), ())), preferred_element_type=F32)

    hidden = add(
        hidden_part(0),
        y_shift(hidden_part(1).astype(BF16), 1),
        y_shift(hidden_part(2).astype(BF16), 2),
        y_shift(hidden_part(3).astype(BF16), 3),
    ) + bias
    activated, slope = silu_parts(hidden)
    output = activated.astype(BF16)
    dz_full = cotangent.astype(F32) * slope
    dz_own = dz_full.astype(BF16)
    dz_parts = [dz_own] + [y_shift(dz_own, NY - dy) for dy in range(1, NY)]

    dmixed = sum(jnp.dot(dz_parts[dy], weight_t[dy], preferred_element_type=F32) for dy in range(NY))
    scaled = (dmixed / degree).astype(BF16)
    scaled_blocks = jnp.concatenate([scaled, swap(scaled, 1)], axis=0).reshape(4, BLK, WIDTH)

    weight_part = jnp.stack(
        [
            lax.dot_general(dz_parts[dy], mixed, (((0,), (0,)), ((), ())), preferred_element_type=F32)
            for dy in range(NY)
        ]
    ).reshape(NY, 2 * NX, 2, W_ROWS, WIDTH)
    mine = jnp.where(core == 0, weight_part[:, :, 0], weight_part[:, :, 1])
    others = jnp.where(core == 0, weight_part[:, :, 1], weight_part[:, :, 0])
    bias_part = jnp.sum(dz_full, axis=0, keepdims=True)
    bias_rows = jnp.pad(bias_part, ((0, 7), (0, 0)))
    sent = jnp.concatenate([others.reshape(-1, WIDTH), bias_rows], axis=0)
    got = swap(sent, 1)
    weight_sums = (mine + got[:-8].reshape(mine.shape)).astype(BF16)
    bias_grad = bias_part + got[-8:-7]

    parts = backward(lists, place, tile_values, other_tiles, scaled_blocks, weight_sums)
    watch = []
    column_sum = scatter(parts, core, watch)
    for bit, seen in zip((2, 4, 8, 16, 32), watch):
        bias_grad = bias_grad + swap(after(bias_grad, seen), bit)

    feats_grad = (scaled.astype(F32) + column_sum[:NODES]).astype(BF16)
    weight_grad = column_sum[NODES:].T
    return (output, feats_grad, weight_grad, bias_grad.reshape(WIDTH))


def solution(mesh):
    return jax.shard_map(
        on_device,
        mesh=mesh,
        in_specs=(
            P("dom", "feat"),
            P("feat", "dom"),
            P("feat"),
            P("dom", None, None),
            P("dom"),
            P("dom"),
            P("dom"),
            P("dom", "feat"),
        ),
        out_specs=(P("dom", "feat"), P("dom", "feat"), P("feat", "dom"), P("feat")),
        check_vma=False,
    )
```

```python
import functools

import jax
import jax.numpy as jnp
from jax import lax
from jax.experimental import pallas as pl
from jax.experimental.pallas import tpu as pltpu
from jax.sharding import PartitionSpec as P

F32 = jnp.float32
BF16 = jnp.bfloat16
NZ, NX, NY = 8, 4, 4
BLK = 128
SLOTS = 128
WIDTH = 256
NODES = 2 * BLK
W_ROWS = 16
ROWS = NODES + W_ROWS
UNROLL = 8
FETCH = 16
BIAS_ROWS = 16
SUM_ROWS = 4 * ROWS + BIAS_ROWS
MIB = 1 << 20
VMEM = 54 * MIB

LOW, HIGH, ACROSS = (0, 1, 7, 2), (6, 3, 5, 4), (0, 1, 3, 2)
GATHER_0 = tuple(
    tuple(k * NZ + j for j in group)
    for k, group in ((0, LOW), (1, LOW), (3, LOW), (2, LOW), (3, HIGH), (1, HIGH), (2, HIGH), (0, HIGH))
)
GATHER_1 = tuple(tuple(k * NZ + j for k in ACROSS) for j in (0, 1, 7, 2, 6, 3, 5, 4))
FORWARD_CHUNKS = ((0, 1, 2, 3, 4, 7), (5, 6), (8,))
BACKWARD_CHUNKS = ((0, 1), (2, 3, 4, 5, 6, 7))
FAR, NEAR = (4, 5, 3, 6), (2, 7, 1, 0)
SCATTER_0 = tuple(
    tuple((dx, dz) for dz in group)
    for dx, group in ((2, FAR), (2, NEAR), (1, FAR), (3, NEAR), (1, NEAR), (3, FAR), (0, NEAR), (0, FAR))
)
SCATTER_1 = tuple(tuple((dx, dz) for dx in ACROSS) for dz in (4, 5, 3, 6, 2, 7, 1, 0))


def shift(value, core_0=None, core_1=None):
    pairs = []
    for z in range(NZ):
        for x in range(NX):
            for core, step in enumerate((core_0, core_1)):
                if step is not None:
                    target = ((z + step[0]) % NZ * NX + (x + step[1]) % NX) * 2 + core
                    pairs.append(((z * NX + x) * 2 + core, target))
    return lax.ppermute(value, "dom", pairs)


Z_UP, Z_DOWN, Z_UP_2, Z_DOWN_2 = (1, 0), (-1, 0), (2, 0), (-2, 0)
X_UP, X_DOWN, X_TWO = (0, 1), (0, -1), (0, 2)


def swap(value, bit):
    return lax.ppermute(value, "dom", [(i, i ^ bit) for i in range(NZ * NX * 2)])


def y_shift(value, dy):
    return lax.ppermute(value, "feat", [(y, (y + dy) % NY) for y in range(NY)])


def smem():
    return pl.BlockSpec(memory_space=pltpu.SMEM)


def vmem():
    return pl.BlockSpec(memory_space=pltpu.VMEM)


def anywhere():
    return pl.BlockSpec(memory_space=pl.ANY)


def list_kernel(place, own, sib, lists):
    core, x, z = place[0], place[1], place[2]
    wide = (1, 2 * SLOTS)
    column = jnp.concatenate([own[1:2], sib[1:2]], axis=1)
    row = jnp.concatenate([own[0:1], sib[0:1] + 2], axis=1)
    slot = lax.broadcasted_iota(jnp.int32, wide, 1)
    live = slot < jnp.where(slot < SLOTS, place[4], SLOTS + place[5])
    owner = column >> 1
    chip = owner >> 1
    k = (x - (chip & (NX - 1))) & (NX - 1)
    j = (z - (chip >> 2)) & (NZ - 1)
    spot = (k * NZ + j) * 2 + (column & 1)
    mine = live & ((owner & 1) == core)
    on_0 = jnp.where(((k == 1) | (k == 2)) & (j >= 3) & (j <= 6), 1, 0)
    on_1 = jnp.where(j == 4, 2, jnp.where((j == 3) | (j == 5), 1, 0))
    forward_call = jnp.where(core == 0, on_0, on_1)
    backward_call = jnp.where(core == 0, jnp.where(k == 2, 0, 1), jnp.where((j == 3) | (j == 4), 0, 1))
    square = (2 * SLOTS, 2 * SLOTS)
    first = lax.broadcasted_iota(jnp.int32, square, 0)
    second = lax.broadcasted_iota(jnp.int32, square, 1)
    up_to = jnp.where(first <= second, 1.0, 0.0).astype(BF16)
    group_of = lax.broadcasted_iota(jnp.int32, (16, 2 * SLOTS), 0)
    lane = lax.broadcasted_iota(jnp.int32, (16, 2 * SLOTS), 1)
    before = jnp.where(
        lax.broadcasted_iota(jnp.int32, (16, 16), 1) < lax.broadcasted_iota(jnp.int32, (16, 16), 0), 1.0, 0.0
    ).astype(BF16)
    values = jnp.concatenate([slot, spot], axis=0).astype(F32)
    values = jnp.concatenate([values, jnp.zeros((14, 2 * SLOTS), F32)], axis=0).astype(BF16)
    lists[...] = jnp.zeros_like(lists)
    for at, call in ((0, forward_call), (3, backward_call)):
        group = jnp.where(mine, call * 4 + row, -1)
        member = jnp.where(group_of == group, 1.0, 0.0)
        rank = jnp.dot(member.astype(BF16), up_to, preferred_element_type=F32)
        counts = jnp.sum(member, axis=1, keepdims=True)
        earlier = jnp.dot(before, member.astype(BF16), preferred_element_type=F32)
        starts = jnp.sum(earlier, axis=1, keepdims=True)
        goal = jnp.sum(member * (starts + rank), axis=0, keepdims=True).astype(jnp.int32) - 1
        moved = jnp.where(first == goal, 1.0, 0.0).astype(BF16)
        ordered = lax.dot_general(values, moved, (((1,), (1,)), ((), ())), preferred_element_type=F32)
        lists[at : at + 1, :] = jnp.sum(jnp.where(group_of == lane, counts, 0.0), axis=0, keepdims=True).astype(jnp.int32)
        lists[at + 1 : at + 2, :] = jnp.sum(jnp.where(group_of == lane, starts, 0.0), axis=0, keepdims=True).astype(jnp.int32)
        lists[at + 2 : at + 3, :] = (ordered[0:1] * 64.0 + ordered[1:2]).astype(jnp.int32)
    told = jnp.zeros(wide, jnp.int32)
    for i in range(6):
        told = jnp.where(slot == i, place[i], told)
    lists[6:7, :] = told


def make_lists(place, own, sib):
    return pl.pallas_call(
        list_kernel,
        out_shape=jax.ShapeDtypeStruct((8, 2 * SLOTS), jnp.int32),
        in_specs=[smem(), vmem(), vmem()],
        out_specs=vmem(),
    )(place, own, sib)


def place_of(lists):
    return [lists[6, i] for i in range(4)]


def copy_each(copies, action):
    for condition, copy in copies:
        call = getattr(copy, action)
        if condition is None:
            call()
        else:
            pl.when(condition)(call)


class Tiles:
    def __init__(self, lists, at, call, every, own, sib, held, sem):
        self.lists, self.at, self.call, self.every = lists, at, call, every
        self.own, self.sib, self.held, self.sem = own, sib, held, sem
        self.begin = lists[at + 1, call * 4]
        self.end = lists[at + 1, call * 4 + 3] + lists[at, call * 4 + 3]

    def bulk(self):
        copies = []
        for which, source in enumerate((self.own, self.sib)):
            for step in range(SLOTS // FETCH):
                first = step * FETCH
                copy = pltpu.make_async_copy(
                    source.at[pl.ds(first, FETCH)],
                    self.held.at[pl.ds(which * SLOTS + first, FETCH)],
                    self.sem.at[which * (SLOTS // FETCH) + step],
                )
                copies.append((first < self.lists[6, 4 + which], copy))
        return copies

    def each(self, action):
        def step(p, carry):
            slot = self.lists[self.at + 2, p] >> 6
            goal = self.held.at[p]

            @pl.when(slot < SLOTS)
            def _():
                getattr(pltpu.make_async_copy(self.own.at[jnp.minimum(slot, SLOTS - 1)], goal, self.sem.at[0]), action)()

            @pl.when(slot >= SLOTS)
            def _():
                getattr(pltpu.make_async_copy(self.sib.at[jnp.maximum(slot - SLOTS, 0)], goal, self.sem.at[0]), action)()

            return carry

        lax.fori_loop(self.begin, self.end, step, 0)

    def start(self):
        if self.every:
            copy_each(self.bulk(), "start")
        else:
            self.each("start")
        self.held[2 * SLOTS] = jnp.zeros((BLK, BLK), BF16)

    def wait(self):
        if self.every:
            copy_each(self.bulk(), "wait")
        else:
            self.each("wait")

    def rows(self):
        for row in range(4):
            group = self.call * 4 + row
            number, first = self.lists[self.at, group], self.lists[self.at + 1, group]

            def pick(it, number=number, first=first):
                lefts, spots = [], []
                for u in range(UNROLL):
                    p = it * UNROLL + u
                    entry = self.lists[self.at + 2, first + jnp.minimum(p, number - 1)]
                    place = entry >> 6 if self.every else first + p
                    lefts.append(self.held[jnp.where(p < number, place, 2 * SLOTS)])
                    spots.append(entry & 63)
                return jnp.concatenate(lefts, axis=1), spots

            yield row, lax.div(number + (UNROLL - 1), UNROLL), pick


def forward_kernel(call, lists, own, sib, *rest):
    chosen = FORWARD_CHUNKS[call]
    chunks, rest = rest[: len(chosen)], rest[len(chosen) :]
    if call:
        sums_before, weight_before, *rest = rest
    sums, weight_out, blocks, held, sem, tile_sem = rest
    core, x, z, y = place_of(lists)
    tiles = Tiles(lists, 0, call, call == 0, own, sib, held, tile_sem)
    tiles.start()
    copies, arrived = [], []
    for n, chunk in zip(chosen, chunks):
        table = min(n, 7)
        condition = None if n < 7 else core == n - 7
        for i in range(4):
            spot = jnp.where(core == 0, GATHER_0[table][i], GATHER_1[table][i])
            copies.append((condition, pltpu.make_async_copy(chunk.at[i], blocks.at[spot], sem.at[len(copies)])))
            arrived.append((condition, spot))
    copy_each(copies, "start")
    copy_each(copies, "wait")
    tiles.wait()
    for row, steps, pick in tiles.rows():

        def step(it, total):
            left, spots = pick(it)
            rights = []
            for spot in spots:
                first = pl.multiple_of((spot & 1) * BLK, BLK)
                rights.append(blocks[spot >> 1, pl.ds(first, BLK), :])
            return total + jnp.dot(left, jnp.concatenate(rights, axis=0), preferred_element_type=F32)

        sums[row] = lax.fori_loop(0, steps, step, sums_before[row] if call else jnp.zeros((BLK, WIDTH), F32))
    if call:
        weight_out[...] = weight_before[...]
    for condition, spot in arrived:

        def keep(spot=spot):
            column = (x - (spot >> 3)) & (NX - 1)
            level = (z - spot) & (NZ - 1)
            part = ((level >> 1) - y) & (NY - 1)
            weight_out[part, (level & 1) * NX + column] = blocks[spot, NODES:ROWS, :]

        if condition is None:
            keep()
        else:
            pl.when(condition)(keep)


def forward(call, lists, own, sib, chunks, before):
    chosen = [chunks[n] for n in FORWARD_CHUNKS[call]]
    return pl.pallas_call(
        functools.partial(forward_kernel, call),
        out_shape=(
            jax.ShapeDtypeStruct((4, BLK, WIDTH), F32),
            jax.ShapeDtypeStruct((NY, 2 * NX, W_ROWS, WIDTH), BF16),
        ),
        in_specs=[smem()] + [anywhere()] * (2 + len(chosen)) + [vmem()] * len(before),
        out_specs=(vmem(),) * 2,
        scratch_shapes=[
            pltpu.VMEM((NX * NZ, ROWS, WIDTH), BF16),
            pltpu.VMEM((2 * SLOTS + 1, BLK, BLK), BF16),
            pltpu.SemaphoreType.DMA((24,)),
            pltpu.SemaphoreType.DMA((2 * SLOTS // FETCH,)),
        ],
        compiler_params=pltpu.CompilerParams(vmem_limit_bytes=VMEM),
        cost_estimate=pl.CostEstimate(
            flops=2 * BLK * BLK * WIDTH * len(chosen) * 16, bytes_accessed=len(chosen) * MIB, transcendentals=0
        ),
    )(lists, own, sib, *chosen, *before)


def backward_kernel(call, lists, own, sib, scaled, weight_sums, bias_rows, *rest):
    chosen = BACKWARD_CHUNKS[call]
    outs, rest = rest[: len(chosen)], rest[len(chosen) :]
    total, held, tile_sem = rest
    core, x, z, y = place_of(lists)
    tiles = Tiles(lists, 3, call, call == 1, own, sib, held, tile_sem)
    tiles.start()
    targets = {}
    for n in chosen:
        for i in range(4):
            dx = jnp.where(core == 0, SCATTER_0[n][i][0], SCATTER_1[n][i][0])
            dz = jnp.where(core == 0, SCATTER_0[n][i][1], SCATTER_1[n][i][1])
            spot = ((0 - dx) & (NX - 1)) * NZ + ((0 - dz) & (NZ - 1))
            targets[n, i] = dx, dz, spot
            total[spot * 2] = jnp.zeros((BLK, WIDTH), F32)
            total[spot * 2 + 1] = jnp.zeros((BLK, WIDTH), F32)
    tiles.wait()
    for row, steps, pick in tiles.rows():
        right = scaled[row]

        def step(it, carry):
            left, spots = pick(it)
            terms = lax.dot_general(left, right, (((0,), (0,)), ((), ())), preferred_element_type=F32)
            for u, spot in enumerate(spots):
                total[spot] += terms[u * BLK : (u + 1) * BLK]
            return carry

        lax.fori_loop(0, steps, step, 0)
    for n, out in zip(chosen, outs):
        for i in range(4):
            dx, dz, spot = targets[n, i]
            first = i * ROWS
            out[first : first + BLK, :] = total[spot * 2].astype(BF16)
            out[first + BLK : first + NODES, :] = total[spot * 2 + 1].astype(BF16)
            column = (x + dx) & (NX - 1)
            level = (z + dz) & (NZ - 1)
            part = ((level >> 1) - y) & (NY - 1)
            out[first + NODES : first + ROWS, :] = weight_sums[part, (level & 1) * NX + column]
        out[4 * ROWS : SUM_ROWS, :] = bias_rows[...] if call == 0 else jnp.zeros((BIAS_ROWS, WIDTH), BF16)


def backward(call, lists, own, sib, scaled, weight_sums, bias_rows):
    number = len(BACKWARD_CHUNKS[call])
    return pl.pallas_call(
        functools.partial(backward_kernel, call),
        out_shape=(jax.ShapeDtypeStruct((SUM_ROWS, WIDTH), BF16),) * number,
        in_specs=[smem()] + [anywhere()] * 2 + [vmem()] * 3,
        out_specs=(vmem(),) * number,
        scratch_shapes=[
            pltpu.VMEM((2 * NX * NZ, BLK, WIDTH), F32),
            pltpu.VMEM((2 * SLOTS + 1, BLK, BLK), BF16),
            pltpu.SemaphoreType.DMA((2 * SLOTS // FETCH,)),
        ],
        compiler_params=pltpu.CompilerParams(vmem_limit_bytes=VMEM),
        cost_estimate=pl.CostEstimate(
            flops=2 * BLK * BLK * WIDTH * number * 16, bytes_accessed=number * MIB, transcendentals=0
        ),
    )(lists, own, sib, scaled, weight_sums, bias_rows)


def gather(block, core, ready, sorted_lists, call):
    p1 = shift(block, Z_UP, X_UP)
    p2 = shift(block, Z_DOWN, X_DOWN)
    p3 = shift(block, Z_UP_2, X_TWO)
    p4 = shift(block, Z_DOWN_2)
    low = jnp.stack([block, p1, p2, p3]) + (ready + nothing(p4[0, 0]))
    c1 = shift(low, X_UP, Z_UP)
    c2 = shift(low, X_DOWN, Z_DOWN)
    p5 = shift(p3, Z_UP)
    p6 = shift(p4, Z_DOWN)
    p7 = shift(p3, Z_UP_2)
    high = jnp.stack([p4, p5, p6, p7])
    c3 = shift(c1 + nothing(high[1:, 0, 0].sum()), X_UP, Z_UP)
    c4 = shift(jnp.where(core == 0, high, c2) + sorted_lists, X_DOWN, Z_DOWN)
    c5 = shift(jnp.where(core == 0, high, c3), X_UP, Z_UP)
    c6 = shift(c4, X_DOWN, Z_DOWN)
    chunks = [low, c1, c2, c3, c4, c5, c6, high]
    sums = call(0, chunks, ())
    c7 = shift(c5 + nothing(sums[0][0, 0, 0]), None, Z_UP)
    chunks.append(c7)
    sums = call(1, chunks, sums)
    return call(2, chunks, sums)


def add(*values):
    total = values[0].astype(F32)
    for value in values[1:]:
        total = total + value.astype(F32)
    return total


def split(value):
    high = lax.reduce_precision(value, 8, 7)
    middle = lax.reduce_precision(value - high, 8, 7)
    rows = jnp.concatenate([high, middle, value - high - middle], axis=0)
    return jnp.pad(rows, ((0, BIAS_ROWS - 3), (0, 0))).astype(BF16)


def joined(block, first=0):
    rows = block[first : first + 3].astype(F32)
    return rows[0:1] + rows[1:2] + rows[2:3]


def in_order(values, place):
    count = len(values)
    rows = jnp.concatenate([values[k] for k in range(count - 1, -1, -1)] * 2, axis=0)
    rows = lax.dynamic_slice_in_dim(rows, count - 1 - place, count, 0)
    total = rows[0:1]
    for i in range(1, count):
        total = total + rows[i : i + 1]
    return total


def scatter(parts, core, x, z, chip_bias):
    a, b, c, d, e, f, g, h = parts
    zero = jnp.zeros((), BF16)
    j1 = shift(a, X_UP, Z_UP)
    j2 = shift(b, X_DOWN, Z_DOWN)
    j3 = shift(add(c, j1).astype(BF16), X_UP, Z_UP)
    j4 = shift(add(d, j2).astype(BF16), X_DOWN, Z_DOWN)
    j5 = shift(add(e, jnp.where(core == 0, zero, j3)).astype(BF16), X_UP, Z_UP)
    j6 = shift(add(f, jnp.where(core == 0, zero, j4)).astype(BF16), X_DOWN, Z_DOWN)
    j7 = shift(add(g, j5).astype(BF16), None, Z_UP)

    def tail(value):
        return value[4 * ROWS :]

    line_bias = in_order([chip_bias, joined(tail(j1)), joined(tail(j3)), joined(tail(j2))], x)
    own_rows = split(line_bias)

    def block(value, i):
        return value[i * ROWS : (i + 1) * ROWS]

    def far(i):
        return add(block(h, i), block(j3, i), block(j6, i))

    def near(i):
        return add(block(g, i), block(j4, i), block(j5, i))

    def across(i):
        return add(block(h, i), block(j6, i), block(j7, i))

    def message(value, rows=own_rows):
        return jnp.concatenate([value.astype(BF16), rows], axis=0)

    r4 = shift(message(far(0)), Z_UP_2)
    r31 = shift(jnp.concatenate([message(far(2)), message(near(2))], axis=0), Z_UP)
    r57 = shift(jnp.concatenate([message(far(1)), message(near(1))], axis=0), Z_DOWN)
    size = ROWS + BIAS_ROWS
    r3, r1, r5, r7 = r31[:size], r31[size:], r57[:size], r57[size:]
    rows = jnp.concatenate([own_rows[:3], r4[ROWS : ROWS + 3], r3[ROWS : ROWS + 3], own_rows[9:]], axis=0)
    on_0 = message(add(near(0), r4[:ROWS], r3[:ROWS], nothing(r57[0, 0])), rows)
    r2 = shift(jnp.where(core == 0, on_0, message(across(1))), Z_UP_2, X_UP)
    rows = jnp.concatenate([own_rows[:3], r5[ROWS : ROWS + 3], own_rows[6:]], axis=0)
    on_0 = message(add(far(3), r5[:ROWS]), rows)
    r6 = shift(jnp.where(core == 0, on_0, message(across(2))), Z_DOWN_2, X_DOWN)
    r0 = shift(across(3).astype(BF16), None, X_TWO)
    total = jnp.where(
        core == 0,
        add(near(3), r1[:ROWS], r2[:ROWS], r6[:ROWS], r7[:ROWS]),
        add(across(0), r2[:ROWS], r6[:ROWS], r0),
    )
    bias = in_order(
        [
            line_bias,
            joined(r1, ROWS),
            joined(r2, ROWS),
            joined(r2, ROWS + 6),
            joined(r2, ROWS + 3),
            joined(r6, ROWS + 3),
            joined(r6, ROWS),
            joined(r7, ROWS),
        ],
        z,
    )
    return total, bias


def nothing(value):
    return jnp.minimum(jnp.abs(value.astype(F32)), 0.0).astype(BF16)


def silu_parts(hidden):
    gate_value = jax.nn.sigmoid(hidden)
    return (hidden * gate_value, gate_value * (1.0 + hidden * (1.0 - gate_value)))


def on_device(feats, weight, bias, tile_values, tile_rows, tile_cols, tile_live, cotangent):
    dom = lax.axis_index("dom")
    y = lax.axis_index("feat")
    core = dom % 2
    x = (dom // 2) % NX
    z = dom // (2 * NX)

    meta = jnp.stack([tile_rows, tile_cols, jnp.broadcast_to(tile_live, (SLOTS,))])
    other_meta = swap(meta, 1)
    other_tiles = swap(tile_values, 1)
    place = jnp.stack([core, x, z, y, tile_live[0], other_meta[2, 0]]).astype(jnp.int32)
    lists = make_lists(place, meta, other_meta)

    own_live = jnp.arange(SLOTS, dtype=jnp.int32) < tile_live[0]
    row_sums = jnp.sum(tile_values, axis=2, dtype=F32)
    degree = 1.0 + jnp.concatenate(
        [
            jnp.sum(jnp.where((own_live & (tile_rows == row))[:, None], row_sums, 0.0), axis=0)
            for row in range(2)
        ]
    ).reshape(NODES, 1)

    sums, weight_lane = gather(
        jnp.concatenate([feats, weight.T], axis=0),
        core,
        nothing(other_tiles[0, 0, 0]) + nothing(other_meta[0, 0]),
        nothing(lists[0, 0]),
        lambda call, chunks, before: forward(call, lists, tile_values, other_tiles, chunks, before),
    )
    neighbour_sum = (sums[:2] + swap(sums[2:], 1)).reshape(NODES, WIDTH)
    weight_other = swap(weight_lane, 1)
    mixed = ((feats.astype(F32) + neighbour_sum) / degree).astype(BF16)

    first = jnp.where(core == 0, weight_lane, weight_other)
    second = jnp.where(core == 0, weight_other, weight_lane)
    weight_t = jnp.stack([first, second], axis=2).reshape(NY, WIDTH, WIDTH)

    def hidden_part(dy):
        return lax.dot_general(mixed, weight_t[dy], (((1,), (1,)), ((), ())), preferred_element_type=F32)

    hidden = add(
        hidden_part(0),
        y_shift(hidden_part(1).astype(BF16), 1),
        y_shift(hidden_part(2).astype(BF16), 2),
        y_shift(hidden_part(3).astype(BF16), 3),
    ) + bias
    activated, slope = silu_parts(hidden)
    output = activated.astype(BF16)
    dz_full = cotangent.astype(F32) * slope
    dz_own = dz_full.astype(BF16)
    dz_parts = [dz_own] + [y_shift(dz_own, NY - dy) for dy in range(1, NY)]

    dmixed = sum(jnp.dot(dz_parts[dy], weight_t[dy], preferred_element_type=F32) for dy in range(NY))
    scaled = (dmixed / degree).astype(BF16)
    scaled_blocks = jnp.concatenate([scaled, swap(scaled, 1)], axis=0).reshape(4, BLK, WIDTH)

    weight_part = jnp.stack(
        [
            lax.dot_general(dz_parts[dy], mixed, (((0,), (0,)), ((), ())), preferred_element_type=F32)
            for dy in range(NY)
        ]
    ).reshape(NY, 2 * NX, 2, W_ROWS, WIDTH)
    mine = jnp.where(core == 0, weight_part[:, :, 0], weight_part[:, :, 1])
    others = jnp.where(core == 0, weight_part[:, :, 1], weight_part[:, :, 0])
    bias_part = jnp.sum(dz_full, axis=0, keepdims=True)
    bias_rows = jnp.pad(bias_part, ((0, 7), (0, 0)))
    sent = jnp.concatenate([others.reshape(-1, WIDTH), bias_rows], axis=0)
    got = swap(sent, 1)
    weight_sums = (mine + got[:-8].reshape(mine.shape)).astype(BF16)

    chip_bias = bias_part + got[-8:-7]
    parts = []
    for call in range(len(BACKWARD_CHUNKS)):
        parts += backward(call, lists, tile_values, other_tiles, scaled_blocks, weight_sums, split(chip_bias))
    column_sum, bias_sum = scatter(parts, core, x, z, chip_bias)
    from_core_0 = lax.ppermute(bias_sum, "dom", [(i, i + 1) for i in range(0, NZ * NX * 2, 2)])
    bias_grad = jnp.where(core == 0, bias_sum, from_core_0)

    feats_grad = (scaled.astype(F32) + column_sum[:NODES]).astype(BF16)
    weight_grad = column_sum[NODES:].T
    return (output, feats_grad, weight_grad, bias_grad.reshape(WIDTH))


def solution(mesh):
    return jax.shard_map(
        on_device,
        mesh=mesh,
        in_specs=(
            P("dom", "feat"),
            P("feat", "dom"),
            P("feat"),
            P("dom", None, None),
            P("dom"),
            P("dom"),
            P("dom"),
            P("dom", "feat"),
        ),
        out_specs=(P("dom", "feat"), P("dom", "feat"), P("feat", "dom"), P("feat")),
        check_vma=False,
    )
```

```python
import functools

import jax
import jax.numpy as jnp
from jax import lax
from jax.experimental import pallas as pl
from jax.experimental.pallas import tpu as pltpu
from jax.sharding import PartitionSpec as P

F32 = jnp.float32
BF16 = jnp.bfloat16
NZ, NX, NY = 8, 4, 4
BLK = 128
SLOTS = 128
WIDTH = 256
NODES = 2 * BLK
W_ROWS = 16
ROWS = NODES + W_ROWS
UNROLL = 8
FETCH = 16
BIAS_ROWS = 16
SUM_ROWS = 4 * ROWS + BIAS_ROWS
MIB = 1 << 20
VMEM = 54 * MIB

LOW, HIGH, ACROSS = (0, 1, 7, 4), (2, 3, 6, 5), (0, 1, 3, 2)
GATHER_0 = tuple(
    tuple(k * NZ + j for j in group)
    for k, group in ((0, LOW), (1, LOW), (3, LOW), (2, LOW), (3, HIGH), (1, HIGH), (2, HIGH), (0, HIGH))
)
GATHER_1 = tuple(tuple(k * NZ + j for k in ACROSS) for j in (0, 1, 7, 2, 6, 3, 5)) + (
    None,
    tuple(k * NZ + 4 for k in ACROSS[:2]),
    tuple(k * NZ + 4 for k in ACROSS[2:]),
)
FORWARD_CHUNKS = ((0, 1, 2, 3, 4, 5, 6, 7), (8, 9))
SCATTER = (
    (
        (None, tuple((dx, 4) for dx in ACROSS)),
        (tuple((2, dz) for dz in HIGH), None),
        (tuple((3, dz) for dz in HIGH), None),
    ),
    (
        (None, tuple((dx, 3) for dx in ACROSS)),
        (None, tuple((dx, 5) for dx in ACROSS)),
        (tuple((1, dz) for dz in HIGH), tuple((dx, 2) for dx in ACROSS)),
        (tuple((2, dz) for dz in LOW), tuple((dx, 6) for dx in ACROSS)),
        (tuple((1, dz) for dz in LOW), tuple((dx, 1) for dx in ACROSS)),
        (tuple((3, dz) for dz in LOW), tuple((dx, 7) for dx in ACROSS)),
        (tuple((0, dz) for dz in HIGH), None),
        (tuple((0, dz) for dz in LOW), tuple((dx, 0) for dx in ACROSS)),
    ),
)


def shift(value, core_0=None, core_1=None):
    pairs = []
    for z in range(NZ):
        for x in range(NX):
            for core, step in enumerate((core_0, core_1)):
                if step is not None:
                    target = ((z + step[0]) % NZ * NX + (x + step[1]) % NX) * 2 + core
                    pairs.append(((z * NX + x) * 2 + core, target))
    return lax.ppermute(value, "dom", pairs)


Z_UP, Z_DOWN, Z_UP_2, Z_DOWN_2, Z_FOUR = (1, 0), (-1, 0), (2, 0), (-2, 0), (4, 0)
X_UP, X_DOWN, X_TWO = (0, 1), (0, -1), (0, 2)


def swap(value, bit):
    return lax.ppermute(value, "dom", [(i, i ^ bit) for i in range(NZ * NX * 2)])


def y_shift(value, dy):
    return lax.ppermute(value, "feat", [(y, (y + dy) % NY) for y in range(NY)])


def smem():
    return pl.BlockSpec(memory_space=pltpu.SMEM)


def vmem():
    return pl.BlockSpec(memory_space=pltpu.VMEM)


def anywhere():
    return pl.BlockSpec(memory_space=pl.ANY)


def list_kernel(place, own, sib, lists):
    core, x, z = place[0], place[1], place[2]
    wide = (1, 2 * SLOTS)
    column = jnp.concatenate([own[1:2], sib[1:2]], axis=1)
    row = jnp.concatenate([own[0:1], sib[0:1] + 2], axis=1)
    slot = lax.broadcasted_iota(jnp.int32, wide, 1)
    live = slot < jnp.where(slot < SLOTS, place[4], SLOTS + place[5])
    owner = column >> 1
    chip = owner >> 1
    k = (x - (chip & (NX - 1))) & (NX - 1)
    j = (z - (chip >> 2)) & (NZ - 1)
    spot = (k * NZ + j) * 2 + (column & 1)
    mine = live & ((owner & 1) == core)
    high = ((j >= 2) & (j <= 6)) & (j != 4)
    forward_call = jnp.where((core == 1) & (j == 4), 1, 0)
    backward_call = jnp.where(core == 0, jnp.where(high & ((k == 1) | (k == 2)), 0, 1), jnp.where(j == 4, 0, 1))
    square = (2 * SLOTS, 2 * SLOTS)
    first = lax.broadcasted_iota(jnp.int32, square, 0)
    second = lax.broadcasted_iota(jnp.int32, square, 1)
    up_to = jnp.where(first <= second, 1.0, 0.0).astype(BF16)
    group_of = lax.broadcasted_iota(jnp.int32, (16, 2 * SLOTS), 0)
    lane = lax.broadcasted_iota(jnp.int32, (16, 2 * SLOTS), 1)
    before = jnp.where(
        lax.broadcasted_iota(jnp.int32, (16, 16), 1) < lax.broadcasted_iota(jnp.int32, (16, 16), 0), 1.0, 0.0
    ).astype(BF16)
    values = jnp.concatenate([slot, spot], axis=0).astype(F32)
    values = jnp.concatenate([values, jnp.zeros((14, 2 * SLOTS), F32)], axis=0).astype(BF16)
    lists[...] = jnp.zeros_like(lists)
    for at, call in ((0, forward_call), (3, backward_call)):
        group = jnp.where(mine, call * 4 + row, -1)
        member = jnp.where(group_of == group, 1.0, 0.0)
        rank = jnp.dot(member.astype(BF16), up_to, preferred_element_type=F32)
        counts = jnp.sum(member, axis=1, keepdims=True)
        earlier = jnp.dot(before, member.astype(BF16), preferred_element_type=F32)
        starts = jnp.sum(earlier, axis=1, keepdims=True)
        goal = jnp.sum(member * (starts + rank), axis=0, keepdims=True).astype(jnp.int32) - 1
        moved = jnp.where(first == goal, 1.0, 0.0).astype(BF16)
        ordered = lax.dot_general(values, moved, (((1,), (1,)), ((), ())), preferred_element_type=F32)
        lists[at : at + 1, :] = jnp.sum(jnp.where(group_of == lane, counts, 0.0), axis=0, keepdims=True).astype(jnp.int32)
        lists[at + 1 : at + 2, :] = jnp.sum(jnp.where(group_of == lane, starts, 0.0), axis=0, keepdims=True).astype(jnp.int32)
        lists[at + 2 : at + 3, :] = (ordered[0:1] * 64.0 + ordered[1:2]).astype(jnp.int32)
    told = jnp.zeros(wide, jnp.int32)
    for i in range(6):
        told = jnp.where(slot == i, place[i], told)
    lists[6:7, :] = told


def make_lists(place, own, sib):
    return pl.pallas_call(
        list_kernel,
        out_shape=jax.ShapeDtypeStruct((8, 2 * SLOTS), jnp.int32),
        in_specs=[smem(), vmem(), vmem()],
        out_specs=vmem(),
    )(place, own, sib)


def place_of(lists):
    return [lists[6, i] for i in range(4)]


def copy_each(copies, action):
    for condition, copy in copies:
        call = getattr(copy, action)
        if condition is None:
            call()
        else:
            pl.when(condition)(call)


class Tiles:
    def __init__(self, lists, at, call, every, own, sib, held, sem):
        self.lists, self.at, self.call, self.every = lists, at, call, every
        self.own, self.sib, self.held, self.sem = own, sib, held, sem
        self.begin = lists[at + 1, call * 4]
        self.end = lists[at + 1, call * 4 + 3] + lists[at, call * 4 + 3]

    def bulk(self):
        copies = []
        for which, source in enumerate((self.own, self.sib)):
            for step in range(SLOTS // FETCH):
                first = step * FETCH
                copy = pltpu.make_async_copy(
                    source.at[pl.ds(first, FETCH)],
                    self.held.at[pl.ds(which * SLOTS + first, FETCH)],
                    self.sem.at[which * (SLOTS // FETCH) + step],
                )
                copies.append((first < self.lists[6, 4 + which], copy))
        return copies

    def each(self, action):
        def step(p, carry):
            slot = self.lists[self.at + 2, p] >> 6
            goal = self.held.at[p]

            @pl.when(slot < SLOTS)
            def _():
                getattr(pltpu.make_async_copy(self.own.at[jnp.minimum(slot, SLOTS - 1)], goal, self.sem.at[0]), action)()

            @pl.when(slot >= SLOTS)
            def _():
                getattr(pltpu.make_async_copy(self.sib.at[jnp.maximum(slot - SLOTS, 0)], goal, self.sem.at[0]), action)()

            return carry

        lax.fori_loop(self.begin, self.end, step, 0)

    def start(self):
        if self.every:
            copy_each(self.bulk(), "start")
        else:
            self.each("start")
        self.held[2 * SLOTS] = jnp.zeros((BLK, BLK), BF16)

    def wait(self):
        if self.every:
            copy_each(self.bulk(), "wait")
        else:
            self.each("wait")

    def rows(self):
        for row in range(4):
            group = self.call * 4 + row
            number, first = self.lists[self.at, group], self.lists[self.at + 1, group]

            def pick(it, number=number, first=first):
                lefts, spots = [], []
                for u in range(UNROLL):
                    p = it * UNROLL + u
                    entry = self.lists[self.at + 2, first + jnp.minimum(p, number - 1)]
                    place = entry >> 6 if self.every else first + p
                    lefts.append(self.held[jnp.where(p < number, place, 2 * SLOTS)])
                    spots.append(entry & 63)
                return jnp.concatenate(lefts, axis=1), spots

            yield row, lax.div(number + (UNROLL - 1), UNROLL), pick


def forward_kernel(call, lists, own, sib, *rest):
    chosen = FORWARD_CHUNKS[call]
    chunks, rest = rest[: len(chosen)], rest[len(chosen) :]
    if call:
        sums_before, weight_before, *rest = rest
    sums, weight_out, blocks, held, sem, tile_sem = rest
    core, x, z, y = place_of(lists)
    tiles = Tiles(lists, 0, call, call == 0, own, sib, held, tile_sem)
    tiles.start()
    copies, arrived = [], []
    for n, chunk in zip(chosen, chunks):
        condition = None if n < 7 else core == (0 if n == 7 else 1)
        for i in range(chunk.shape[0]):
            if n < 7:
                spot = jnp.where(core == 0, GATHER_0[n][i], GATHER_1[n][i])
            else:
                spot = GATHER_0[n][i] if n == 7 else GATHER_1[n][i]
            copies.append((condition, pltpu.make_async_copy(chunk.at[i], blocks.at[spot], sem.at[len(copies)])))
            arrived.append((condition, spot))
    copy_each(copies, "start")
    copy_each(copies, "wait")
    tiles.wait()
    for row, steps, pick in tiles.rows():

        def step(it, total):
            left, spots = pick(it)
            rights = []
            for spot in spots:
                first = pl.multiple_of((spot & 1) * BLK, BLK)
                rights.append(blocks[spot >> 1, pl.ds(first, BLK), :])
            return total + jnp.dot(left, jnp.concatenate(rights, axis=0), preferred_element_type=F32)

        sums[row] = lax.fori_loop(0, steps, step, sums_before[row] if call else jnp.zeros((BLK, WIDTH), F32))
    if call:
        weight_out[...] = weight_before[...]
    for condition, spot in arrived:

        def keep(spot=spot):
            column = (x - (spot >> 3)) & (NX - 1)
            level = (z - spot) & (NZ - 1)
            part = ((level >> 1) - y) & (NY - 1)
            weight_out[part, (level & 1) * NX + column] = blocks[spot, NODES:ROWS, :]

        if condition is None:
            keep()
        else:
            pl.when(condition)(keep)


def forward(call, lists, own, sib, chunks, before):
    chosen = [chunks[n] for n in FORWARD_CHUNKS[call]]
    return pl.pallas_call(
        functools.partial(forward_kernel, call),
        out_shape=(
            jax.ShapeDtypeStruct((4, BLK, WIDTH), F32),
            jax.ShapeDtypeStruct((NY, 2 * NX, W_ROWS, WIDTH), BF16),
        ),
        in_specs=[smem()] + [anywhere()] * (2 + len(chosen)) + [vmem()] * len(before),
        out_specs=(vmem(),) * 2,
        scratch_shapes=[
            pltpu.VMEM((NX * NZ, ROWS, WIDTH), BF16),
            pltpu.VMEM((2 * SLOTS + 1, BLK, BLK), BF16),
            pltpu.SemaphoreType.DMA((32,)),
            pltpu.SemaphoreType.DMA((2 * SLOTS // FETCH,)),
        ],
        compiler_params=pltpu.CompilerParams(vmem_limit_bytes=VMEM),
        cost_estimate=pl.CostEstimate(
            flops=2 * BLK * BLK * WIDTH * len(chosen) * 16, bytes_accessed=len(chosen) * MIB, transcendentals=0
        ),
    )(lists, own, sib, *chosen, *before)


def backward_kernel(call, lists, own, sib, scaled, weight_sums, bias_rows, *rest):
    chunks = SCATTER[call]
    outs, rest = rest[: len(chunks)], rest[len(chunks) :]
    total, held, tile_sem = rest
    core, x, z, y = place_of(lists)
    tiles = Tiles(lists, 3, call, call == 1, own, sib, held, tile_sem)
    tiles.start()

    def each_chunk(action):
        for out, chunk in zip(outs, chunks):
            if None in chunk:
                side = 1 if chunk[0] is None else 0

                @pl.when(core == side)
                def _(out=out, places=chunk[side]):
                    action(out, places)
            else:
                action(out, [[jnp.where(core == 0, p, q) for p, q in zip(*pair)] for pair in zip(*chunk)])

    def spot_of(dx, dz):
        return ((0 - dx) & (NX - 1)) * NZ + ((0 - dz) & (NZ - 1))

    def clear(out, places):
        for dx, dz in places:
            spot = spot_of(dx, dz)
            total[spot * 2] = jnp.zeros((BLK, WIDTH), F32)
            total[spot * 2 + 1] = jnp.zeros((BLK, WIDTH), F32)

    def emit(out, places):
        for i, (dx, dz) in enumerate(places):
            spot = spot_of(dx, dz)
            first = i * ROWS
            out[first : first + BLK, :] = total[spot * 2].astype(BF16)
            out[first + BLK : first + NODES, :] = total[spot * 2 + 1].astype(BF16)
            column = (x + dx) & (NX - 1)
            level = (z + dz) & (NZ - 1)
            part = ((level >> 1) - y) & (NY - 1)
            out[first + NODES : first + ROWS, :] = weight_sums[part, (level & 1) * NX + column]
        out[4 * ROWS : SUM_ROWS, :] = bias_rows[...] if call == 0 else jnp.zeros((BIAS_ROWS, WIDTH), BF16)

    each_chunk(clear)
    tiles.wait()
    for row, steps, pick in tiles.rows():
        right = scaled[row]

        def step(it, carry):
            left, spots = pick(it)
            terms = lax.dot_general(left, right, (((0,), (0,)), ((), ())), preferred_element_type=F32)
            for u, spot in enumerate(spots):
                total[spot] += terms[u * BLK : (u + 1) * BLK]
            return carry

        lax.fori_loop(0, steps, step, 0)
    each_chunk(emit)


def backward(call, lists, own, sib, scaled, weight_sums, bias_rows):
    shapes = []
    for _ in SCATTER[call]:
        shapes.append(jax.ShapeDtypeStruct((SUM_ROWS, WIDTH), BF16))
    return pl.pallas_call(
        functools.partial(backward_kernel, call),
        out_shape=tuple(shapes),
        in_specs=[smem()] + [anywhere()] * 2 + [vmem()] * 3,
        out_specs=(vmem(),) * len(shapes),
        scratch_shapes=[
            pltpu.VMEM((2 * NX * NZ, BLK, WIDTH), F32),
            pltpu.VMEM((2 * SLOTS + 1, BLK, BLK), BF16),
            pltpu.SemaphoreType.DMA((2 * SLOTS // FETCH,)),
        ],
        compiler_params=pltpu.CompilerParams(vmem_limit_bytes=VMEM),
        cost_estimate=pl.CostEstimate(
            flops=2 * BLK * BLK * WIDTH * len(shapes) * 16, bytes_accessed=len(shapes) * MIB, transcendentals=0
        ),
    )(lists, own, sib, scaled, weight_sums, bias_rows)


def gather(block, core, early, call):
    p1 = shift(block, Z_UP, X_UP)
    p2 = shift(block, Z_DOWN, X_DOWN)
    p3 = shift(block, Z_FOUR, X_TWO)
    pa = shift(jnp.stack([block, p1]), Z_UP_2)
    pb = shift(jnp.stack([block, p2]), Z_DOWN_2)
    low, *early = lax.optimization_barrier((jnp.stack([block, p1, p2, p3]), *early))
    c1 = shift(low, X_UP, Z_UP)
    c2 = shift(low, X_DOWN, Z_DOWN)
    c1, c2, pa, pb = lax.optimization_barrier((c1, c2, pa, pb))
    high = jnp.concatenate([pa, pb], axis=0)
    c3 = shift(c1, X_UP, Z_UP)
    c4 = shift(jnp.where(core == 0, high, c2), X_DOWN, Z_DOWN)
    c5 = shift(jnp.where(core == 0, high, c3), X_UP, Z_UP)
    c6 = shift(c4, X_DOWN, Z_DOWN)
    c7 = shift(c5[:2], None, Z_UP)
    c8 = shift(c6[2:], None, Z_DOWN)
    chunks = [low, c1, c2, c3, c4, c5, c6, high, c7, c8]
    return call(1, early, chunks, call(0, early, chunks, ()))


def add(*values):
    total = values[0].astype(F32)
    for value in values[1:]:
        total = total + value.astype(F32)
    return total


def split(value):
    high = lax.reduce_precision(value, 8, 7)
    middle = lax.reduce_precision(value - high, 8, 7)
    rows = jnp.concatenate([high, middle, value - high - middle], axis=0)
    return jnp.pad(rows, ((0, BIAS_ROWS - 3), (0, 0))).astype(BF16)


def rows_of(value):
    high = value.astype(BF16)
    middle = (value - high.astype(F32)).astype(BF16)
    low = (value - high.astype(F32) - middle.astype(F32)).astype(BF16)
    return [high.astype(F32), middle.astype(F32), low.astype(F32)]


def bias_block(rows):
    used = sum(row.shape[0] for row in rows)
    rows = rows + [jnp.zeros((BIAS_ROWS - used, WIDTH), F32)]
    return jnp.concatenate(rows, axis=0).astype(BF16)


def joined(block, first=0):
    rows = block.astype(F32)
    return rows[first : first + 1] + rows[first + 1 : first + 2] + rows[first + 2 : first + 3]


def in_order(values, place, held):
    count = len(values)
    for k, value in enumerate(values):
        held[k : k + 1, :] = value
    total = held[pl.ds(place & (count - 1), 1), :]
    for i in range(1, count):
        total = total + held[pl.ds((place - i) & (count - 1), 1), :]
    return total


def block_sum(i, *chunks):
    total = chunks[0][i * ROWS : (i + 1) * ROWS, :].astype(F32)
    for chunk in chunks[1:]:
        total = total + chunk[i * ROWS : (i + 1) * ROWS, :].astype(F32)
    return total


def tail_of(chunk):
    return chunk[4 * ROWS : SUM_ROWS, :]


def pair_kernel(lists, chip_bias, h0, ja1, ja2, jb1, pair_a, pair_b, line_bias, held):
    line = in_order([chip_bias[...], joined(tail_of(ja1)), joined(tail_of(jb1)), joined(tail_of(ja2))], lists[6, 1], held)
    line_bias[...] = line
    rows = bias_block(rows_of(line))
    for pair, first in ((pair_a, 0), (pair_b, 2)):
        for i in range(2):
            pair[i * ROWS : (i + 1) * ROWS, :] = block_sum(first + i, h0, jb1, ja2).astype(BF16)
        pair[2 * ROWS : 2 * ROWS + BIAS_ROWS, :] = rows


def message_kernel(line_bias, h1, jc1, jc2, ra, rb, m1, m2, m3, rest):
    own = rows_of(line_bias[...])
    rest[...] = block_sum(0, h1, jc1, jc2) + block_sum(0, ra, rb)
    relayed = [chunk[2 * ROWS : 2 * ROWS + BIAS_ROWS, :].astype(F32)[0:3] for chunk in (ra, rb)]
    m1[0:ROWS, :] = (block_sum(1, h1, jc1, jc2) + block_sum(1, ra)).astype(BF16)
    m1[ROWS:, :] = bias_block(own + [relayed[0]])
    m2[0:ROWS, :] = (block_sum(2, h1, jc1, jc2) + block_sum(1, rb)).astype(BF16)
    m2[ROWS:, :] = bias_block(own + [relayed[1]])
    m3[0:ROWS, :] = block_sum(3, h1, jc1, jc2).astype(BF16)
    m3[ROWS:, :] = bias_block(own)


def last_kernel(lists, line_bias, rest, r1, r2, r3, ra, rb, scaled, feats_grad, weight_grad, bias, held):
    total = rest[...] + block_sum(0, r1, r2, r3)
    feats_grad[...] = (scaled[...].astype(F32) + total[0:NODES]).astype(BF16)
    weight_grad[...] = total[NODES:ROWS]
    t1, t2, t3 = (chunk[ROWS:, :] for chunk in (r1, r2, r3))
    ta, tb = (chunk[2 * ROWS :, :] for chunk in (ra, rb))
    values = [line_bias[...], joined(t1), joined(ta), joined(t1, 3), joined(t3), joined(t2, 3), joined(tb), joined(t2)]
    bias[...] = in_order(values, lists[6, 2], held)


def small_call(kernel, shapes, lists, operands, scratch):
    first = [] if lists is None else [lists]
    return pl.pallas_call(
        kernel,
        out_shape=tuple(jax.ShapeDtypeStruct(shape, dtype) for shape, dtype in shapes),
        in_specs=[smem()] * len(first) + [vmem()] * len(operands),
        out_specs=(vmem(),) * len(shapes),
        scratch_shapes=[pltpu.VMEM((8, WIDTH), F32)] * scratch,
        compiler_params=pltpu.CompilerParams(vmem_limit_bytes=16 * MIB),
    )(*first, *operands)


def scatter(first, second, core, lists, chip_bias, scaled):
    first_up, x1, x2 = first
    y1, y2, b1, b2, q1, q2, h0, h1 = second
    zero = jnp.zeros((), BF16)
    j0 = shift(first_up, None, Z_UP)
    ja1 = shift(jnp.where(core == 0, x1, add(y1, j0).astype(BF16)), X_UP, Z_UP)
    ja2 = shift(jnp.where(core == 0, x2, y2), X_DOWN, Z_DOWN)
    jb1 = shift(add(b1, ja1).astype(BF16), X_UP, Z_UP)
    jb2 = shift(add(b2, jnp.where(core == 0, zero, ja2)).astype(BF16), X_DOWN, Z_DOWN)
    wide = (2 * ROWS + BIAS_ROWS, WIDTH)
    pair_a, pair_b, line_bias = small_call(
        pair_kernel, ((wide, BF16), (wide, BF16), ((1, WIDTH), F32)), lists, (chip_bias, h0, ja1, ja2, jb1), 1
    )
    ra = shift(pair_a, Z_UP_2)
    rb = shift(pair_b, Z_DOWN_2)
    jc1 = shift(add(q1, jnp.where(core == 0, zero, jb1)).astype(BF16), X_UP, Z_UP)
    jc2 = shift(add(q2, jb2).astype(BF16), X_DOWN, Z_DOWN)
    size = (ROWS + BIAS_ROWS, WIDTH)
    m1, m2, m3, rest = small_call(
        message_kernel,
        ((size, BF16), (size, BF16), (size, BF16), ((ROWS, WIDTH), F32)),
        None,
        (line_bias, h1, jc1, jc2, ra, rb),
        0,
    )
    r1 = shift(m1, Z_UP, X_UP)
    r2 = shift(m2, Z_DOWN, X_DOWN)
    r3 = shift(m3, Z_FOUR, X_TWO)
    return small_call(
        last_kernel,
        (((NODES, WIDTH), BF16), ((W_ROWS, WIDTH), F32), ((1, WIDTH), F32)),
        lists,
        (line_bias, rest, r1, r2, r3, ra, rb, scaled),
        1,
    )


def nothing(value):
    return jnp.minimum(jnp.abs(value.astype(F32)), 0.0).astype(BF16)


def silu_parts(hidden):
    gate_value = jax.nn.sigmoid(hidden)
    return (hidden * gate_value, gate_value * (1.0 + hidden * (1.0 - gate_value)))


def on_device(feats, weight, bias, tile_values, tile_rows, tile_cols, tile_live, cotangent):
    dom = lax.axis_index("dom")
    y = lax.axis_index("feat")
    core = dom % 2
    x = (dom // 2) % NX
    z = dom // (2 * NX)

    meta = jnp.stack([tile_rows, tile_cols, jnp.broadcast_to(tile_live, (SLOTS,))])
    other_meta = swap(meta, 1)
    place = jnp.stack([core, x, z, y, tile_live[0], other_meta[2, 0]]).astype(jnp.int32)
    lists = make_lists(place, meta, other_meta)

    own_live = jnp.arange(SLOTS, dtype=jnp.int32) < tile_live[0]
    row_sums = jnp.sum(tile_values, axis=2, dtype=F32)
    degree = 1.0 + jnp.concatenate(
        [
            jnp.sum(jnp.where((own_live & (tile_rows == row))[:, None], row_sums, 0.0), axis=0)
            for row in range(2)
        ]
    ).reshape(NODES, 1)

    other_tiles = swap(tile_values, 1)
    sums, weight_lane = gather(
        jnp.concatenate([feats, weight.T], axis=0),
        core,
        (lists, other_tiles),
        lambda call, early, chunks, before: forward(call, early[0], tile_values, early[1], chunks, before),
    )
    neighbour_sum = (sums[:2] + swap(sums[2:], 1)).reshape(NODES, WIDTH)
    weight_other = swap(weight_lane, 1)
    mixed = ((feats.astype(F32) + neighbour_sum) / degree).astype(BF16)

    first = jnp.where(core == 0, weight_lane, weight_other)
    second = jnp.where(core == 0, weight_other, weight_lane)
    weight_t = jnp.stack([first, second], axis=2).reshape(NY, WIDTH, WIDTH)

    def hidden_part(dy):
        return lax.dot_general(mixed, weight_t[dy], (((1,), (1,)), ((), ())), preferred_element_type=F32)

    hidden = add(
        hidden_part(0),
        y_shift(hidden_part(1).astype(BF16), 1),
        y_shift(hidden_part(2).astype(BF16), 2),
        y_shift(hidden_part(3).astype(BF16), 3),
    ) + bias
    activated, slope = silu_parts(hidden)
    output = activated.astype(BF16)
    dz_full = cotangent.astype(F32) * slope
    dz_own = dz_full.astype(BF16)
    dz_parts = [dz_own] + [y_shift(dz_own, NY - dy) for dy in range(1, NY)]

    dmixed = sum(jnp.dot(dz_parts[dy], weight_t[dy], preferred_element_type=F32) for dy in range(NY))
    scaled = (dmixed / degree).astype(BF16)
    scaled_blocks = jnp.concatenate([scaled, swap(scaled, 1)], axis=0).reshape(4, BLK, WIDTH)

    weight_part = jnp.stack(
        [
            lax.dot_general(dz_parts[dy], mixed, (((0,), (0,)), ((), ())), preferred_element_type=F32)
            for dy in range(NY)
        ]
    ).reshape(NY, 2 * NX, 2, W_ROWS, WIDTH)
    mine = jnp.where(core == 0, weight_part[:, :, 0], weight_part[:, :, 1])
    others = jnp.where(core == 0, weight_part[:, :, 1], weight_part[:, :, 0])
    bias_part = jnp.sum(dz_full, axis=0, keepdims=True)
    sent = jnp.concatenate([others.reshape(-1, WIDTH), jnp.pad(bias_part, ((0, 7), (0, 0)))], axis=0)
    got = swap(sent, 1)
    weight_sums = (mine + got[:-8].reshape(mine.shape)).astype(BF16)

    chip_bias = bias_part + got[-8:-7]
    bias_rows = split(chip_bias)
    parts = [
        backward(call, lists, tile_values, other_tiles, scaled_blocks, weight_sums, bias_rows)
        for call in range(len(SCATTER))
    ]
    feats_grad, weight_sum, bias_sum = scatter(*parts, core, lists, chip_bias, scaled)
    from_core_0 = lax.ppermute(bias_sum, "dom", [(i, i + 1) for i in range(0, NZ * NX * 2, 2)])
    bias_grad = jnp.where(core == 0, bias_sum, from_core_0)

    return (output, feats_grad, weight_sum.T, bias_grad.reshape(WIDTH))


def solution(mesh):
    return jax.shard_map(
        on_device,
        mesh=mesh,
        in_specs=(
            P("dom", "feat"),
            P("feat", "dom"),
            P("feat"),
            P("dom", None, None),
            P("dom"),
            P("dom"),
            P("dom"),
            P("dom", "feat"),
        ),
        out_specs=(P("dom", "feat"), P("dom", "feat"), P("feat", "dom"), P("feat")),
        check_vma=False,
    )
```

```python
import functools

import jax
import jax.numpy as jnp
from jax import lax
from jax.experimental import pallas as pl
from jax.experimental.pallas import tpu as pltpu
from jax.sharding import PartitionSpec as P

F32 = jnp.float32
BF16 = jnp.bfloat16
NZ, NX, NY = 8, 4, 4
BLK = 128
SLOTS = 128
WIDTH = 256
NODES = 2 * BLK
W_ROWS = 16
ROWS = NODES + W_ROWS
UNROLL = 8
FETCH = 16
BIAS_ROWS = 16
SUM_ROWS = 4 * ROWS + BIAS_ROWS
MIB = 1 << 20
VMEM = 54 * MIB

LOW, HIGH, ACROSS = (0, 1, 7, 4), (2, 3, 6, 5), (0, 1, 3, 2)
GATHER_0 = tuple(
    tuple(k * NZ + j for j in group)
    for k, group in ((0, LOW), (1, LOW), (3, LOW), (2, LOW), (3, HIGH), (1, HIGH), (2, HIGH), (0, HIGH))
)
GATHER_1 = tuple(tuple(k * NZ + j for k in ACROSS) for j in (0, 1, 7, 2, 6, 3, 5)) + (
    None,
    tuple(k * NZ + 4 for k in ACROSS[:2]),
    tuple(k * NZ + 4 for k in ACROSS[2:]),
)
FORWARD_CHUNKS = ((0, 1, 2, 3, 4, 7), (5, 6), (8, 9))
SCATTER = (
    (
        (None, tuple((dx, 4) for dx in ACROSS)),
        (tuple((2, dz) for dz in HIGH), None),
        (tuple((3, dz) for dz in HIGH), None),
    ),
    (
        (None, tuple((dx, 3) for dx in ACROSS)),
        (None, tuple((dx, 5) for dx in ACROSS)),
        (tuple((1, dz) for dz in HIGH), tuple((dx, 2) for dx in ACROSS)),
        (tuple((2, dz) for dz in LOW), tuple((dx, 6) for dx in ACROSS)),
        (tuple((1, dz) for dz in LOW), tuple((dx, 1) for dx in ACROSS)),
        (tuple((3, dz) for dz in LOW), tuple((dx, 7) for dx in ACROSS)),
        (tuple((0, dz) for dz in HIGH), None),
        (tuple((0, dz) for dz in LOW), tuple((dx, 0) for dx in ACROSS)),
    ),
)


def shift(value, core_0=None, core_1=None):
    pairs = []
    for z in range(NZ):
        for x in range(NX):
            for core, step in enumerate((core_0, core_1)):
                if step is not None:
                    target = ((z + step[0]) % NZ * NX + (x + step[1]) % NX) * 2 + core
                    pairs.append(((z * NX + x) * 2 + core, target))
    return lax.ppermute(value, "dom", pairs)


Z_UP, Z_DOWN, Z_UP_2, Z_DOWN_2, Z_FOUR = (1, 0), (-1, 0), (2, 0), (-2, 0), (4, 0)
X_UP, X_DOWN, X_TWO = (0, 1), (0, -1), (0, 2)


def swap(value, bit):
    return lax.ppermute(value, "dom", [(i, i ^ bit) for i in range(NZ * NX * 2)])


def y_shift(value, dy):
    return lax.ppermute(value, "feat", [(y, (y + dy) % NY) for y in range(NY)])


def smem():
    return pl.BlockSpec(memory_space=pltpu.SMEM)


def vmem():
    return pl.BlockSpec(memory_space=pltpu.VMEM)


def anywhere():
    return pl.BlockSpec(memory_space=pl.ANY)


def list_kernel(place, own, sib, lists):
    core, x, z = place[0], place[1], place[2]
    wide = (1, 2 * SLOTS)
    column = jnp.concatenate([own[1:2], sib[1:2]], axis=1)
    row = jnp.concatenate([own[0:1], sib[0:1] + 2], axis=1)
    slot = lax.broadcasted_iota(jnp.int32, wide, 1)
    live = slot < jnp.where(slot < SLOTS, place[4], SLOTS + place[5])
    owner = column >> 1
    chip = owner >> 1
    k = (x - (chip & (NX - 1))) & (NX - 1)
    j = (z - (chip >> 2)) & (NZ - 1)
    spot = (k * NZ + j) * 2 + (column & 1)
    mine = live & ((owner & 1) == core)
    high = ((j >= 2) & (j <= 6)) & (j != 4)
    on_0 = jnp.where(high & ((k == 1) | (k == 2)), 1, 0)
    on_1 = jnp.where(j == 4, 2, jnp.where((j == 3) | (j == 5), 1, 0))
    forward_call = jnp.where(core == 0, on_0, on_1)
    backward_call = jnp.where(core == 0, jnp.where(high & ((k == 1) | (k == 2)), 0, 1), jnp.where(j == 4, 0, 1))
    square = (2 * SLOTS, 2 * SLOTS)
    first = lax.broadcasted_iota(jnp.int32, square, 0)
    second = lax.broadcasted_iota(jnp.int32, square, 1)
    up_to = jnp.where(first <= second, 1.0, 0.0).astype(BF16)
    group_of = lax.broadcasted_iota(jnp.int32, (16, 2 * SLOTS), 0)
    lane = lax.broadcasted_iota(jnp.int32, (16, 2 * SLOTS), 1)
    before = jnp.where(
        lax.broadcasted_iota(jnp.int32, (16, 16), 1) < lax.broadcasted_iota(jnp.int32, (16, 16), 0), 1.0, 0.0
    ).astype(BF16)
    values = jnp.concatenate([slot, spot], axis=0).astype(F32)
    values = jnp.concatenate([values, jnp.zeros((14, 2 * SLOTS), F32)], axis=0).astype(BF16)
    lists[...] = jnp.zeros_like(lists)
    for at, call in ((0, forward_call), (3, backward_call)):
        group = jnp.where(mine, call * 4 + row, -1)
        member = jnp.where(group_of == group, 1.0, 0.0)
        rank = jnp.dot(member.astype(BF16), up_to, preferred_element_type=F32)
        counts = jnp.sum(member, axis=1, keepdims=True)
        earlier = jnp.dot(before, member.astype(BF16), preferred_element_type=F32)
        starts = jnp.sum(earlier, axis=1, keepdims=True)
        goal = jnp.sum(member * (starts + rank), axis=0, keepdims=True).astype(jnp.int32) - 1
        moved = jnp.where(first == goal, 1.0, 0.0).astype(BF16)
        ordered = lax.dot_general(values, moved, (((1,), (1,)), ((), ())), preferred_element_type=F32)
        lists[at : at + 1, :] = jnp.sum(jnp.where(group_of == lane, counts, 0.0), axis=0, keepdims=True).astype(jnp.int32)
        lists[at + 1 : at + 2, :] = jnp.sum(jnp.where(group_of == lane, starts, 0.0), axis=0, keepdims=True).astype(jnp.int32)
        lists[at + 2 : at + 3, :] = (ordered[0:1] * 64.0 + ordered[1:2]).astype(jnp.int32)
    told = jnp.zeros(wide, jnp.int32)
    for i in range(6):
        told = jnp.where(slot == i, place[i], told)
    lists[6:7, :] = told


def make_lists(place, own, sib):
    return pl.pallas_call(
        list_kernel,
        out_shape=jax.ShapeDtypeStruct((8, 2 * SLOTS), jnp.int32),
        in_specs=[smem(), vmem(), vmem()],
        out_specs=vmem(),
    )(place, own, sib)


def place_of(lists):
    return [lists[6, i] for i in range(4)]


def copy_each(copies, action):
    for condition, copy in copies:
        call = getattr(copy, action)
        if condition is None:
            call()
        else:
            pl.when(condition)(call)


class Tiles:
    def __init__(self, lists, at, call, every, own, sib, held, sem):
        self.lists, self.at, self.call, self.every = lists, at, call, every
        self.own, self.sib, self.held, self.sem = own, sib, held, sem
        self.begin = lists[at + 1, call * 4]
        self.end = lists[at + 1, call * 4 + 3] + lists[at, call * 4 + 3]

    def bulk(self):
        copies = []
        for which, source in enumerate((self.own, self.sib)):
            for step in range(SLOTS // FETCH):
                first = step * FETCH
                copy = pltpu.make_async_copy(
                    source.at[pl.ds(first, FETCH)],
                    self.held.at[pl.ds(which * SLOTS + first, FETCH)],
                    self.sem.at[which * (SLOTS // FETCH) + step],
                )
                copies.append((first < self.lists[6, 4 + which], copy))
        return copies

    def each(self, action):
        def step(p, carry):
            slot = self.lists[self.at + 2, p] >> 6
            goal = self.held.at[p]

            @pl.when(slot < SLOTS)
            def _():
                getattr(pltpu.make_async_copy(self.own.at[jnp.minimum(slot, SLOTS - 1)], goal, self.sem.at[0]), action)()

            @pl.when(slot >= SLOTS)
            def _():
                getattr(pltpu.make_async_copy(self.sib.at[jnp.maximum(slot - SLOTS, 0)], goal, self.sem.at[0]), action)()

            return carry

        lax.fori_loop(self.begin, self.end, step, 0)

    def start(self):
        if self.every:
            copy_each(self.bulk(), "start")
        else:
            self.each("start")
        self.held[2 * SLOTS] = jnp.zeros((BLK, BLK), BF16)

    def wait(self):
        if self.every:
            copy_each(self.bulk(), "wait")
        else:
            self.each("wait")

    def rows(self):
        for row in range(4):
            group = self.call * 4 + row
            number, first = self.lists[self.at, group], self.lists[self.at + 1, group]

            def pick(it, number=number, first=first):
                lefts, spots = [], []
                for u in range(UNROLL):
                    p = it * UNROLL + u
                    entry = self.lists[self.at + 2, first + jnp.minimum(p, number - 1)]
                    place = entry >> 6 if self.every else first + p
                    lefts.append(self.held[jnp.where(p < number, place, 2 * SLOTS)])
                    spots.append(entry & 63)
                return jnp.concatenate(lefts, axis=1), spots

            yield row, lax.div(number + (UNROLL - 1), UNROLL), pick


def forward_kernel(call, lists, own, sib, *rest):
    chosen = FORWARD_CHUNKS[call]
    chunks, rest = rest[: len(chosen)], rest[len(chosen) :]
    if call:
        sums_before, weight_before, *rest = rest
    sums, weight_out, blocks, held, sem, tile_sem = rest
    core, x, z, y = place_of(lists)
    tiles = Tiles(lists, 0, call, call == 0, own, sib, held, tile_sem)
    tiles.start()
    copies, arrived = [], []
    for n, chunk in zip(chosen, chunks):
        condition = None if n < 7 else core == (0 if n == 7 else 1)
        for i in range(chunk.shape[0]):
            if n < 7:
                spot = jnp.where(core == 0, GATHER_0[n][i], GATHER_1[n][i])
            else:
                spot = GATHER_0[n][i] if n == 7 else GATHER_1[n][i]
            copies.append((condition, pltpu.make_async_copy(chunk.at[i], blocks.at[spot], sem.at[len(copies)])))
            arrived.append((condition, spot))
    copy_each(copies, "start")
    copy_each(copies, "wait")
    tiles.wait()
    for row, steps, pick in tiles.rows():

        def step(it, total):
            left, spots = pick(it)
            rights = []
            for spot in spots:
                first = pl.multiple_of((spot & 1) * BLK, BLK)
                rights.append(blocks[spot >> 1, pl.ds(first, BLK), :])
            return total + jnp.dot(left, jnp.concatenate(rights, axis=0), preferred_element_type=F32)

        sums[row] = lax.fori_loop(0, steps, step, sums_before[row] if call else jnp.zeros((BLK, WIDTH), F32))
    if call:
        weight_out[...] = weight_before[...]
    for condition, spot in arrived:

        def keep(spot=spot):
            column = (x - (spot >> 3)) & (NX - 1)
            level = (z - spot) & (NZ - 1)
            part = ((level >> 1) - y) & (NY - 1)
            weight_out[part, (level & 1) * NX + column] = blocks[spot, NODES:ROWS, :]

        if condition is None:
            keep()
        else:
            pl.when(condition)(keep)


def forward(call, lists, own, sib, chunks, before):
    chosen = [chunks[n] for n in FORWARD_CHUNKS[call]]
    return pl.pallas_call(
        functools.partial(forward_kernel, call),
        out_shape=(
            jax.ShapeDtypeStruct((4, BLK, WIDTH), F32),
            jax.ShapeDtypeStruct((NY, 2 * NX, W_ROWS, WIDTH), BF16),
        ),
        in_specs=[smem()] + [anywhere()] * (2 + len(chosen)) + [vmem()] * len(before),
        out_specs=(vmem(),) * 2,
        scratch_shapes=[
            pltpu.VMEM((NX * NZ, ROWS, WIDTH), BF16),
            pltpu.VMEM((2 * SLOTS + 1, BLK, BLK), BF16),
            pltpu.SemaphoreType.DMA((32,)),
            pltpu.SemaphoreType.DMA((2 * SLOTS // FETCH,)),
        ],
        compiler_params=pltpu.CompilerParams(vmem_limit_bytes=VMEM),
        cost_estimate=pl.CostEstimate(
            flops=2 * BLK * BLK * WIDTH * len(chosen) * 16, bytes_accessed=len(chosen) * MIB, transcendentals=0
        ),
    )(lists, own, sib, *chosen, *before)


def backward_kernel(call, lists, own, sib, scaled, weight_sums, bias_rows, *rest):
    chunks = SCATTER[call]
    outs, rest = rest[: len(chunks)], rest[len(chunks) :]
    total, held, tile_sem = rest
    core, x, z, y = place_of(lists)
    tiles = Tiles(lists, 3, call, call == 1, own, sib, held, tile_sem)
    tiles.start()

    def each_chunk(action):
        for out, chunk in zip(outs, chunks):
            if None in chunk:
                side = 1 if chunk[0] is None else 0

                @pl.when(core == side)
                def _(out=out, places=chunk[side]):
                    action(out, places)
            else:
                action(out, [[jnp.where(core == 0, p, q) for p, q in zip(*pair)] for pair in zip(*chunk)])

    def spot_of(dx, dz):
        return ((0 - dx) & (NX - 1)) * NZ + ((0 - dz) & (NZ - 1))

    def clear(out, places):
        for dx, dz in places:
            spot = spot_of(dx, dz)
            total[spot * 2] = jnp.zeros((BLK, WIDTH), F32)
            total[spot * 2 + 1] = jnp.zeros((BLK, WIDTH), F32)

    def emit(out, places):
        for i, (dx, dz) in enumerate(places):
            spot = spot_of(dx, dz)
            first = i * ROWS
            out[first : first + BLK, :] = total[spot * 2].astype(BF16)
            out[first + BLK : first + NODES, :] = total[spot * 2 + 1].astype(BF16)
            column = (x + dx) & (NX - 1)
            level = (z + dz) & (NZ - 1)
            part = ((level >> 1) - y) & (NY - 1)
            out[first + NODES : first + ROWS, :] = weight_sums[part, (level & 1) * NX + column]
        out[4 * ROWS : SUM_ROWS, :] = bias_rows[...] if call == 0 else jnp.zeros((BIAS_ROWS, WIDTH), BF16)

    each_chunk(clear)
    tiles.wait()
    for row, steps, pick in tiles.rows():
        right = scaled[row]

        def step(it, carry):
            left, spots = pick(it)
            terms = lax.dot_general(left, right, (((0,), (0,)), ((), ())), preferred_element_type=F32)
            for u, spot in enumerate(spots):
                total[spot] += terms[u * BLK : (u + 1) * BLK]
            return carry

        lax.fori_loop(0, steps, step, 0)
    each_chunk(emit)


def backward(call, lists, own, sib, scaled, weight_sums, bias_rows):
    shapes = []
    for _ in SCATTER[call]:
        shapes.append(jax.ShapeDtypeStruct((SUM_ROWS, WIDTH), BF16))
    return pl.pallas_call(
        functools.partial(backward_kernel, call),
        out_shape=tuple(shapes),
        in_specs=[smem()] + [anywhere()] * 2 + [vmem()] * 3,
        out_specs=(vmem(),) * len(shapes),
        scratch_shapes=[
            pltpu.VMEM((2 * NX * NZ, BLK, WIDTH), F32),
            pltpu.VMEM((2 * SLOTS + 1, BLK, BLK), BF16),
            pltpu.SemaphoreType.DMA((2 * SLOTS // FETCH,)),
        ],
        compiler_params=pltpu.CompilerParams(vmem_limit_bytes=VMEM),
        cost_estimate=pl.CostEstimate(
            flops=2 * BLK * BLK * WIDTH * len(shapes) * 16, bytes_accessed=len(shapes) * MIB, transcendentals=0
        ),
    )(lists, own, sib, scaled, weight_sums, bias_rows)


def gather(block, core, early, call):
    p1 = shift(block, Z_UP, X_UP)
    p2 = shift(block, Z_DOWN, X_DOWN)
    p3 = shift(block, Z_FOUR, X_TWO)
    pa = shift(jnp.stack([block, p1]), Z_UP_2)
    pb = shift(jnp.stack([block, p2]), Z_DOWN_2)
    low, pa, pb, *early = lax.optimization_barrier((jnp.stack([block, p1, p2, p3]), pa, pb, *early))
    c1 = shift(low, X_UP, Z_UP)
    c2 = shift(low, X_DOWN, Z_DOWN)
    high = jnp.concatenate([pa, pb], axis=0)
    c1, c2 = lax.optimization_barrier((c1, c2))
    c3 = shift(c1, X_UP, Z_UP)
    c4 = shift(jnp.where(core == 0, high, c2), X_DOWN, Z_DOWN)
    c3, c4 = lax.optimization_barrier((c3, c4))
    chunks = [low, c1, c2, c3, c4, None, None, high]
    sums = call(0, early, chunks, ())
    c5 = shift(jnp.where(core == 0, high, c3), X_UP, Z_UP)
    c6 = shift(c4, X_DOWN, Z_DOWN)
    c5, c6, sums = lax.optimization_barrier((c5, c6, sums))
    chunks[5:7] = c5, c6
    chunks += [shift(c5[:2], None, Z_UP), shift(c6[2:], None, Z_DOWN)]
    return call(2, early, chunks, call(1, early, chunks, sums))


def add(*values):
    total = values[0].astype(F32)
    for value in values[1:]:
        total = total + value.astype(F32)
    return total


def split(value):
    high = lax.reduce_precision(value, 8, 7)
    middle = lax.reduce_precision(value - high, 8, 7)
    rows = jnp.concatenate([high, middle, value - high - middle], axis=0)
    return jnp.pad(rows, ((0, BIAS_ROWS - 3), (0, 0))).astype(BF16)


def rows_of(value):
    high = value.astype(BF16)
    middle = (value - high.astype(F32)).astype(BF16)
    low = (value - high.astype(F32) - middle.astype(F32)).astype(BF16)
    return [high.astype(F32), middle.astype(F32), low.astype(F32)]


def bias_block(rows):
    used = sum(row.shape[0] for row in rows)
    rows = rows + [jnp.zeros((BIAS_ROWS - used, WIDTH), F32)]
    return jnp.concatenate(rows, axis=0).astype(BF16)


def joined(block, first=0):
    rows = block.astype(F32)
    return rows[first : first + 1] + rows[first + 1 : first + 2] + rows[first + 2 : first + 3]


def in_order(values, place, held):
    count = len(values)
    for k, value in enumerate(values):
        held[k : k + 1, :] = value
    total = held[pl.ds(place & (count - 1), 1), :]
    for i in range(1, count):
        total = total + held[pl.ds((place - i) & (count - 1), 1), :]
    return total


def block_sum(i, *chunks):
    total = chunks[0][i * ROWS : (i + 1) * ROWS, :].astype(F32)
    for chunk in chunks[1:]:
        total = total + chunk[i * ROWS : (i + 1) * ROWS, :].astype(F32)
    return total


def tail_of(chunk):
    return chunk[4 * ROWS : SUM_ROWS, :]


def pair_kernel(lists, chip_bias, h0, ja1, ja2, jb1, pair_a, pair_b, line_bias, held):
    line = in_order([chip_bias[...], joined(tail_of(ja1)), joined(tail_of(jb1)), joined(tail_of(ja2))], lists[6, 1], held)
    line_bias[...] = line
    rows = bias_block(rows_of(line))
    for pair, first in ((pair_a, 0), (pair_b, 2)):
        for i in range(2):
            pair[i * ROWS : (i + 1) * ROWS, :] = block_sum(first + i, h0, jb1, ja2).astype(BF16)
        pair[2 * ROWS : 2 * ROWS + BIAS_ROWS, :] = rows


def message_kernel(line_bias, h1, jc1, jc2, ra, rb, m1, m2, m3, rest):
    own = rows_of(line_bias[...])
    rest[...] = block_sum(0, h1, jc1, jc2) + block_sum(0, ra, rb)
    relayed = [chunk[2 * ROWS : 2 * ROWS + BIAS_ROWS, :].astype(F32)[0:3] for chunk in (ra, rb)]
    m1[0:ROWS, :] = (block_sum(1, h1, jc1, jc2) + block_sum(1, ra)).astype(BF16)
    m1[ROWS:, :] = bias_block(own + [relayed[0]])
    m2[0:ROWS, :] = (block_sum(2, h1, jc1, jc2) + block_sum(1, rb)).astype(BF16)
    m2[ROWS:, :] = bias_block(own + [relayed[1]])
    m3[0:ROWS, :] = block_sum(3, h1, jc1, jc2).astype(BF16)
    m3[ROWS:, :] = bias_block(own)


def last_kernel(lists, line_bias, rest, r1, r2, r3, ra, rb, scaled, feats_grad, weight_grad, bias, held):
    total = rest[...] + block_sum(0, r1, r2, r3)
    feats_grad[...] = (scaled[...].astype(F32) + total[0:NODES]).astype(BF16)
    weight_grad[...] = total[NODES:ROWS]
    t1, t2, t3 = (chunk[ROWS:, :] for chunk in (r1, r2, r3))
    ta, tb = (chunk[2 * ROWS :, :] for chunk in (ra, rb))
    values = [line_bias[...], joined(t1), joined(ta), joined(t1, 3), joined(t3), joined(t2, 3), joined(tb), joined(t2)]
    bias[...] = in_order(values, lists[6, 2], held)


def small_call(kernel, shapes, lists, operands, scratch):
    first = [] if lists is None else [lists]
    return pl.pallas_call(
        kernel,
        out_shape=tuple(jax.ShapeDtypeStruct(shape, dtype) for shape, dtype in shapes),
        in_specs=[smem()] * len(first) + [vmem()] * len(operands),
        out_specs=(vmem(),) * len(shapes),
        scratch_shapes=[pltpu.VMEM((8, WIDTH), F32)] * scratch,
        compiler_params=pltpu.CompilerParams(vmem_limit_bytes=16 * MIB),
    )(*first, *operands)


def scatter(first, second, core, lists, chip_bias, scaled):
    first_up, x1, x2 = first
    y1, y2, b1, b2, q1, q2, h0, h1 = second
    zero = jnp.zeros((), BF16)
    j0 = shift(first_up, None, Z_UP)
    ja1 = shift(jnp.where(core == 0, x1, add(y1, j0).astype(BF16)), X_UP, Z_UP)
    ja2 = shift(jnp.where(core == 0, x2, y2), X_DOWN, Z_DOWN)
    ja1, ja2 = lax.optimization_barrier((ja1, ja2))
    jb1 = shift(add(b1, ja1).astype(BF16), X_UP, Z_UP)
    jb2 = shift(add(b2, jnp.where(core == 0, zero, ja2)).astype(BF16), X_DOWN, Z_DOWN)
    jb1, jb2 = lax.optimization_barrier((jb1, jb2))
    wide = (2 * ROWS + BIAS_ROWS, WIDTH)
    pair_a, pair_b, line_bias = small_call(
        pair_kernel, ((wide, BF16), (wide, BF16), ((1, WIDTH), F32)), lists, (chip_bias, h0, ja1, ja2, jb1), 1
    )
    jc1 = shift(add(q1, jnp.where(core == 0, zero, jb1)).astype(BF16), X_UP, Z_UP)
    jc2 = shift(add(q2, jb2).astype(BF16), X_DOWN, Z_DOWN)
    jc1, jc2, pair_a, pair_b = lax.optimization_barrier((jc1, jc2, pair_a, pair_b))
    ra = shift(pair_a, Z_UP_2)
    rb = shift(pair_b, Z_DOWN_2)
    size = (ROWS + BIAS_ROWS, WIDTH)
    m1, m2, m3, rest = small_call(
        message_kernel,
        ((size, BF16), (size, BF16), (size, BF16), ((ROWS, WIDTH), F32)),
        None,
        (line_bias, h1, jc1, jc2, ra, rb),
        0,
    )
    r1 = shift(m1, Z_UP, X_UP)
    r2 = shift(m2, Z_DOWN, X_DOWN)
    r3 = shift(m3, Z_FOUR, X_TWO)
    return small_call(
        last_kernel,
        (((NODES, WIDTH), BF16), ((W_ROWS, WIDTH), F32), ((1, WIDTH), F32)),
        lists,
        (line_bias, rest, r1, r2, r3, ra, rb, scaled),
        1,
    )


def nothing(value):
    return jnp.minimum(jnp.abs(value.astype(F32)), 0.0).astype(BF16)


def silu_parts(hidden):
    gate_value = jax.nn.sigmoid(hidden)
    return (hidden * gate_value, gate_value * (1.0 + hidden * (1.0 - gate_value)))


def on_device(feats, weight, bias, tile_values, tile_rows, tile_cols, tile_live, cotangent):
    dom = lax.axis_index("dom")
    y = lax.axis_index("feat")
    core = dom % 2
    x = (dom // 2) % NX
    z = dom // (2 * NX)

    meta = jnp.stack([tile_rows, tile_cols, jnp.broadcast_to(tile_live, (SLOTS,))])
    other_meta = swap(meta, 1)
    place = jnp.stack([core, x, z, y, tile_live[0], other_meta[2, 0]]).astype(jnp.int32)
    lists = make_lists(place, meta, other_meta)

    own_live = jnp.arange(SLOTS, dtype=jnp.int32) < tile_live[0]
    row_sums = jnp.sum(tile_values, axis=2, dtype=F32)
    degree = 1.0 + jnp.concatenate(
        [
            jnp.sum(jnp.where((own_live & (tile_rows == row))[:, None], row_sums, 0.0), axis=0)
            for row in range(2)
        ]
    ).reshape(NODES, 1)

    other_tiles = swap(tile_values, 1)
    sums, weight_lane = gather(
        jnp.concatenate([feats, weight.T], axis=0),
        core,
        (lists, other_tiles),
        lambda call, early, chunks, before: forward(call, early[0], tile_values, early[1], chunks, before),
    )
    neighbour_sum = (sums[:2] + swap(sums[2:], 1)).reshape(NODES, WIDTH)
    weight_other = swap(weight_lane, 1)
    mixed = ((feats.astype(F32) + neighbour_sum) / degree).astype(BF16)

    first = jnp.where(core == 0, weight_lane, weight_other)
    second = jnp.where(core == 0, weight_other, weight_lane)
    weight_t = jnp.stack([first, second], axis=2).reshape(NY, WIDTH, WIDTH)

    def hidden_part(dy):
        return lax.dot_general(mixed, weight_t[dy], (((1,), (1,)), ((), ())), preferred_element_type=F32)

    hidden = add(
        hidden_part(0),
        y_shift(hidden_part(1).astype(BF16), 1),
        y_shift(hidden_part(2).astype(BF16), 2),
        y_shift(hidden_part(3).astype(BF16), 3),
    ) + bias
    activated, slope = silu_parts(hidden)
    output = activated.astype(BF16)
    dz_full = cotangent.astype(F32) * slope
    dz_own = dz_full.astype(BF16)
    dz_parts = [dz_own] + [y_shift(dz_own, NY - dy) for dy in range(1, NY)]

    dmixed = sum(jnp.dot(dz_parts[dy], weight_t[dy], preferred_element_type=F32) for dy in range(NY))
    scaled = (dmixed / degree).astype(BF16)
    scaled_blocks = jnp.concatenate([scaled, swap(scaled, 1)], axis=0).reshape(4, BLK, WIDTH)

    weight_part = jnp.stack(
        [
            lax.dot_general(dz_parts[dy], mixed, (((0,), (0,)), ((), ())), preferred_element_type=F32)
            for dy in range(NY)
        ]
    ).reshape(NY, 2 * NX, 2, W_ROWS, WIDTH)
    mine = jnp.where(core == 0, weight_part[:, :, 0], weight_part[:, :, 1])
    others = jnp.where(core == 0, weight_part[:, :, 1], weight_part[:, :, 0])
    bias_part = jnp.sum(dz_full, axis=0, keepdims=True)
    sent = jnp.concatenate([others.reshape(-1, WIDTH), jnp.pad(bias_part, ((0, 7), (0, 0)))], axis=0)
    got = swap(sent, 1)
    weight_sums = (mine + got[:-8].reshape(mine.shape)).astype(BF16)

    chip_bias = bias_part + got[-8:-7]
    bias_rows = split(chip_bias)
    parts = [
        backward(call, lists, tile_values, other_tiles, scaled_blocks, weight_sums, bias_rows)
        for call in range(len(SCATTER))
    ]
    feats_grad, weight_sum, bias_sum = scatter(*parts, core, lists, chip_bias, scaled)
    from_core_0 = lax.ppermute(bias_sum, "dom", [(i, i + 1) for i in range(0, NZ * NX * 2, 2)])
    bias_grad = jnp.where(core == 0, bias_sum, from_core_0)

    return (output, feats_grad, weight_sum.T, bias_grad.reshape(WIDTH))


def solution(mesh):
    return jax.shard_map(
        on_device,
        mesh=mesh,
        in_specs=(
            P("dom", "feat"),
            P("feat", "dom"),
            P("feat"),
            P("dom", None, None),
            P("dom"),
            P("dom"),
            P("dom"),
            P("dom", "feat"),
        ),
        out_specs=(P("dom", "feat"), P("dom", "feat"), P("feat", "dom"), P("feat")),
        check_vma=False,
    )
```

```python
import functools

import jax
import jax.numpy as jnp
from jax import lax
from jax.experimental import pallas as pl
from jax.experimental.pallas import tpu as pltpu
from jax.sharding import PartitionSpec as P

F32 = jnp.float32
BF16 = jnp.bfloat16
NZ, NX, NY = 8, 4, 4
BLK = 128
SLOTS = 128
WIDTH = 256
NODES = 2 * BLK
W_ROWS = 16
ROWS = NODES + W_ROWS
UNROLL = 8
FETCH = 16
BIAS_ROWS = 16
SUM_ROWS = 4 * ROWS + BIAS_ROWS
MIB = 1 << 20
VMEM = 54 * MIB

LOW, HIGH, ACROSS = (0, 1, 7, 4), (3, 5, 2, 6), (0, 1, 3, 2)
HIGH_STEPS = (3, -3, 2, -2)
GATHER_0 = tuple(
    tuple(k * NZ + j for j in group)
    for k, group in ((0, LOW), (1, LOW), (3, LOW), (2, LOW), (3, HIGH), (1, HIGH), (2, HIGH), (0, HIGH))
)
GATHER_1 = tuple(tuple(k * NZ + j for k in ACROSS) for j in (0, 1, 7, 2, 6, 3, 5)) + (
    None,
    tuple(k * NZ + 4 for k in ACROSS[:2]),
    tuple(k * NZ + 4 for k in ACROSS[2:]),
)
FORWARD_CHUNKS = ((0, 1, 2, 3, 4, 7), (5, 6), (8, 9))
SCATTER = (
    (
        (None, tuple((dx, 4) for dx in ACROSS)),
        (tuple((2, dz) for dz in HIGH), None),
        (tuple((3, dz) for dz in HIGH), None),
    ),
    (
        (None, tuple((dx, 3) for dx in ACROSS)),
        (None, tuple((dx, 5) for dx in ACROSS)),
        (tuple((1, dz) for dz in HIGH), tuple((dx, 2) for dx in ACROSS)),
        (tuple((2, dz) for dz in LOW), tuple((dx, 6) for dx in ACROSS)),
        (tuple((1, dz) for dz in LOW), tuple((dx, 1) for dx in ACROSS)),
        (tuple((3, dz) for dz in LOW), tuple((dx, 7) for dx in ACROSS)),
        (tuple((0, dz) for dz in HIGH), None),
        (tuple((0, dz) for dz in LOW), tuple((dx, 0) for dx in ACROSS)),
    ),
)


def shift(value, core_0=None, core_1=None):
    pairs = []
    for z in range(NZ):
        for x in range(NX):
            for core, step in enumerate((core_0, core_1)):
                if step is not None:
                    target = ((z + step[0]) % NZ * NX + (x + step[1]) % NX) * 2 + core
                    pairs.append(((z * NX + x) * 2 + core, target))
    return lax.ppermute(value, "dom", pairs)


Z_UP, Z_DOWN, Z_FOUR = (1, 0), (-1, 0), (4, 0)
X_UP, X_DOWN, X_TWO = (0, 1), (0, -1), (0, 2)


def swap(value, bit):
    return lax.ppermute(value, "dom", [(i, i ^ bit) for i in range(NZ * NX * 2)])


def y_shift(value, dy):
    return lax.ppermute(value, "feat", [(y, (y + dy) % NY) for y in range(NY)])


def smem():
    return pl.BlockSpec(memory_space=pltpu.SMEM)


def vmem():
    return pl.BlockSpec(memory_space=pltpu.VMEM)


def anywhere():
    return pl.BlockSpec(memory_space=pl.ANY)


def list_kernel(place, own, sib, lists):
    core, x, z = place[0], place[1], place[2]
    wide = (1, 2 * SLOTS)
    column = jnp.concatenate([own[1:2], sib[1:2]], axis=1)
    row = jnp.concatenate([own[0:1], sib[0:1] + 2], axis=1)
    slot = lax.broadcasted_iota(jnp.int32, wide, 1)
    live = slot < jnp.where(slot < SLOTS, place[4], SLOTS + place[5])
    owner = column >> 1
    chip = owner >> 1
    k = (x - (chip & (NX - 1))) & (NX - 1)
    j = (z - (chip >> 2)) & (NZ - 1)
    spot = (k * NZ + j) * 2 + (column & 1)
    mine = live & ((owner & 1) == core)
    high = ((j >= 2) & (j <= 6)) & (j != 4)
    on_0 = jnp.where(high & ((k == 1) | (k == 2)), 1, 0)
    on_1 = jnp.where(j == 4, 2, jnp.where((j == 3) | (j == 5), 1, 0))
    forward_call = jnp.where(core == 0, on_0, on_1)
    backward_call = jnp.where(core == 0, jnp.where(high & ((k == 1) | (k == 2)), 0, 1), jnp.where(j == 4, 0, 1))
    square = (2 * SLOTS, 2 * SLOTS)
    first = lax.broadcasted_iota(jnp.int32, square, 0)
    second = lax.broadcasted_iota(jnp.int32, square, 1)
    up_to = jnp.where(first <= second, 1.0, 0.0).astype(BF16)
    group_of = lax.broadcasted_iota(jnp.int32, (16, 2 * SLOTS), 0)
    lane = lax.broadcasted_iota(jnp.int32, (16, 2 * SLOTS), 1)
    before = jnp.where(
        lax.broadcasted_iota(jnp.int32, (16, 16), 1) < lax.broadcasted_iota(jnp.int32, (16, 16), 0), 1.0, 0.0
    ).astype(BF16)
    values = jnp.concatenate([slot, spot], axis=0).astype(F32)
    values = jnp.concatenate([values, jnp.zeros((14, 2 * SLOTS), F32)], axis=0).astype(BF16)
    lists[...] = jnp.zeros_like(lists)
    for at, call in ((0, forward_call), (3, backward_call)):
        group = jnp.where(mine, call * 4 + row, -1)
        member = jnp.where(group_of == group, 1.0, 0.0)
        rank = jnp.dot(member.astype(BF16), up_to, preferred_element_type=F32)
        counts = jnp.sum(member, axis=1, keepdims=True)
        earlier = jnp.dot(before, member.astype(BF16), preferred_element_type=F32)
        starts = jnp.sum(earlier, axis=1, keepdims=True)
        goal = jnp.sum(member * (starts + rank), axis=0, keepdims=True).astype(jnp.int32) - 1
        moved = jnp.where(first == goal, 1.0, 0.0).astype(BF16)
        ordered = lax.dot_general(values, moved, (((1,), (1,)), ((), ())), preferred_element_type=F32)
        lists[at : at + 1, :] = jnp.sum(jnp.where(group_of == lane, counts, 0.0), axis=0, keepdims=True).astype(jnp.int32)
        lists[at + 1 : at + 2, :] = jnp.sum(jnp.where(group_of == lane, starts, 0.0), axis=0, keepdims=True).astype(jnp.int32)
        lists[at + 2 : at + 3, :] = (ordered[0:1] * 64.0 + ordered[1:2]).astype(jnp.int32)
    told = jnp.zeros(wide, jnp.int32)
    for i in range(6):
        told = jnp.where(slot == i, place[i], told)
    lists[6:7, :] = told


def make_lists(place, own, sib):
    return pl.pallas_call(
        list_kernel,
        out_shape=jax.ShapeDtypeStruct((8, 2 * SLOTS), jnp.int32),
        in_specs=[smem(), vmem(), vmem()],
        out_specs=vmem(),
    )(place, own, sib)


def place_of(lists):
    return [lists[6, i] for i in range(4)]


def copy_each(copies, action):
    for condition, copy in copies:
        call = getattr(copy, action)
        if condition is None:
            call()
        else:
            pl.when(condition)(call)


class Tiles:
    def __init__(self, lists, at, call, every, own, sib, held, sem):
        self.lists, self.at, self.call, self.every = lists, at, call, every
        self.own, self.sib, self.held, self.sem = own, sib, held, sem
        self.begin = lists[at + 1, call * 4]
        self.end = lists[at + 1, call * 4 + 3] + lists[at, call * 4 + 3]

    def bulk(self):
        copies = []
        for which, source in enumerate((self.own, self.sib)):
            for step in range(SLOTS // FETCH):
                first = step * FETCH
                copy = pltpu.make_async_copy(
                    source.at[pl.ds(first, FETCH)],
                    self.held.at[pl.ds(which * SLOTS + first, FETCH)],
                    self.sem.at[which * (SLOTS // FETCH) + step],
                )
                copies.append((first < self.lists[6, 4 + which], copy))
        return copies

    def each(self, action):
        def step(p, carry):
            slot = self.lists[self.at + 2, p] >> 6
            goal = self.held.at[p]

            @pl.when(slot < SLOTS)
            def _():
                getattr(pltpu.make_async_copy(self.own.at[jnp.minimum(slot, SLOTS - 1)], goal, self.sem.at[0]), action)()

            @pl.when(slot >= SLOTS)
            def _():
                getattr(pltpu.make_async_copy(self.sib.at[jnp.maximum(slot - SLOTS, 0)], goal, self.sem.at[0]), action)()

            return carry

        lax.fori_loop(self.begin, self.end, step, 0)

    def start(self):
        if self.every:
            copy_each(self.bulk(), "start")
        else:
            self.each("start")
        self.held[2 * SLOTS] = jnp.zeros((BLK, BLK), BF16)

    def wait(self):
        if self.every:
            copy_each(self.bulk(), "wait")
        else:
            self.each("wait")

    def rows(self):
        for row in range(4):
            group = self.call * 4 + row
            number, first = self.lists[self.at, group], self.lists[self.at + 1, group]

            def pick(it, number=number, first=first):
                lefts, spots = [], []
                for u in range(UNROLL):
                    p = it * UNROLL + u
                    entry = self.lists[self.at + 2, first + jnp.minimum(p, number - 1)]
                    place = entry >> 6 if self.every else first + p
                    lefts.append(self.held[jnp.where(p < number, place, 2 * SLOTS)])
                    spots.append(entry & 63)
                return jnp.concatenate(lefts, axis=1), spots

            yield row, lax.div(number + (UNROLL - 1), UNROLL), pick


def forward_kernel(call, lists, own, sib, *rest):
    chosen = FORWARD_CHUNKS[call]
    chunks, rest = rest[: len(chosen)], rest[len(chosen) :]
    if call:
        own_before, sib_before, weight_before, *rest = rest
    own_sums, sib_sums, weight_out, blocks, held, sem, tile_sem = rest
    core, x, z, y = place_of(lists)
    tiles = Tiles(lists, 0, call, call == 0, own, sib, held, tile_sem)
    tiles.start()
    copies, arrived = [], []
    for n, chunk in zip(chosen, chunks):
        condition = None if n < 7 else core == (0 if n == 7 else 1)
        for i in range(chunk.shape[0]):
            if n < 7:
                spot = jnp.where(core == 0, GATHER_0[n][i], GATHER_1[n][i])
            else:
                spot = GATHER_0[n][i] if n == 7 else GATHER_1[n][i]
            copies.append((condition, pltpu.make_async_copy(chunk.at[i], blocks.at[spot], sem.at[len(copies)])))
            arrived.append((condition, spot))
    copy_each(copies, "start")
    copy_each(copies, "wait")
    tiles.wait()
    for row, steps, pick in tiles.rows():

        def step(it, total):
            left, spots = pick(it)
            rights = []
            for spot in spots:
                first = pl.multiple_of((spot & 1) * BLK, BLK)
                rights.append(blocks[spot >> 1, pl.ds(first, BLK), :])
            return total + jnp.dot(left, jnp.concatenate(rights, axis=0), preferred_element_type=F32)

        sums, at = (own_sums, row) if row < 2 else (sib_sums, row - 2)
        before = jnp.zeros((BLK, WIDTH), F32)
        if call:
            before = own_before[at] if row < 2 else sib_before[at]
        sums[at] = lax.fori_loop(0, steps, step, before)
    if call:
        weight_out[...] = weight_before[...]
    for condition, spot in arrived:

        def keep(spot=spot):
            column = (x - (spot >> 3)) & (NX - 1)
            level = (z - spot) & (NZ - 1)
            part = ((level >> 1) - y) & (NY - 1)
            weight_out[part, (level & 1) * NX + column] = blocks[spot, NODES:ROWS, :]

        if condition is None:
            keep()
        else:
            pl.when(condition)(keep)


def forward(call, lists, own, sib, chunks, before):
    chosen = [chunks[n] for n in FORWARD_CHUNKS[call]]
    return pl.pallas_call(
        functools.partial(forward_kernel, call),
        out_shape=(
            jax.ShapeDtypeStruct((2, BLK, WIDTH), F32),
            jax.ShapeDtypeStruct((2, BLK, WIDTH), F32),
            jax.ShapeDtypeStruct((NY, 2 * NX, W_ROWS, WIDTH), BF16),
        ),
        in_specs=[smem()] + [anywhere()] * (2 + len(chosen)) + [vmem()] * len(before),
        out_specs=(vmem(),) * 3,
        scratch_shapes=[
            pltpu.VMEM((NX * NZ, ROWS, WIDTH), BF16),
            pltpu.VMEM((2 * SLOTS + 1, BLK, BLK), BF16),
            pltpu.SemaphoreType.DMA((32,)),
            pltpu.SemaphoreType.DMA((2 * SLOTS // FETCH,)),
        ],
        compiler_params=pltpu.CompilerParams(vmem_limit_bytes=VMEM),
        cost_estimate=pl.CostEstimate(
            flops=2 * BLK * BLK * WIDTH * len(chosen) * 16, bytes_accessed=len(chosen) * MIB, transcendentals=0
        ),
    )(lists, own, sib, *chosen, *before)


def backward_kernel(call, lists, own, sib, scaled, weight_sums, bias_rows, *rest):
    chunks = SCATTER[call]
    outs, rest = rest[: len(chunks)], rest[len(chunks) :]
    total, held, tile_sem = rest
    core, x, z, y = place_of(lists)
    tiles = Tiles(lists, 3, call, call == 1, own, sib, held, tile_sem)
    tiles.start()

    def each_chunk(action):
        for out, chunk in zip(outs, chunks):
            if None in chunk:
                side = 1 if chunk[0] is None else 0

                @pl.when(core == side)
                def _(out=out, places=chunk[side]):
                    action(out, places)
            else:
                action(out, [[jnp.where(core == 0, p, q) for p, q in zip(*pair)] for pair in zip(*chunk)])

    def spot_of(dx, dz):
        return ((0 - dx) & (NX - 1)) * NZ + ((0 - dz) & (NZ - 1))

    def clear(out, places):
        for dx, dz in places:
            spot = spot_of(dx, dz)
            total[spot * 2] = jnp.zeros((BLK, WIDTH), F32)
            total[spot * 2 + 1] = jnp.zeros((BLK, WIDTH), F32)

    def emit(out, places):
        for i, (dx, dz) in enumerate(places):
            spot = spot_of(dx, dz)
            first = i * ROWS
            out[first : first + BLK, :] = total[spot * 2].astype(BF16)
            out[first + BLK : first + NODES, :] = total[spot * 2 + 1].astype(BF16)
            column = (x + dx) & (NX - 1)
            level = (z + dz) & (NZ - 1)
            part = ((level >> 1) - y) & (NY - 1)
            out[first + NODES : first + ROWS, :] = weight_sums[part, (level & 1) * NX + column]
        out[4 * ROWS : SUM_ROWS, :] = bias_rows[...] if call == 0 else jnp.zeros((BIAS_ROWS, WIDTH), BF16)

    each_chunk(clear)
    tiles.wait()
    for row, steps, pick in tiles.rows():
        right = scaled[row]

        def step(it, carry):
            left, spots = pick(it)
            terms = lax.dot_general(left, right, (((0,), (0,)), ((), ())), preferred_element_type=F32)
            for u, spot in enumerate(spots):
                total[spot] += terms[u * BLK : (u + 1) * BLK]
            return carry

        lax.fori_loop(0, steps, step, 0)
    each_chunk(emit)


def backward(call, lists, own, sib, scaled, weight_sums, bias_rows):
    shapes = []
    for _ in SCATTER[call]:
        shapes.append(jax.ShapeDtypeStruct((SUM_ROWS, WIDTH), BF16))
    return pl.pallas_call(
        functools.partial(backward_kernel, call),
        out_shape=tuple(shapes),
        in_specs=[smem()] + [anywhere()] * 2 + [vmem()] * 3,
        out_specs=(vmem(),) * len(shapes),
        scratch_shapes=[
            pltpu.VMEM((2 * NX * NZ, BLK, WIDTH), F32),
            pltpu.VMEM((2 * SLOTS + 1, BLK, BLK), BF16),
            pltpu.SemaphoreType.DMA((2 * SLOTS // FETCH,)),
        ],
        compiler_params=pltpu.CompilerParams(vmem_limit_bytes=VMEM),
        cost_estimate=pl.CostEstimate(
            flops=2 * BLK * BLK * WIDTH * len(shapes) * 16, bytes_accessed=len(shapes) * MIB, transcendentals=0
        ),
    )(lists, own, sib, scaled, weight_sums, bias_rows)


def gather(block, core, lists, other_tiles, call):
    p1 = shift(block, Z_UP, X_UP)
    p2 = shift(block, Z_DOWN, X_DOWN)
    p3 = shift(block, Z_FOUR, X_TWO)
    far = [shift(block, (dz, 0)) for dz in HIGH_STEPS]
    low, high = jnp.stack([block, p1, p2, p3]), jnp.stack(far)
    low, high, other_tiles = lax.optimization_barrier((low, high, other_tiles))
    c1 = shift(low, X_UP, Z_UP)
    c2 = shift(low, X_DOWN, Z_DOWN)
    c1, c2 = lax.optimization_barrier((c1, c2))
    c3 = shift(c1, X_UP, Z_UP)
    c4 = shift(jnp.where(core == 0, high, c2), X_DOWN, Z_DOWN)
    c3, c4, lists = lax.optimization_barrier((c3, c4, lists))
    early = lists, other_tiles
    chunks = [low, c1, c2, c3, c4, None, None, high]
    sums = call(0, early, chunks, ())
    c5 = shift(jnp.where(core == 0, high, c3), X_UP, Z_UP)
    c6 = shift(c4, X_DOWN, Z_DOWN)
    c5, c6, sums = lax.optimization_barrier((c5, c6, sums))
    chunks[5:7] = c5, c6
    chunks += [shift(c5[:2], None, Z_UP), shift(c6[2:], None, Z_DOWN)]
    return call(2, early, chunks, call(1, early, chunks, sums))


def add(*values):
    total = values[0].astype(F32)
    for value in values[1:]:
        total = total + value.astype(F32)
    return total


def split(value):
    high = lax.reduce_precision(value, 8, 7)
    middle = lax.reduce_precision(value - high, 8, 7)
    rows = jnp.concatenate([high, middle, value - high - middle], axis=0)
    return jnp.pad(rows, ((0, BIAS_ROWS - 3), (0, 0))).astype(BF16)


def rows_of(value):
    high = value.astype(BF16)
    middle = (value - high.astype(F32)).astype(BF16)
    low = (value - high.astype(F32) - middle.astype(F32)).astype(BF16)
    return [high.astype(F32), middle.astype(F32), low.astype(F32)]


def bias_block(rows):
    used = sum(row.shape[0] for row in rows)
    rows = rows + [jnp.zeros((BIAS_ROWS - used, WIDTH), F32)]
    return jnp.concatenate(rows, axis=0).astype(BF16)


def joined(block, first=0):
    rows = block.astype(F32)
    return rows[first : first + 1] + rows[first + 1 : first + 2] + rows[first + 2 : first + 3]


def in_order(values, place, held):
    count = len(values)
    for k, value in enumerate(values):
        held[k : k + 1, :] = value
    total = held[pl.ds(place & (count - 1), 1), :]
    for i in range(1, count):
        total = total + held[pl.ds((place - i) & (count - 1), 1), :]
    return total


def block_sum(i, *chunks):
    total = chunks[0][i * ROWS : (i + 1) * ROWS, :].astype(F32)
    for chunk in chunks[1:]:
        total = total + chunk[i * ROWS : (i + 1) * ROWS, :].astype(F32)
    return total


def tail_of(chunk):
    return chunk[4 * ROWS : SUM_ROWS, :]


def high_kernel(lists, chip_bias, h0, ja1, ja2, jb1, *rest):
    messages, (line_bias, held) = rest[:4], rest[4:]
    line = in_order([chip_bias[...], joined(tail_of(ja1)), joined(tail_of(jb1)), joined(tail_of(ja2))], lists[6, 1], held)
    line_bias[...] = line
    rows = bias_block(rows_of(line))
    for i, message in enumerate(messages):
        message[0:ROWS, :] = block_sum(i, h0, jb1, ja2).astype(BF16)
        message[ROWS:, :] = rows


def low_kernel(line_bias, h1, jc1, jc2, m1, m2, m3, rest):
    rows = bias_block(rows_of(line_bias[...]))
    rest[...] = block_sum(0, h1, jc1, jc2)
    for i, message in enumerate((m1, m2, m3)):
        message[0:ROWS, :] = block_sum(i + 1, h1, jc1, jc2).astype(BF16)
        message[ROWS:, :] = rows


def last_kernel(lists, line_bias, rest, scaled, *more):
    arrived, (feats_grad, weight_grad, bias, held) = more[:7], more[7:]
    total = rest[...] + block_sum(0, *arrived)
    feats_grad[...] = (scaled[...].astype(F32) + total[0:NODES]).astype(BF16)
    weight_grad[...] = total[NODES:ROWS]
    values = {0: line_bias[...]}
    for dz, message in zip(LOW[1:] + HIGH, arrived):
        values[dz] = joined(message[ROWS:, :])
    bias[...] = in_order([values[dz] for dz in range(NZ)], lists[6, 2], held)


def small_call(kernel, shapes, lists, operands, scratch):
    first = [] if lists is None else [lists]
    return pl.pallas_call(
        kernel,
        out_shape=tuple(jax.ShapeDtypeStruct(shape, dtype) for shape, dtype in shapes),
        in_specs=[smem()] * len(first) + [vmem()] * len(operands),
        out_specs=(vmem(),) * len(shapes),
        scratch_shapes=[pltpu.VMEM((8, WIDTH), F32)] * scratch,
        compiler_params=pltpu.CompilerParams(vmem_limit_bytes=16 * MIB),
    )(*first, *operands)


def scatter(first, second, core, lists, chip_bias, scaled):
    first_up, x1, x2 = first
    y1, y2, b1, b2, q1, q2, h0, h1 = second
    zero = jnp.zeros((), BF16)
    j0 = shift(first_up, None, Z_UP)
    ja1 = shift(jnp.where(core == 0, x1, add(y1, j0).astype(BF16)), X_UP, Z_UP)
    ja2 = shift(jnp.where(core == 0, x2, y2), X_DOWN, Z_DOWN)
    ja1, ja2 = lax.optimization_barrier((ja1, ja2))
    jb1 = shift(add(b1, ja1).astype(BF16), X_UP, Z_UP)
    jb2 = shift(add(b2, jnp.where(core == 0, zero, ja2)).astype(BF16), X_DOWN, Z_DOWN)
    jb1, jb2 = lax.optimization_barrier((jb1, jb2))
    size = (ROWS + BIAS_ROWS, WIDTH)
    *high, line_bias = small_call(
        high_kernel, [(size, BF16)] * 4 + [((1, WIDTH), F32)], lists, (chip_bias, h0, ja1, ja2, jb1), 1
    )
    jc1 = shift(add(q1, jnp.where(core == 0, zero, jb1)).astype(BF16), X_UP, Z_UP)
    jc2 = shift(add(q2, jb2).astype(BF16), X_DOWN, Z_DOWN)
    jc1, jc2, *high = lax.optimization_barrier((jc1, jc2, *high))
    *low, rest = small_call(
        low_kernel, [(size, BF16)] * 3 + [((ROWS, WIDTH), F32)], None, (line_bias, h1, jc1, jc2), 0
    )
    arrived = [shift(low[0], Z_UP, X_UP), shift(low[1], Z_DOWN, X_DOWN), shift(low[2], Z_FOUR, X_TWO)]
    arrived += [shift(message, (dz, 0)) for dz, message in zip(HIGH_STEPS, high)]
    return small_call(
        last_kernel,
        (((NODES, WIDTH), BF16), ((W_ROWS, WIDTH), F32), ((1, WIDTH), F32)),
        lists,
        (line_bias, rest, scaled, *arrived),
        1,
    )


def nothing(value):
    return jnp.minimum(jnp.abs(value.astype(F32)), 0.0).astype(BF16)


def silu_parts(hidden):
    gate_value = jax.nn.sigmoid(hidden)
    return (hidden * gate_value, gate_value * (1.0 + hidden * (1.0 - gate_value)))


def on_device(feats, weight, bias, tile_values, tile_rows, tile_cols, tile_live, cotangent):
    dom = lax.axis_index("dom")
    y = lax.axis_index("feat")
    core = dom % 2
    x = (dom // 2) % NX
    z = dom // (2 * NX)

    meta = jnp.stack([tile_rows, tile_cols, jnp.broadcast_to(tile_live, (SLOTS,))])
    other_meta = swap(meta, 1)
    place = jnp.stack([core, x, z, y, tile_live[0], other_meta[2, 0]]).astype(jnp.int32)
    lists = make_lists(place, meta, other_meta)

    own_live = jnp.arange(SLOTS, dtype=jnp.int32) < tile_live[0]
    row_sums = jnp.sum(tile_values, axis=2, dtype=F32)
    degree = 1.0 + jnp.concatenate(
        [
            jnp.sum(jnp.where((own_live & (tile_rows == row))[:, None], row_sums, 0.0), axis=0)
            for row in range(2)
        ]
    ).reshape(NODES, 1)

    other_tiles = swap(tile_values, 1)
    sums, other_sums, weight_lane = gather(
        jnp.concatenate([feats, weight.T], axis=0),
        core,
        lists,
        other_tiles,
        lambda call, early, chunks, before: forward(call, early[0], tile_values, early[1], chunks, before),
    )
    neighbour_sum = (sums + swap(other_sums, 1)).reshape(NODES, WIDTH)
    weight_other = swap(weight_lane, 1)
    mixed = ((feats.astype(F32) + neighbour_sum) / degree).astype(BF16)

    first = jnp.where(core == 0, weight_lane, weight_other)
    second = jnp.where(core == 0, weight_other, weight_lane)
    weight_t = jnp.stack([first, second], axis=2).reshape(NY, WIDTH, WIDTH)

    def hidden_part(dy):
        return lax.dot_general(mixed, weight_t[dy], (((1,), (1,)), ((), ())), preferred_element_type=F32)

    hidden = add(
        hidden_part(0),
        y_shift(hidden_part(1).astype(BF16), 1),
        y_shift(hidden_part(2).astype(BF16), 2),
        y_shift(hidden_part(3).astype(BF16), 3),
    ) + bias
    activated, slope = silu_parts(hidden)
    output = activated.astype(BF16)
    dz_full = cotangent.astype(F32) * slope
    dz_own = dz_full.astype(BF16)
    dz_parts = [dz_own] + [y_shift(dz_own, NY - dy) for dy in range(1, NY)]

    dmixed = sum(jnp.dot(dz_parts[dy], weight_t[dy], preferred_element_type=F32) for dy in range(NY))
    scaled = (dmixed / degree).astype(BF16)
    scaled_blocks = jnp.concatenate([scaled, swap(scaled, 1)], axis=0).reshape(4, BLK, WIDTH)

    weight_part = jnp.stack(
        [
            lax.dot_general(dz_parts[dy], mixed, (((0,), (0,)), ((), ())), preferred_element_type=F32)
            for dy in range(NY)
        ]
    ).reshape(NY, 2 * NX, 2, W_ROWS, WIDTH)
    mine = jnp.where(core == 0, weight_part[:, :, 0], weight_part[:, :, 1])
    others = jnp.where(core == 0, weight_part[:, :, 1], weight_part[:, :, 0])
    bias_part = jnp.sum(dz_full, axis=0, keepdims=True)
    sent = jnp.concatenate([others.reshape(-1, WIDTH), jnp.pad(bias_part, ((0, 7), (0, 0)))], axis=0)
    got = swap(sent, 1)
    weight_sums = (mine + got[:-8].reshape(mine.shape)).astype(BF16)

    chip_bias = bias_part + got[-8:-7]
    bias_rows = split(chip_bias)
    parts = [
        backward(call, lists, tile_values, other_tiles, scaled_blocks, weight_sums, bias_rows)
        for call in range(len(SCATTER))
    ]
    feats_grad, weight_sum, bias_sum = scatter(*parts, core, lists, chip_bias, scaled)
    from_core_0 = lax.ppermute(bias_sum, "dom", [(i, i + 1) for i in range(0, NZ * NX * 2, 2)])
    bias_grad = jnp.where(core == 0, bias_sum, from_core_0)

    return (output, feats_grad, weight_sum.T, bias_grad.reshape(WIDTH))


def solution(mesh):
    return jax.shard_map(
        on_device,
        mesh=mesh,
        in_specs=(
            P("dom", "feat"),
            P("feat", "dom"),
            P("feat"),
            P("dom", None, None),
            P("dom"),
            P("dom"),
            P("dom"),
            P("dom", "feat"),
        ),
        out_specs=(P("dom", "feat"), P("dom", "feat"), P("feat", "dom"), P("feat")),
        check_vma=False,
    )
```

```python
import functools

import jax
import jax.numpy as jnp
from jax import lax
from jax.experimental import pallas as pl
from jax.experimental.pallas import tpu as pltpu
from jax.sharding import PartitionSpec as P

F32 = jnp.float32
BF16 = jnp.bfloat16
NZ, NX, NY = 8, 4, 4
BLK = 128
SLOTS = 128
WIDTH = 256
NODES = 2 * BLK
W_ROWS = 16
ROWS = NODES + W_ROWS
UNROLL = 8
FETCH = 16
BIAS_ROWS = 16
SUM_ROWS = 4 * ROWS + BIAS_ROWS
MIB = 1 << 20
VMEM = 54 * MIB

LOW, HIGH, ACROSS = (0, 1, 7, 2), (3, 4, 6, 5), (0, 1, 3, 2)
GATHER_0 = tuple(
    tuple(k * NZ + j for j in group)
    for k, group in ((0, LOW), (1, LOW), (3, LOW), (2, LOW), (3, HIGH), (1, HIGH), (2, HIGH), (0, HIGH))
)
GATHER_1 = tuple(tuple(k * NZ + j for k in ACROSS) for j in (0, 1, 7, 2, 6, 3, 5)) + (
    None,
    tuple(k * NZ + 4 for k in ACROSS[:2]),
    tuple(k * NZ + 4 for k in ACROSS[2:]),
)
FORWARD_CHUNKS = ((0, 1, 2, 3, 4, 7), (5, 6), (8, 9))
SCATTER = (
    (
        (None, tuple((dx, 4) for dx in ACROSS)),
        (tuple((2, dz) for dz in HIGH), None),
        (tuple((3, dz) for dz in HIGH), None),
    ),
    (
        (None, tuple((dx, 3) for dx in ACROSS)),
        (None, tuple((dx, 5) for dx in ACROSS)),
        (tuple((1, dz) for dz in HIGH), tuple((dx, 2) for dx in ACROSS)),
        (tuple((2, dz) for dz in LOW), tuple((dx, 6) for dx in ACROSS)),
        (tuple((1, dz) for dz in LOW), tuple((dx, 1) for dx in ACROSS)),
        (tuple((3, dz) for dz in LOW), tuple((dx, 7) for dx in ACROSS)),
        (tuple((0, dz) for dz in HIGH), None),
        (tuple((0, dz) for dz in LOW), tuple((dx, 0) for dx in ACROSS)),
    ),
)


def shift(value, core_0=None, core_1=None):
    pairs = []
    for z in range(NZ):
        for x in range(NX):
            for core, step in enumerate((core_0, core_1)):
                if step is not None:
                    target = ((z + step[0]) % NZ * NX + (x + step[1]) % NX) * 2 + core
                    pairs.append(((z * NX + x) * 2 + core, target))
    return lax.ppermute(value, "dom", pairs)


Z_UP, Z_DOWN, Z_UP_2, Z_DOWN_2 = (1, 0), (-1, 0), (2, 0), (-2, 0)
X_UP, X_DOWN, X_TWO = (0, 1), (0, -1), (0, 2)


def swap(value, bit):
    return lax.ppermute(value, "dom", [(i, i ^ bit) for i in range(NZ * NX * 2)])


def y_shift(value, dy):
    return lax.ppermute(value, "feat", [(y, (y + dy) % NY) for y in range(NY)])


def smem():
    return pl.BlockSpec(memory_space=pltpu.SMEM)


def vmem():
    return pl.BlockSpec(memory_space=pltpu.VMEM)


def anywhere():
    return pl.BlockSpec(memory_space=pl.ANY)


def list_kernel(place, own, sib, lists):
    core, x, z = place[0], place[1], place[2]
    wide = (1, 2 * SLOTS)
    column = jnp.concatenate([own[1:2], sib[1:2]], axis=1)
    row = jnp.concatenate([own[0:1], sib[0:1] + 2], axis=1)
    slot = lax.broadcasted_iota(jnp.int32, wide, 1)
    live = slot < jnp.where(slot < SLOTS, place[4], SLOTS + place[5])
    owner = column >> 1
    chip = owner >> 1
    k = (x - (chip & (NX - 1))) & (NX - 1)
    j = (z - (chip >> 2)) & (NZ - 1)
    spot = (k * NZ + j) * 2 + (column & 1)
    mine = live & ((owner & 1) == core)
    high, back = (j >= 3) & (j <= 6), (j >= 2) & (j <= 5)
    on_0 = jnp.where(high & ((k == 1) | (k == 2)), 1, 0)
    on_1 = jnp.where(j == 4, 2, jnp.where((j == 3) | (j == 5), 1, 0))
    forward_call = jnp.where(core == 0, on_0, on_1)
    backward_call = jnp.where(core == 0, jnp.where(back & ((k == 1) | (k == 2)), 0, 1), jnp.where(j == 4, 0, 1))
    square = (2 * SLOTS, 2 * SLOTS)
    first = lax.broadcasted_iota(jnp.int32, square, 0)
    second = lax.broadcasted_iota(jnp.int32, square, 1)
    up_to = jnp.where(first <= second, 1.0, 0.0).astype(BF16)
    group_of = lax.broadcasted_iota(jnp.int32, (16, 2 * SLOTS), 0)
    lane = lax.broadcasted_iota(jnp.int32, (16, 2 * SLOTS), 1)
    before = jnp.where(
        lax.broadcasted_iota(jnp.int32, (16, 16), 1) < lax.broadcasted_iota(jnp.int32, (16, 16), 0), 1.0, 0.0
    ).astype(BF16)
    values = jnp.concatenate([slot, spot], axis=0).astype(F32)
    values = jnp.concatenate([values, jnp.zeros((14, 2 * SLOTS), F32)], axis=0).astype(BF16)
    lists[...] = jnp.zeros_like(lists)
    for at, call in ((0, forward_call), (3, backward_call)):
        group = jnp.where(mine, call * 4 + row, -1)
        member = jnp.where(group_of == group, 1.0, 0.0)
        rank = jnp.dot(member.astype(BF16), up_to, preferred_element_type=F32)
        counts = jnp.sum(member, axis=1, keepdims=True)
        earlier = jnp.dot(before, member.astype(BF16), preferred_element_type=F32)
        starts = jnp.sum(earlier, axis=1, keepdims=True)
        goal = jnp.sum(member * (starts + rank), axis=0, keepdims=True).astype(jnp.int32) - 1
        moved = jnp.where(first == goal, 1.0, 0.0).astype(BF16)
        ordered = lax.dot_general(values, moved, (((1,), (1,)), ((), ())), preferred_element_type=F32)
        lists[at : at + 1, :] = jnp.sum(jnp.where(group_of == lane, counts, 0.0), axis=0, keepdims=True).astype(jnp.int32)
        lists[at + 1 : at + 2, :] = jnp.sum(jnp.where(group_of == lane, starts, 0.0), axis=0, keepdims=True).astype(jnp.int32)
        lists[at + 2 : at + 3, :] = (ordered[0:1] * 64.0 + ordered[1:2]).astype(jnp.int32)
    told = jnp.zeros(wide, jnp.int32)
    for i in range(6):
        told = jnp.where(slot == i, place[i], told)
    lists[6:7, :] = told


def make_lists(place, own, sib):
    return pl.pallas_call(
        list_kernel,
        out_shape=jax.ShapeDtypeStruct((8, 2 * SLOTS), jnp.int32),
        in_specs=[smem(), vmem(), vmem()],
        out_specs=vmem(),
    )(place, own, sib)


def place_of(lists):
    return [lists[6, i] for i in range(4)]


def copy_each(copies, action):
    for condition, copy in copies:
        call = getattr(copy, action)
        if condition is None:
            call()
        else:
            pl.when(condition)(call)


class Tiles:
    def __init__(self, lists, at, call, every, own, sib, held, sem):
        self.lists, self.at, self.call, self.every = lists, at, call, every
        self.own, self.sib, self.held, self.sem = own, sib, held, sem
        self.begin = lists[at + 1, call * 4]
        self.end = lists[at + 1, call * 4 + 3] + lists[at, call * 4 + 3]

    def bulk(self):
        copies = []
        for which, source in enumerate((self.own, self.sib)):
            for step in range(SLOTS // FETCH):
                first = step * FETCH
                copy = pltpu.make_async_copy(
                    source.at[pl.ds(first, FETCH)],
                    self.held.at[pl.ds(which * SLOTS + first, FETCH)],
                    self.sem.at[which * (SLOTS // FETCH) + step],
                )
                copies.append((first < self.lists[6, 4 + which], copy))
        return copies

    def each(self, action):
        def step(p, carry):
            slot = self.lists[self.at + 2, p] >> 6
            goal = self.held.at[p]

            @pl.when(slot < SLOTS)
            def _():
                getattr(pltpu.make_async_copy(self.own.at[jnp.minimum(slot, SLOTS - 1)], goal, self.sem.at[0]), action)()

            @pl.when(slot >= SLOTS)
            def _():
                getattr(pltpu.make_async_copy(self.sib.at[jnp.maximum(slot - SLOTS, 0)], goal, self.sem.at[0]), action)()

            return carry

        lax.fori_loop(self.begin, self.end, step, 0)

    def start(self):
        if self.every:
            copy_each(self.bulk(), "start")
        else:
            self.each("start")
        self.held[2 * SLOTS] = jnp.zeros((BLK, BLK), BF16)

    def wait(self):
        if self.every:
            copy_each(self.bulk(), "wait")
        else:
            self.each("wait")

    def rows(self):
        for row in range(4):
            group = self.call * 4 + row
            number, first = self.lists[self.at, group], self.lists[self.at + 1, group]

            def pick(it, number=number, first=first):
                lefts, spots = [], []
                for u in range(UNROLL):
                    p = it * UNROLL + u
                    entry = self.lists[self.at + 2, first + jnp.minimum(p, number - 1)]
                    place = entry >> 6 if self.every else first + p
                    lefts.append(self.held[jnp.where(p < number, place, 2 * SLOTS)])
                    spots.append(entry & 63)
                return jnp.concatenate(lefts, axis=1), spots

            yield row, lax.div(number + (UNROLL - 1), UNROLL), pick


def forward_kernel(call, lists, own, sib, *rest):
    chosen = FORWARD_CHUNKS[call]
    chunks, rest = rest[: len(chosen)], rest[len(chosen) :]
    if call:
        own_before, sib_before, weight_before, *rest = rest
    own_sums, sib_sums, weight_out, blocks, held, sem, tile_sem = rest
    core, x, z, y = place_of(lists)
    tiles = Tiles(lists, 0, call, call == 0, own, sib, held, tile_sem)
    tiles.start()
    copies, arrived = [], []
    for n, chunk in zip(chosen, chunks):
        condition = None if n < 7 else core == (0 if n == 7 else 1)
        for i in range(chunk.shape[0]):
            if n < 7:
                spot = jnp.where(core == 0, GATHER_0[n][i], GATHER_1[n][i])
            else:
                spot = GATHER_0[n][i] if n == 7 else GATHER_1[n][i]
            copies.append((condition, pltpu.make_async_copy(chunk.at[i], blocks.at[spot], sem.at[len(copies)])))
            arrived.append((condition, spot))
    copy_each(copies, "start")
    copy_each(copies, "wait")
    tiles.wait()
    for row, steps, pick in tiles.rows():

        def step(it, total):
            left, spots = pick(it)
            rights = []
            for spot in spots:
                first = pl.multiple_of((spot & 1) * BLK, BLK)
                rights.append(blocks[spot >> 1, pl.ds(first, BLK), :])
            return total + jnp.dot(left, jnp.concatenate(rights, axis=0), preferred_element_type=F32)

        sums, at = (own_sums, row) if row < 2 else (sib_sums, row - 2)
        before = jnp.zeros((BLK, WIDTH), F32)
        if call:
            before = own_before[at] if row < 2 else sib_before[at]
        sums[at] = lax.fori_loop(0, steps, step, before)
    if call:
        weight_out[...] = weight_before[...]
    for condition, spot in arrived:

        def keep(spot=spot):
            column = (x - (spot >> 3)) & (NX - 1)
            level = (z - spot) & (NZ - 1)
            part = ((level >> 1) - y) & (NY - 1)
            weight_out[part, (level & 1) * NX + column] = blocks[spot, NODES:ROWS, :]

        if condition is None:
            keep()
        else:
            pl.when(condition)(keep)


def forward(call, lists, own, sib, chunks, before):
    chosen = [chunks[n] for n in FORWARD_CHUNKS[call]]
    return pl.pallas_call(
        functools.partial(forward_kernel, call),
        out_shape=(
            jax.ShapeDtypeStruct((2, BLK, WIDTH), F32),
            jax.ShapeDtypeStruct((2, BLK, WIDTH), F32),
            jax.ShapeDtypeStruct((NY, 2 * NX, W_ROWS, WIDTH), BF16),
        ),
        in_specs=[smem()] + [anywhere()] * (2 + len(chosen)) + [vmem()] * len(before),
        out_specs=(vmem(),) * 3,
        scratch_shapes=[
            pltpu.VMEM((NX * NZ, ROWS, WIDTH), BF16),
            pltpu.VMEM((2 * SLOTS + 1, BLK, BLK), BF16),
            pltpu.SemaphoreType.DMA((32,)),
            pltpu.SemaphoreType.DMA((2 * SLOTS // FETCH,)),
        ],
        compiler_params=pltpu.CompilerParams(vmem_limit_bytes=VMEM),
        cost_estimate=pl.CostEstimate(
            flops=2 * BLK * BLK * WIDTH * len(chosen) * 16, bytes_accessed=len(chosen) * MIB, transcendentals=0
        ),
    )(lists, own, sib, *chosen, *before)


def backward_kernel(call, lists, own, sib, scaled, weight_sums, bias_rows, *rest):
    chunks = SCATTER[call]
    outs, rest = rest[: len(chunks)], rest[len(chunks) :]
    total, held, tile_sem = rest
    core, x, z, y = place_of(lists)
    tiles = Tiles(lists, 3, call, call == 1, own, sib, held, tile_sem)
    tiles.start()

    def each_chunk(action):
        for out, chunk in zip(outs, chunks):
            if None in chunk:
                side = 1 if chunk[0] is None else 0

                @pl.when(core == side)
                def _(out=out, places=chunk[side]):
                    action(out, places)
            else:
                action(out, [[jnp.where(core == 0, p, q) for p, q in zip(*pair)] for pair in zip(*chunk)])

    def spot_of(dx, dz):
        return ((0 - dx) & (NX - 1)) * NZ + ((0 - dz) & (NZ - 1))

    def clear(out, places):
        for dx, dz in places:
            spot = spot_of(dx, dz)
            total[spot * 2] = jnp.zeros((BLK, WIDTH), F32)
            total[spot * 2 + 1] = jnp.zeros((BLK, WIDTH), F32)

    def emit(out, places):
        for i, (dx, dz) in enumerate(places):
            spot = spot_of(dx, dz)
            first = i * ROWS
            out[first : first + BLK, :] = total[spot * 2].astype(BF16)
            out[first + BLK : first + NODES, :] = total[spot * 2 + 1].astype(BF16)
            column = (x + dx) & (NX - 1)
            level = (z + dz) & (NZ - 1)
            part = ((level >> 1) - y) & (NY - 1)
            out[first + NODES : first + ROWS, :] = weight_sums[part, (level & 1) * NX + column]
        out[4 * ROWS : SUM_ROWS, :] = bias_rows[...] if call == 0 else jnp.zeros((BIAS_ROWS, WIDTH), BF16)

    each_chunk(clear)
    tiles.wait()
    for row, steps, pick in tiles.rows():
        right = scaled[row]

        def step(it, carry):
            left, spots = pick(it)
            terms = lax.dot_general(left, right, (((0,), (0,)), ((), ())), preferred_element_type=F32)
            for u, spot in enumerate(spots):
                total[spot] += terms[u * BLK : (u + 1) * BLK]
            return carry

        lax.fori_loop(0, steps, step, 0)
    each_chunk(emit)


def backward(call, lists, own, sib, scaled, weight_sums, bias_rows):
    shapes = []
    for _ in SCATTER[call]:
        shapes.append(jax.ShapeDtypeStruct((SUM_ROWS, WIDTH), BF16))
    return pl.pallas_call(
        functools.partial(backward_kernel, call),
        out_shape=tuple(shapes),
        in_specs=[smem()] + [anywhere()] * 2 + [vmem()] * 3,
        out_specs=(vmem(),) * len(shapes),
        scratch_shapes=[
            pltpu.VMEM((2 * NX * NZ, BLK, WIDTH), F32),
            pltpu.VMEM((2 * SLOTS + 1, BLK, BLK), BF16),
            pltpu.SemaphoreType.DMA((2 * SLOTS // FETCH,)),
        ],
        compiler_params=pltpu.CompilerParams(vmem_limit_bytes=VMEM),
        cost_estimate=pl.CostEstimate(
            flops=2 * BLK * BLK * WIDTH * len(shapes) * 16, bytes_accessed=len(shapes) * MIB, transcendentals=0
        ),
    )(lists, own, sib, scaled, weight_sums, bias_rows)


def gather(block, core, lists, other_tiles, call):
    p1 = shift(block, Z_UP, X_UP)
    p2 = shift(block, Z_DOWN, X_DOWN)
    p3 = shift(block, Z_UP_2, X_TWO)
    low, other_tiles = lax.optimization_barrier((jnp.stack([block, p1, p2, p3]), other_tiles))
    c1 = shift(low, X_UP, Z_UP)
    c2 = shift(low, X_DOWN, Z_DOWN)
    pa = shift(jnp.stack([low[1], low[3]]), Z_UP_2)
    pb = shift(jnp.stack([low[0], low[2]]), Z_DOWN_2)
    c1, c2, pa, pb = lax.optimization_barrier((c1, c2, pa, pb))
    high = jnp.concatenate([pa, pb], axis=0)
    c3 = shift(c1, X_UP, Z_UP)
    c4 = shift(jnp.where(core == 0, high, c2), X_DOWN, Z_DOWN)
    c3, c4, lists = lax.optimization_barrier((c3, c4, lists))
    early = lists, other_tiles
    chunks = [low, c1, c2, c3, c4, None, None, high]
    sums = call(0, early, chunks, ())
    c5 = shift(jnp.where(core == 0, high, c3), X_UP, Z_UP)
    c6 = shift(c4, X_DOWN, Z_DOWN)
    c5, c6, sums = lax.optimization_barrier((c5, c6, sums))
    chunks[5:7] = c5, c6
    chunks += [shift(c5[:2], None, Z_UP), shift(c6[2:], None, Z_DOWN)]
    return call(2, early, chunks, call(1, early, chunks, sums))


def add(*values):
    total = values[0].astype(F32)
    for value in values[1:]:
        total = total + value.astype(F32)
    return total


def split(value):
    high = lax.reduce_precision(value, 8, 7)
    middle = lax.reduce_precision(value - high, 8, 7)
    rows = jnp.concatenate([high, middle, value - high - middle], axis=0)
    return jnp.pad(rows, ((0, BIAS_ROWS - 3), (0, 0))).astype(BF16)


def rows_of(value):
    high = value.astype(BF16)
    middle = (value - high.astype(F32)).astype(BF16)
    low = (value - high.astype(F32) - middle.astype(F32)).astype(BF16)
    return [high.astype(F32), middle.astype(F32), low.astype(F32)]


def bias_block(rows):
    used = sum(row.shape[0] for row in rows)
    rows = rows + [jnp.zeros((BIAS_ROWS - used, WIDTH), F32)]
    return jnp.concatenate(rows, axis=0).astype(BF16)


def joined(block, first=0):
    rows = block.astype(F32)
    return rows[first : first + 1] + rows[first + 1 : first + 2] + rows[first + 2 : first + 3]


def in_order(values, place, held):
    count = len(values)
    for k, value in enumerate(values):
        held[k : k + 1, :] = value
    total = held[pl.ds(place & (count - 1), 1), :]
    for i in range(1, count):
        total = total + held[pl.ds((place - i) & (count - 1), 1), :]
    return total


def block_sum(i, *chunks):
    total = chunks[0][i * ROWS : (i + 1) * ROWS, :].astype(F32)
    for chunk in chunks[1:]:
        total = total + chunk[i * ROWS : (i + 1) * ROWS, :].astype(F32)
    return total


def tail_of(chunk):
    return chunk[4 * ROWS : SUM_ROWS, :]


def pair_kernel(lists, chip_bias, h0, ja1, ja2, jb1, pair_a, pair_b, line_bias, held):
    line = in_order([chip_bias[...], joined(tail_of(ja1)), joined(tail_of(jb1)), joined(tail_of(ja2))], lists[6, 1], held)
    line_bias[...] = line
    rows = bias_block(rows_of(line))
    for pair, first in ((pair_a, 0), (pair_b, 2)):
        for i in range(2):
            pair[i * ROWS : (i + 1) * ROWS, :] = block_sum(first + i, h0, jb1, ja2).astype(BF16)
        pair[2 * ROWS : 2 * ROWS + BIAS_ROWS, :] = rows


def message_kernel(line_bias, h1, jc1, jc2, ra, rb, m1, m2, m3, rest):
    own = rows_of(line_bias[...])
    rest[...] = block_sum(0, h1, jc1, jc2) + block_sum(0, rb)
    relayed = [chunk[2 * ROWS : 2 * ROWS + BIAS_ROWS, :].astype(F32)[0:3] for chunk in (ra, rb)]
    m1[0:ROWS, :] = (block_sum(1, h1, jc1, jc2) + block_sum(0, ra)).astype(BF16)
    m1[ROWS:, :] = bias_block(own + [relayed[0]])
    m2[0:ROWS, :] = (block_sum(2, h1, jc1, jc2) + block_sum(1, rb)).astype(BF16)
    m2[ROWS:, :] = bias_block(own + [relayed[1]])
    m3[0:ROWS, :] = (block_sum(3, h1, jc1, jc2) + block_sum(1, ra)).astype(BF16)
    m3[ROWS:, :] = bias_block(own + [relayed[0]])


def last_kernel(lists, line_bias, rest, r1, r2, r3, rb, scaled, feats_grad, weight_grad, bias, held):
    total = rest[...] + block_sum(0, r1, r2, r3)
    feats_grad[...] = (scaled[...].astype(F32) + total[0:NODES]).astype(BF16)
    weight_grad[...] = total[NODES:ROWS]
    t1, t2, t3 = (chunk[ROWS:, :] for chunk in (r1, r2, r3))
    tb = rb[2 * ROWS :, :]
    values = [line_bias[...], joined(t1), joined(t3), joined(t1, 3), joined(t3, 3), joined(t2, 3), joined(tb), joined(t2)]
    bias[...] = in_order(values, lists[6, 2], held)


def small_call(kernel, shapes, lists, operands, scratch):
    first = [] if lists is None else [lists]
    return pl.pallas_call(
        kernel,
        out_shape=tuple(jax.ShapeDtypeStruct(shape, dtype) for shape, dtype in shapes),
        in_specs=[smem()] * len(first) + [vmem()] * len(operands),
        out_specs=(vmem(),) * len(shapes),
        scratch_shapes=[pltpu.VMEM((8, WIDTH), F32)] * scratch,
        compiler_params=pltpu.CompilerParams(vmem_limit_bytes=16 * MIB),
    )(*first, *operands)


def scatter(first, second, core, lists, chip_bias, scaled):
    first_up, x1, x2 = first
    y1, y2, b1, b2, q1, q2, h0, h1 = second
    zero = jnp.zeros((), BF16)
    j0 = shift(first_up, None, Z_UP)
    ja1 = shift(jnp.where(core == 0, x1, add(y1, j0).astype(BF16)), X_UP, Z_UP)
    ja2 = shift(jnp.where(core == 0, x2, y2), X_DOWN, Z_DOWN)
    ja1, ja2 = lax.optimization_barrier((ja1, ja2))
    jb1 = shift(add(b1, ja1).astype(BF16), X_UP, Z_UP)
    jb2 = shift(add(b2, jnp.where(core == 0, zero, ja2)).astype(BF16), X_DOWN, Z_DOWN)
    jb1, jb2 = lax.optimization_barrier((jb1, jb2))
    wide = (2 * ROWS + BIAS_ROWS, WIDTH)
    pair_a, pair_b, line_bias = small_call(
        pair_kernel, ((wide, BF16), (wide, BF16), ((1, WIDTH), F32)), lists, (chip_bias, h0, ja1, ja2, jb1), 1
    )
    jc1 = shift(add(q1, jnp.where(core == 0, zero, jb1)).astype(BF16), X_UP, Z_UP)
    jc2 = shift(add(q2, jb2).astype(BF16), X_DOWN, Z_DOWN)
    ra = shift(pair_a, Z_UP_2)
    rb = shift(pair_b, Z_DOWN_2)
    jc1, jc2, ra, rb = lax.optimization_barrier((jc1, jc2, ra, rb))
    size = (ROWS + BIAS_ROWS, WIDTH)
    m1, m2, m3, rest = small_call(
        message_kernel,
        ((size, BF16), (size, BF16), (size, BF16), ((ROWS, WIDTH), F32)),
        None,
        (line_bias, h1, jc1, jc2, ra, rb),
        0,
    )
    r1 = shift(m1, Z_UP, X_UP)
    r2 = shift(m2, Z_DOWN, X_DOWN)
    r3 = shift(m3, Z_UP_2, X_TWO)
    return small_call(
        last_kernel,
        (((NODES, WIDTH), BF16), ((W_ROWS, WIDTH), F32), ((1, WIDTH), F32)),
        lists,
        (line_bias, rest, r1, r2, r3, rb, scaled),
        1,
    )


def nothing(value):
    return jnp.minimum(jnp.abs(value.astype(F32)), 0.0).astype(BF16)


def silu_parts(hidden):
    gate_value = jax.nn.sigmoid(hidden)
    return (hidden * gate_value, gate_value * (1.0 + hidden * (1.0 - gate_value)))


def on_device(feats, weight, bias, tile_values, tile_rows, tile_cols, tile_live, cotangent):
    dom = lax.axis_index("dom")
    y = lax.axis_index("feat")
    core = dom % 2
    x = (dom // 2) % NX
    z = dom // (2 * NX)

    meta = jnp.stack([tile_rows, tile_cols, jnp.broadcast_to(tile_live, (SLOTS,))])
    other_meta = swap(meta, 1)
    place = jnp.stack([core, x, z, y, tile_live[0], other_meta[2, 0]]).astype(jnp.int32)
    lists = make_lists(place, meta, other_meta)

    own_live = jnp.arange(SLOTS, dtype=jnp.int32) < tile_live[0]
    row_sums = jnp.sum(tile_values, axis=2, dtype=F32)
    degree = 1.0 + jnp.concatenate(
        [
            jnp.sum(jnp.where((own_live & (tile_rows == row))[:, None], row_sums, 0.0), axis=0)
            for row in range(2)
        ]
    ).reshape(NODES, 1)

    other_tiles = swap(tile_values, 1)
    sums, other_sums, weight_lane = gather(
        jnp.concatenate([feats, weight.T], axis=0),
        core,
        lists,
        other_tiles,
        lambda call, early, chunks, before: forward(call, early[0], tile_values, early[1], chunks, before),
    )
    neighbour_sum = (sums + swap(other_sums, 1)).reshape(NODES, WIDTH)
    weight_other = swap(weight_lane, 1)
    mixed = ((feats.astype(F32) + neighbour_sum) / degree).astype(BF16)

    first = jnp.where(core == 0, weight_lane, weight_other)
    second = jnp.where(core == 0, weight_other, weight_lane)
    weight_t = jnp.stack([first, second], axis=2).reshape(NY, WIDTH, WIDTH)

    def hidden_part(dy):
        return lax.dot_general(mixed, weight_t[dy], (((1,), (1,)), ((), ())), preferred_element_type=F32)

    hidden = add(
        hidden_part(0),
        y_shift(hidden_part(1).astype(BF16), 1),
        y_shift(hidden_part(2).astype(BF16), 2),
        y_shift(hidden_part(3).astype(BF16), 3),
    ) + bias
    activated, slope = silu_parts(hidden)
    output = activated.astype(BF16)
    dz_full = cotangent.astype(F32) * slope
    dz_own = dz_full.astype(BF16)
    dz_parts = [dz_own] + [y_shift(dz_own, NY - dy) for dy in range(1, NY)]

    dmixed = sum(jnp.dot(dz_parts[dy], weight_t[dy], preferred_element_type=F32) for dy in range(NY))
    scaled = (dmixed / degree).astype(BF16)
    scaled_blocks = jnp.concatenate([scaled, swap(scaled, 1)], axis=0).reshape(4, BLK, WIDTH)

    weight_part = jnp.stack(
        [
            lax.dot_general(dz_parts[dy], mixed, (((0,), (0,)), ((), ())), preferred_element_type=F32)
            for dy in range(NY)
        ]
    ).reshape(NY, 2 * NX, 2, W_ROWS, WIDTH)
    mine = jnp.where(core == 0, weight_part[:, :, 0], weight_part[:, :, 1])
    others = jnp.where(core == 0, weight_part[:, :, 1], weight_part[:, :, 0])
    bias_part = jnp.sum(dz_full, axis=0, keepdims=True)
    sent = jnp.concatenate([others.reshape(-1, WIDTH), jnp.pad(bias_part, ((0, 7), (0, 0)))], axis=0)
    got = swap(sent, 1)
    weight_sums = (mine + got[:-8].reshape(mine.shape)).astype(BF16)

    chip_bias = bias_part + got[-8:-7]
    bias_rows = split(chip_bias)
    parts = [
        backward(call, lists, tile_values, other_tiles, scaled_blocks, weight_sums, bias_rows)
        for call in range(len(SCATTER))
    ]
    feats_grad, weight_sum, bias_sum = scatter(*parts, core, lists, chip_bias, scaled)
    from_core_0 = lax.ppermute(bias_sum, "dom", [(i, i + 1) for i in range(0, NZ * NX * 2, 2)])
    bias_grad = jnp.where(core == 0, bias_sum, from_core_0)

    return (output, feats_grad, weight_sum.T, bias_grad.reshape(WIDTH))


def solution(mesh):
    return jax.shard_map(
        on_device,
        mesh=mesh,
        in_specs=(
            P("dom", "feat"),
            P("feat", "dom"),
            P("feat"),
            P("dom", None, None),
            P("dom"),
            P("dom"),
            P("dom"),
            P("dom", "feat"),
        ),
        out_specs=(P("dom", "feat"), P("dom", "feat"), P("feat", "dom"), P("feat")),
        check_vma=False,
    )
```

```python
import functools

import jax
import jax.numpy as jnp
from jax import lax
from jax.experimental import pallas as pl
from jax.experimental.pallas import tpu as pltpu
from jax.sharding import PartitionSpec as P

F32 = jnp.float32
BF16 = jnp.bfloat16
NZ, NX, NY = 8, 4, 4
BLK = 128
SLOTS = 128
WIDTH = 256
NODES = 2 * BLK
W_ROWS = 16
ROWS = NODES + W_ROWS
UNROLL = 8
FETCH = 16
BIAS_ROWS = 16
SUM_ROWS = 4 * ROWS + BIAS_ROWS
MIB = 1 << 20
VMEM = 54 * MIB

LOW, HIGH, ACROSS = (0, 1, 7, 2), (3, 4, 6, 5), (0, 1, 3, 2)
GATHER_0 = tuple(
    tuple(k * NZ + j for j in group)
    for k, group in ((0, LOW), (1, LOW), (3, LOW), (2, LOW), (3, HIGH), (1, HIGH), (2, HIGH), (0, HIGH))
)
GATHER_1 = tuple(tuple(k * NZ + j for k in ACROSS) for j in (0, 1, 7, 2, 6, 3, 5)) + (
    None,
    tuple(k * NZ + 4 for k in ACROSS[:2]),
    tuple(k * NZ + 4 for k in ACROSS[2:]),
)
FORWARD_CHUNKS = ((0, 1, 2), (3, 4, 7), (5, 6), (8, 9))
SCATTER = (
    (
        (None, tuple((dx, 4) for dx in ACROSS)),
        (tuple((2, dz) for dz in HIGH), None),
        (tuple((3, dz) for dz in HIGH), None),
    ),
    (
        (None, tuple((dx, 3) for dx in ACROSS)),
        (None, tuple((dx, 5) for dx in ACROSS)),
    ),
    (
        (tuple((1, dz) for dz in HIGH), tuple((dx, 2) for dx in ACROSS)),
        (tuple((2, dz) for dz in LOW), tuple((dx, 6) for dx in ACROSS)),
        (tuple((1, dz) for dz in LOW), tuple((dx, 1) for dx in ACROSS)),
        (tuple((3, dz) for dz in LOW), tuple((dx, 7) for dx in ACROSS)),
        (tuple((0, dz) for dz in HIGH), None),
        (tuple((0, dz) for dz in LOW), tuple((dx, 0) for dx in ACROSS)),
    ),
)


def shift(value, core_0=None, core_1=None):
    pairs = []
    for z in range(NZ):
        for x in range(NX):
            for core, step in enumerate((core_0, core_1)):
                if step is not None:
                    target = ((z + step[0]) % NZ * NX + (x + step[1]) % NX) * 2 + core
                    pairs.append(((z * NX + x) * 2 + core, target))
    return lax.ppermute(value, "dom", pairs)


Z_UP, Z_DOWN, Z_UP_2, Z_DOWN_2 = (1, 0), (-1, 0), (2, 0), (-2, 0)
X_UP, X_DOWN, X_TWO = (0, 1), (0, -1), (0, 2)


def swap(value, bit):
    return lax.ppermute(value, "dom", [(i, i ^ bit) for i in range(NZ * NX * 2)])


def y_shift(value, dy):
    return lax.ppermute(value, "feat", [(y, (y + dy) % NY) for y in range(NY)])


def smem():
    return pl.BlockSpec(memory_space=pltpu.SMEM)


def vmem():
    return pl.BlockSpec(memory_space=pltpu.VMEM)


def anywhere():
    return pl.BlockSpec(memory_space=pl.ANY)


def list_kernel(place, own, sib, lists):
    core, x, z = place[0], place[1], place[2]
    wide = (1, 2 * SLOTS)
    column = jnp.concatenate([own[1:2], sib[1:2]], axis=1)
    row = jnp.concatenate([own[0:1], sib[0:1] + 2], axis=1)
    slot = lax.broadcasted_iota(jnp.int32, wide, 1)
    live = slot < jnp.where(slot < SLOTS, place[4], SLOTS + place[5])
    owner = column >> 1
    chip = owner >> 1
    k = (x - (chip & (NX - 1))) & (NX - 1)
    j = (z - (chip >> 2)) & (NZ - 1)
    spot = (k * NZ + j) * 2 + (column & 1)
    mine = live & ((owner & 1) == core)
    high, back = (j >= 3) & (j <= 6), (j >= 2) & (j <= 5)
    on_0 = jnp.where(high, jnp.where((k == 1) | (k == 2), 2, 1), jnp.where(k == 2, 1, 0))
    on_1 = jnp.where(j == 4, 3, jnp.where((j == 3) | (j == 5), 2, jnp.where((j == 2) | (j == 6), 1, 0)))
    forward_call = jnp.where(core == 0, on_0, on_1)
    on_0 = jnp.where(back & ((k == 1) | (k == 2)), 0, 2)
    on_1 = jnp.where(j == 4, 0, jnp.where((j == 3) | (j == 5), 1, 2))
    backward_call = jnp.where(core == 0, on_0, on_1)
    square = (2 * SLOTS, 2 * SLOTS)
    first = lax.broadcasted_iota(jnp.int32, square, 0)
    second = lax.broadcasted_iota(jnp.int32, square, 1)
    up_to = jnp.where(first <= second, 1.0, 0.0).astype(BF16)
    group_of = lax.broadcasted_iota(jnp.int32, (16, 2 * SLOTS), 0)
    lane = lax.broadcasted_iota(jnp.int32, (16, 2 * SLOTS), 1)
    before = jnp.where(
        lax.broadcasted_iota(jnp.int32, (16, 16), 1) < lax.broadcasted_iota(jnp.int32, (16, 16), 0), 1.0, 0.0
    ).astype(BF16)
    values = jnp.concatenate([slot, spot], axis=0).astype(F32)
    values = jnp.concatenate([values, jnp.zeros((14, 2 * SLOTS), F32)], axis=0).astype(BF16)
    lists[...] = jnp.zeros_like(lists)
    for at, call in ((0, forward_call), (3, backward_call)):
        group = jnp.where(mine, call * 4 + row, -1)
        member = jnp.where(group_of == group, 1.0, 0.0)
        rank = jnp.dot(member.astype(BF16), up_to, preferred_element_type=F32)
        counts = jnp.sum(member, axis=1, keepdims=True)
        earlier = jnp.dot(before, member.astype(BF16), preferred_element_type=F32)
        starts = jnp.sum(earlier, axis=1, keepdims=True)
        goal = jnp.sum(member * (starts + rank), axis=0, keepdims=True).astype(jnp.int32) - 1
        moved = jnp.where(first == goal, 1.0, 0.0).astype(BF16)
        ordered = lax.dot_general(values, moved, (((1,), (1,)), ((), ())), preferred_element_type=F32)
        lists[at : at + 1, :] = jnp.sum(jnp.where(group_of == lane, counts, 0.0), axis=0, keepdims=True).astype(jnp.int32)
        lists[at + 1 : at + 2, :] = jnp.sum(jnp.where(group_of == lane, starts, 0.0), axis=0, keepdims=True).astype(jnp.int32)
        lists[at + 2 : at + 3, :] = (ordered[0:1] * 64.0 + ordered[1:2]).astype(jnp.int32)
    told = jnp.zeros(wide, jnp.int32)
    for i in range(6):
        told = jnp.where(slot == i, place[i], told)
    lists[6:7, :] = told


def make_lists(place, own, sib):
    return pl.pallas_call(
        list_kernel,
        out_shape=jax.ShapeDtypeStruct((8, 2 * SLOTS), jnp.int32),
        in_specs=[smem(), vmem(), vmem()],
        out_specs=vmem(),
    )(place, own, sib)


def place_of(lists):
    return [lists[6, i] for i in range(4)]


def copy_each(copies, action):
    for condition, copy in copies:
        call = getattr(copy, action)
        if condition is None:
            call()
        else:
            pl.when(condition)(call)


class Tiles:
    def __init__(self, lists, at, call, every, own, sib, held, sem):
        self.lists, self.at, self.call, self.every = lists, at, call, every
        self.own, self.sib, self.held, self.sem = own, sib, held, sem
        self.begin = lists[at + 1, call * 4]
        self.end = lists[at + 1, call * 4 + 3] + lists[at, call * 4 + 3]

    def bulk(self):
        copies = []
        for which, source in enumerate((self.own, self.sib)):
            for step in range(SLOTS // FETCH):
                first = step * FETCH
                copy = pltpu.make_async_copy(
                    source.at[pl.ds(first, FETCH)],
                    self.held.at[pl.ds(which * SLOTS + first, FETCH)],
                    self.sem.at[which * (SLOTS // FETCH) + step],
                )
                copies.append((first < self.lists[6, 4 + which], copy))
        return copies

    def each(self, action):
        def step(p, carry):
            slot = self.lists[self.at + 2, p] >> 6
            goal = self.held.at[p]

            @pl.when(slot < SLOTS)
            def _():
                getattr(pltpu.make_async_copy(self.own.at[jnp.minimum(slot, SLOTS - 1)], goal, self.sem.at[0]), action)()

            @pl.when(slot >= SLOTS)
            def _():
                getattr(pltpu.make_async_copy(self.sib.at[jnp.maximum(slot - SLOTS, 0)], goal, self.sem.at[0]), action)()

            return carry

        lax.fori_loop(self.begin, self.end, step, 0)

    def start(self):
        if self.every:
            copy_each(self.bulk(), "start")
        else:
            self.each("start")
        self.held[2 * SLOTS] = jnp.zeros((BLK, BLK), BF16)

    def wait(self):
        if self.every:
            copy_each(self.bulk(), "wait")
        else:
            self.each("wait")

    def rows(self):
        for row in range(4):
            group = self.call * 4 + row
            number, first = self.lists[self.at, group], self.lists[self.at + 1, group]

            def pick(it, number=number, first=first):
                lefts, spots = [], []
                for u in range(UNROLL):
                    p = it * UNROLL + u
                    entry = self.lists[self.at + 2, first + jnp.minimum(p, number - 1)]
                    place = entry >> 6 if self.every else first + p
                    lefts.append(self.held[jnp.where(p < number, place, 2 * SLOTS)])
                    spots.append(entry & 63)
                return jnp.concatenate(lefts, axis=1), spots

            yield row, lax.div(number + (UNROLL - 1), UNROLL), pick


def forward_kernel(call, lists, own, sib, *rest):
    chosen = FORWARD_CHUNKS[call]
    chunks, rest = rest[: len(chosen)], rest[len(chosen) :]
    if call:
        own_before, sib_before, weight_before, *rest = rest
    own_sums, sib_sums, weight_out, blocks, held, sem, tile_sem = rest
    core, x, z, y = place_of(lists)
    tiles = Tiles(lists, 0, call, False, own, sib, held, tile_sem)
    tiles.start()
    copies, arrived = [], []
    for n, chunk in zip(chosen, chunks):
        condition = None if n < 7 else core == (0 if n == 7 else 1)
        for i in range(chunk.shape[0]):
            if n < 7:
                spot = jnp.where(core == 0, GATHER_0[n][i], GATHER_1[n][i])
            else:
                spot = GATHER_0[n][i] if n == 7 else GATHER_1[n][i]
            copies.append((condition, pltpu.make_async_copy(chunk.at[i], blocks.at[spot], sem.at[len(copies)])))
            arrived.append((condition, spot))
    copy_each(copies, "start")
    copy_each(copies, "wait")
    tiles.wait()
    for row, steps, pick in tiles.rows():

        def step(it, total):
            left, spots = pick(it)
            rights = []
            for spot in spots:
                first = pl.multiple_of((spot & 1) * BLK, BLK)
                rights.append(blocks[spot >> 1, pl.ds(first, BLK), :])
            return total + jnp.dot(left, jnp.concatenate(rights, axis=0), preferred_element_type=F32)

        sums, at = (own_sums, row) if row < 2 else (sib_sums, row - 2)
        before = jnp.zeros((BLK, WIDTH), F32)
        if call:
            before = own_before[at] if row < 2 else sib_before[at]
        sums[at] = lax.fori_loop(0, steps, step, before)
    if call:
        weight_out[...] = weight_before[...]
    for condition, spot in arrived:

        def keep(spot=spot):
            column = (x - (spot >> 3)) & (NX - 1)
            level = (z - spot) & (NZ - 1)
            part = ((level >> 1) - y) & (NY - 1)
            weight_out[part, (level & 1) * NX + column] = blocks[spot, NODES:ROWS, :]

        if condition is None:
            keep()
        else:
            pl.when(condition)(keep)


def forward(call, lists, own, sib, chunks, before):
    chosen = [chunks[n] for n in FORWARD_CHUNKS[call]]
    return pl.pallas_call(
        functools.partial(forward_kernel, call),
        out_shape=(
            jax.ShapeDtypeStruct((2, BLK, WIDTH), F32),
            jax.ShapeDtypeStruct((2, BLK, WIDTH), F32),
            jax.ShapeDtypeStruct((NY, 2 * NX, W_ROWS, WIDTH), BF16),
        ),
        in_specs=[smem()] + [anywhere()] * (2 + len(chosen)) + [vmem()] * len(before),
        out_specs=(vmem(),) * 3,
        scratch_shapes=[
            pltpu.VMEM((NX * NZ, ROWS, WIDTH), BF16),
            pltpu.VMEM((2 * SLOTS + 1, BLK, BLK), BF16),
            pltpu.SemaphoreType.DMA((32,)),
            pltpu.SemaphoreType.DMA((2 * SLOTS // FETCH,)),
        ],
        compiler_params=pltpu.CompilerParams(vmem_limit_bytes=VMEM),
        cost_estimate=pl.CostEstimate(
            flops=2 * BLK * BLK * WIDTH * len(chosen) * 16, bytes_accessed=len(chosen) * MIB, transcendentals=0
        ),
    )(lists, own, sib, *chosen, *before)


def backward_kernel(call, lists, own, sib, scaled, weight_sums, bias_rows, *rest):
    chunks = SCATTER[call]
    outs, rest = rest[: len(chunks)], rest[len(chunks) :]
    total, held, tile_sem = rest
    core, x, z, y = place_of(lists)
    tiles = Tiles(lists, 3, call, call == 2, own, sib, held, tile_sem)
    tiles.start()

    def each_chunk(action):
        for out, chunk in zip(outs, chunks):
            if None in chunk:
                side = 1 if chunk[0] is None else 0

                @pl.when(core == side)
                def _(out=out, places=chunk[side]):
                    action(out, places)
            else:
                action(out, [[jnp.where(core == 0, p, q) for p, q in zip(*pair)] for pair in zip(*chunk)])

    def spot_of(dx, dz):
        return ((0 - dx) & (NX - 1)) * NZ + ((0 - dz) & (NZ - 1))

    def clear(out, places):
        for dx, dz in places:
            spot = spot_of(dx, dz)
            total[spot * 2] = jnp.zeros((BLK, WIDTH), F32)
            total[spot * 2 + 1] = jnp.zeros((BLK, WIDTH), F32)

    def emit(out, places):
        for i, (dx, dz) in enumerate(places):
            spot = spot_of(dx, dz)
            first = i * ROWS
            out[first : first + BLK, :] = total[spot * 2].astype(BF16)
            out[first + BLK : first + NODES, :] = total[spot * 2 + 1].astype(BF16)
            column = (x + dx) & (NX - 1)
            level = (z + dz) & (NZ - 1)
            part = ((level >> 1) - y) & (NY - 1)
            out[first + NODES : first + ROWS, :] = weight_sums[part, (level & 1) * NX + column]
        out[4 * ROWS : SUM_ROWS, :] = bias_rows[...] if call == 0 else jnp.zeros((BIAS_ROWS, WIDTH), BF16)

    each_chunk(clear)
    tiles.wait()
    for row, steps, pick in tiles.rows():
        right = scaled[row]

        def step(it, carry):
            left, spots = pick(it)
            terms = lax.dot_general(left, right, (((0,), (0,)), ((), ())), preferred_element_type=F32)
            for u, spot in enumerate(spots):
                total[spot] += terms[u * BLK : (u + 1) * BLK]
            return carry

        lax.fori_loop(0, steps, step, 0)
    each_chunk(emit)


def backward(call, lists, own, sib, scaled, weight_sums, bias_rows):
    shapes = []
    for _ in SCATTER[call]:
        shapes.append(jax.ShapeDtypeStruct((SUM_ROWS, WIDTH), BF16))
    return pl.pallas_call(
        functools.partial(backward_kernel, call),
        out_shape=tuple(shapes),
        in_specs=[smem()] + [anywhere()] * 2 + [vmem()] * 3,
        out_specs=(vmem(),) * len(shapes),
        scratch_shapes=[
            pltpu.VMEM((2 * NX * NZ, BLK, WIDTH), F32),
            pltpu.VMEM((2 * SLOTS + 1, BLK, BLK), BF16),
            pltpu.SemaphoreType.DMA((2 * SLOTS // FETCH,)),
        ],
        compiler_params=pltpu.CompilerParams(vmem_limit_bytes=VMEM),
        cost_estimate=pl.CostEstimate(
            flops=2 * BLK * BLK * WIDTH * len(shapes) * 16, bytes_accessed=len(shapes) * MIB, transcendentals=0
        ),
    )(lists, own, sib, scaled, weight_sums, bias_rows)


def gather(block, core, lists, other_tiles, degree, call):
    p1 = shift(block, Z_UP, X_UP)
    p2 = shift(block, Z_DOWN, X_DOWN)
    p3 = shift(block, Z_UP_2, X_TWO)
    low, other_tiles = lax.optimization_barrier((jnp.stack([block, p1, p2, p3]), other_tiles))
    c1 = shift(low, X_UP, Z_UP)
    c2 = shift(low, X_DOWN, Z_DOWN)
    pa = shift(jnp.stack([low[1], low[3]]), Z_UP_2)
    pb = shift(jnp.stack([low[0], low[2]]), Z_DOWN_2)
    c1, c2, pa, pb, lists, degree = lax.optimization_barrier((c1, c2, pa, pb, lists, degree))
    high = jnp.concatenate([pa, pb], axis=0)
    early = lists, other_tiles
    c3 = shift(c1, X_UP, Z_UP)
    c4 = shift(jnp.where(core == 0, high, c2), X_DOWN, Z_DOWN)
    chunks = [low, c1, c2]
    sums = call(0, early, chunks, ())
    c3, c4, sums = lax.optimization_barrier((c3, c4, sums))
    chunks += [c3, c4, None, None, high]
    sums = call(1, early, chunks, sums)
    c5 = shift(jnp.where(core == 0, high, c3), X_UP, Z_UP)
    c6 = shift(c4, X_DOWN, Z_DOWN)
    c5, c6, sums = lax.optimization_barrier((c5, c6, sums))
    chunks[5:7] = c5, c6
    chunks += [shift(c5[:2], None, Z_UP), shift(c6[2:], None, Z_DOWN)]
    return degree, call(3, early, chunks, call(2, early, chunks, sums))


def add(*values):
    total = values[0].astype(F32)
    for value in values[1:]:
        total = total + value.astype(F32)
    return total


def split(value):
    high = lax.reduce_precision(value, 8, 7)
    middle = lax.reduce_precision(value - high, 8, 7)
    rows = jnp.concatenate([high, middle, value - high - middle], axis=0)
    return jnp.pad(rows, ((0, BIAS_ROWS - 3), (0, 0))).astype(BF16)


def rows_of(value):
    high = value.astype(BF16)
    middle = (value - high.astype(F32)).astype(BF16)
    low = (value - high.astype(F32) - middle.astype(F32)).astype(BF16)
    return [high.astype(F32), middle.astype(F32), low.astype(F32)]


def bias_block(rows):
    used = sum(row.shape[0] for row in rows)
    rows = rows + [jnp.zeros((BIAS_ROWS - used, WIDTH), F32)]
    return jnp.concatenate(rows, axis=0).astype(BF16)


def joined(block, first=0):
    rows = block.astype(F32)
    return rows[first : first + 1] + rows[first + 1 : first + 2] + rows[first + 2 : first + 3]


def in_order(values, place, held):
    count = len(values)
    for k, value in enumerate(values):
        held[k : k + 1, :] = value
    total = held[pl.ds(place & (count - 1), 1), :]
    for i in range(1, count):
        total = total + held[pl.ds((place - i) & (count - 1), 1), :]
    return total


def block_sum(i, *chunks):
    total = chunks[0][i * ROWS : (i + 1) * ROWS, :].astype(F32)
    for chunk in chunks[1:]:
        total = total + chunk[i * ROWS : (i + 1) * ROWS, :].astype(F32)
    return total


def tail_of(chunk):
    return chunk[4 * ROWS : SUM_ROWS, :]


def pair_kernel(lists, chip_bias, h0, ja1, ja2, jb1, pair_a, pair_b, line_bias, held):
    line = in_order([chip_bias[...], joined(tail_of(ja1)), joined(tail_of(jb1)), joined(tail_of(ja2))], lists[6, 1], held)
    line_bias[...] = line
    rows = bias_block(rows_of(line))
    for pair, first in ((pair_a, 0), (pair_b, 2)):
        for i in range(2):
            pair[i * ROWS : (i + 1) * ROWS, :] = block_sum(first + i, h0, jb1, ja2).astype(BF16)
        pair[2 * ROWS : 2 * ROWS + BIAS_ROWS, :] = rows


def message_kernel(line_bias, h1, jc1, jc2, ra, rb, m1, m2, m3, rest):
    own = rows_of(line_bias[...])
    rest[...] = block_sum(0, h1, jc1, jc2) + block_sum(0, rb)
    relayed = [chunk[2 * ROWS : 2 * ROWS + BIAS_ROWS, :].astype(F32)[0:3] for chunk in (ra, rb)]
    m1[0:ROWS, :] = (block_sum(1, h1, jc1, jc2) + block_sum(0, ra)).astype(BF16)
    m1[ROWS:, :] = bias_block(own + [relayed[0]])
    m2[0:ROWS, :] = (block_sum(2, h1, jc1, jc2) + block_sum(1, rb)).astype(BF16)
    m2[ROWS:, :] = bias_block(own + [relayed[1]])
    m3[0:ROWS, :] = (block_sum(3, h1, jc1, jc2) + block_sum(1, ra)).astype(BF16)
    m3[ROWS:, :] = bias_block(own + [relayed[0]])


def bias_kernel(lists, line_bias, r1, r2, r3, rb, bias, held):
    t1, t2, t3 = (chunk[ROWS:, :] for chunk in (r1, r2, r3))
    tb = rb[2 * ROWS :, :]
    values = [line_bias[...], joined(t1), joined(t3), joined(t1, 3), joined(t3, 3), joined(t2, 3), joined(tb), joined(t2)]
    bias[...] = in_order(values, lists[6, 2], held)


def last_kernel(rest, r1, r2, r3, scaled, feats_grad, weight_grad):
    total = rest[...] + block_sum(0, r1, r2, r3)
    feats_grad[...] = (scaled[...].astype(F32) + total[0:NODES]).astype(BF16)
    weight_grad[...] = total[NODES:ROWS]


def small_call(kernel, shapes, lists, operands, scratch):
    first = [] if lists is None else [lists]
    return pl.pallas_call(
        kernel,
        out_shape=tuple(jax.ShapeDtypeStruct(shape, dtype) for shape, dtype in shapes),
        in_specs=[smem()] * len(first) + [vmem()] * len(operands),
        out_specs=(vmem(),) * len(shapes),
        scratch_shapes=[pltpu.VMEM((8, WIDTH), F32)] * scratch,
        compiler_params=pltpu.CompilerParams(vmem_limit_bytes=16 * MIB),
    )(*first, *operands)


def scatter(parts, weight_sums, core, lists, chip_bias, scaled):
    first_up, x1, x2 = parts(0, weight_sums)
    zero = jnp.zeros((), BF16)
    j0 = shift(first_up, None, Z_UP)
    y1, y2 = parts(1, weight_sums)
    j0, y1, y2, weight_sums = lax.optimization_barrier((j0, y1, y2, weight_sums))
    b1, b2, q1, q2, h0, h1 = parts(2, weight_sums)
    ja1 = shift(jnp.where(core == 0, x1, add(y1, j0).astype(BF16)), X_UP, Z_UP)
    ja2 = shift(jnp.where(core == 0, x2, y2), X_DOWN, Z_DOWN)
    ja1, ja2 = lax.optimization_barrier((ja1, ja2))
    jb1 = shift(add(b1, ja1).astype(BF16), X_UP, Z_UP)
    jb2 = shift(add(b2, jnp.where(core == 0, zero, ja2)).astype(BF16), X_DOWN, Z_DOWN)
    jb1, jb2 = lax.optimization_barrier((jb1, jb2))
    wide = (2 * ROWS + BIAS_ROWS, WIDTH)
    pair_a, pair_b, line_bias = small_call(
        pair_kernel, ((wide, BF16), (wide, BF16), ((1, WIDTH), F32)), lists, (chip_bias, h0, ja1, ja2, jb1), 1
    )
    jc1 = shift(add(q1, jnp.where(core == 0, zero, jb1)).astype(BF16), X_UP, Z_UP)
    jc2 = shift(add(q2, jb2).astype(BF16), X_DOWN, Z_DOWN)
    ra = shift(pair_a, Z_UP_2)
    rb = shift(pair_b, Z_DOWN_2)
    jc1, jc2, ra, rb = lax.optimization_barrier((jc1, jc2, ra, rb))
    size = (ROWS + BIAS_ROWS, WIDTH)
    m1, m2, m3, rest = small_call(
        message_kernel,
        ((size, BF16), (size, BF16), (size, BF16), ((ROWS, WIDTH), F32)),
        None,
        (line_bias, h1, jc1, jc2, ra, rb),
        0,
    )
    r1 = shift(m1, Z_UP, X_UP)
    r2 = shift(m2, Z_DOWN, X_DOWN)
    r3 = shift(m3, Z_UP_2, X_TWO)
    (bias,) = small_call(bias_kernel, (((1, WIDTH), F32),), lists, (line_bias, r1, r2, r3, rb), 1)
    from_core_0 = lax.ppermute(bias, "dom", [(i, i + 1) for i in range(0, NZ * NX * 2, 2)])
    feats_grad, weight_grad = small_call(
        last_kernel, (((NODES, WIDTH), BF16), ((W_ROWS, WIDTH), F32)), None, (rest, r1, r2, r3, scaled), 0
    )
    return feats_grad, weight_grad, jnp.where(core == 0, bias, from_core_0)


def silu_parts(hidden):
    gate_value = jax.nn.sigmoid(hidden)
    return (hidden * gate_value, gate_value * (1.0 + hidden * (1.0 - gate_value)))


def on_device(feats, weight, bias, tile_values, tile_rows, tile_cols, tile_live, cotangent):
    dom = lax.axis_index("dom")
    y = lax.axis_index("feat")
    core = dom % 2
    x = (dom // 2) % NX
    z = dom // (2 * NX)

    meta = jnp.stack([tile_rows, tile_cols, jnp.broadcast_to(tile_live, (SLOTS,))])
    other_meta = swap(meta, 1)
    place = jnp.stack([core, x, z, y, tile_live[0], other_meta[2, 0]]).astype(jnp.int32)
    lists = make_lists(place, meta, other_meta)

    own_live = jnp.arange(SLOTS, dtype=jnp.int32) < tile_live[0]
    row_sums = jnp.sum(tile_values, axis=2, dtype=F32)
    degree = 1.0 + jnp.concatenate(
        [
            jnp.sum(jnp.where((own_live & (tile_rows == row))[:, None], row_sums, 0.0), axis=0)
            for row in range(2)
        ]
    ).reshape(NODES, 1)

    other_tiles = swap(tile_values, 1)
    degree, (sums, other_sums, weight_lane) = gather(
        jnp.concatenate([feats, weight.T], axis=0),
        core,
        lists,
        other_tiles,
        degree,
        lambda call, early, chunks, before: forward(call, early[0], tile_values, early[1], chunks, before),
    )
    neighbour_sum = (sums + swap(other_sums, 1)).reshape(NODES, WIDTH)
    weight_other = swap(weight_lane, 1)
    mixed = ((feats.astype(F32) + neighbour_sum) / degree).astype(BF16)

    first = jnp.where(core == 0, weight_lane, weight_other)
    second = jnp.where(core == 0, weight_other, weight_lane)
    weight_t = jnp.stack([first, second], axis=2).reshape(NY, WIDTH, WIDTH)

    def hidden_part(dy):
        return lax.dot_general(mixed, weight_t[dy], (((1,), (1,)), ((), ())), preferred_element_type=F32)

    hidden = add(
        hidden_part(0),
        y_shift(hidden_part(1).astype(BF16), 1),
        y_shift(hidden_part(2).astype(BF16), 2),
        y_shift(hidden_part(3).astype(BF16), 3),
    ) + bias
    activated, slope = silu_parts(hidden)
    output = activated.astype(BF16)
    dz_full = cotangent.astype(F32) * slope
    dz_own = dz_full.astype(BF16)
    dz_parts = [dz_own] + [y_shift(dz_own, NY - dy) for dy in range(1, NY)]

    dmixed = sum(jnp.dot(dz_parts[dy], weight_t[dy], preferred_element_type=F32) for dy in range(NY))
    scaled = (dmixed / degree).astype(BF16)
    scaled_blocks = jnp.concatenate([scaled, swap(scaled, 1)], axis=0).reshape(4, BLK, WIDTH)

    weight_part = jnp.stack(
        [
            lax.dot_general(dz_parts[dy], mixed, (((0,), (0,)), ((), ())), preferred_element_type=F32)
            for dy in range(NY)
        ]
    ).reshape(NY, 2 * NX, 2, W_ROWS, WIDTH)
    mine = jnp.where(core == 0, weight_part[:, :, 0], weight_part[:, :, 1])
    others = jnp.where(core == 0, weight_part[:, :, 1], weight_part[:, :, 0])
    bias_part = jnp.sum(dz_full, axis=0, keepdims=True)
    sent = jnp.concatenate([others.reshape(-1, WIDTH), jnp.pad(bias_part, ((0, 7), (0, 0)))], axis=0)
    got = swap(sent, 1)
    weight_sums = (mine + got[:-8].reshape(mine.shape)).astype(BF16)

    chip_bias = bias_part + got[-8:-7]
    bias_rows = split(chip_bias)

    def parts(call, weight_sums):
        return backward(call, lists, tile_values, other_tiles, scaled_blocks, weight_sums, bias_rows)

    feats_grad, weight_sum, bias_grad = scatter(parts, weight_sums, core, lists, chip_bias, scaled)
    return (output, feats_grad, weight_sum.T, bias_grad.reshape(WIDTH))


def solution(mesh):
    return jax.shard_map(
        on_device,
        mesh=mesh,
        in_specs=(
            P("dom", "feat"),
            P("feat", "dom"),
            P("feat"),
            P("dom", None, None),
            P("dom"),
            P("dom"),
            P("dom"),
            P("dom", "feat"),
        ),
        out_specs=(P("dom", "feat"), P("dom", "feat"), P("feat", "dom"), P("feat")),
        check_vma=False,
    )
```

```python
import functools

import jax
import jax.numpy as jnp
from jax import lax
from jax.experimental import pallas as pl
from jax.experimental.pallas import tpu as pltpu
from jax.sharding import PartitionSpec as P

F32 = jnp.float32
BF16 = jnp.bfloat16
NZ, NX, NY = 8, 4, 4
BLK = 128
SLOTS = 128
WIDTH = 256
NODES = 2 * BLK
W_ROWS = 16
ROWS = NODES + W_ROWS
UNROLL = 8
FETCH = 16
BIAS_ROWS = 16
SUM_ROWS = 4 * ROWS + BIAS_ROWS
MIB = 1 << 20
VMEM = 54 * MIB

LOW, HIGH, ACROSS = (0, 1, 7, 2), (3, 4, 6, 5), (0, 1, 3, 2)
GATHER_0 = tuple(
    tuple(k * NZ + j for j in group)
    for k, group in ((0, LOW), (1, LOW), (3, LOW), (2, LOW), (3, HIGH), (1, HIGH), (2, HIGH), (0, HIGH))
)
GATHER_1 = tuple(tuple(k * NZ + j for k in ACROSS) for j in (0, 1, 7, 2, 6, 3, 5)) + (
    None,
    tuple(k * NZ + 4 for k in ACROSS[:2]),
    tuple(k * NZ + 4 for k in ACROSS[2:]),
)
FORWARD_CHUNKS = ((0, 1, 2), (3, 4, 7), (5, 6), (8, 9))
SCATTER = (
    (
        (None, tuple((dx, 4) for dx in ACROSS)),
        (tuple((2, dz) for dz in HIGH), None),
        (tuple((3, dz) for dz in HIGH), None),
    ),
    (
        (None, tuple((dx, 3) for dx in ACROSS)),
        (None, tuple((dx, 5) for dx in ACROSS)),
        (tuple((1, dz) for dz in HIGH), tuple((dx, 2) for dx in ACROSS)),
        (tuple((2, dz) for dz in LOW), tuple((dx, 6) for dx in ACROSS)),
        (tuple((1, dz) for dz in LOW), tuple((dx, 1) for dx in ACROSS)),
        (tuple((3, dz) for dz in LOW), tuple((dx, 7) for dx in ACROSS)),
        (tuple((0, dz) for dz in HIGH), None),
        (tuple((0, dz) for dz in LOW), tuple((dx, 0) for dx in ACROSS)),
    ),
)


def shift(value, core_0=None, core_1=None):
    pairs = []
    for z in range(NZ):
        for x in range(NX):
            for core, step in enumerate((core_0, core_1)):
                if step is not None:
                    target = ((z + step[0]) % NZ * NX + (x + step[1]) % NX) * 2 + core
                    pairs.append(((z * NX + x) * 2 + core, target))
    return lax.ppermute(value, "dom", pairs)


Z_UP, Z_DOWN, Z_UP_2, Z_DOWN_2 = (1, 0), (-1, 0), (2, 0), (-2, 0)
X_UP, X_DOWN, X_TWO = (0, 1), (0, -1), (0, 2)


def swap(value, bit):
    return lax.ppermute(value, "dom", [(i, i ^ bit) for i in range(NZ * NX * 2)])


def y_shift(value, dy):
    return lax.ppermute(value, "feat", [(y, (y + dy) % NY) for y in range(NY)])


def smem():
    return pl.BlockSpec(memory_space=pltpu.SMEM)


def vmem():
    return pl.BlockSpec(memory_space=pltpu.VMEM)


def anywhere():
    return pl.BlockSpec(memory_space=pl.ANY)


def list_kernel(place, own, sib, lists):
    core, x, z = place[0], place[1], place[2]
    wide = (1, 2 * SLOTS)
    column = jnp.concatenate([own[1:2], sib[1:2]], axis=1)
    row = jnp.concatenate([own[0:1], sib[0:1] + 2], axis=1)
    slot = lax.broadcasted_iota(jnp.int32, wide, 1)
    live = slot < jnp.where(slot < SLOTS, place[4], SLOTS + place[5])
    owner = column >> 1
    chip = owner >> 1
    k = (x - (chip & (NX - 1))) & (NX - 1)
    j = (z - (chip >> 2)) & (NZ - 1)
    spot = (k * NZ + j) * 2 + (column & 1)
    mine = live & ((owner & 1) == core)
    high, back = (j >= 3) & (j <= 6), (j >= 2) & (j <= 5)
    on_0 = jnp.where(high, jnp.where((k == 1) | (k == 2), 2, 1), jnp.where(k == 2, 1, 0))
    on_1 = jnp.where(j == 4, 3, jnp.where((j == 3) | (j == 5), 2, jnp.where((j == 2) | (j == 6), 1, 0)))
    forward_call = jnp.where(core == 0, on_0, on_1)
    backward_call = jnp.where(core == 0, jnp.where(back & ((k == 1) | (k == 2)), 0, 1), jnp.where(j == 4, 0, 1))
    square = (2 * SLOTS, 2 * SLOTS)
    first = lax.broadcasted_iota(jnp.int32, square, 0)
    second = lax.broadcasted_iota(jnp.int32, square, 1)
    up_to = jnp.where(first <= second, 1.0, 0.0).astype(BF16)
    group_of = lax.broadcasted_iota(jnp.int32, (16, 2 * SLOTS), 0)
    lane = lax.broadcasted_iota(jnp.int32, (16, 2 * SLOTS), 1)
    before = jnp.where(
        lax.broadcasted_iota(jnp.int32, (16, 16), 1) < lax.broadcasted_iota(jnp.int32, (16, 16), 0), 1.0, 0.0
    ).astype(BF16)
    values = jnp.concatenate([slot, spot], axis=0).astype(F32)
    values = jnp.concatenate([values, jnp.zeros((14, 2 * SLOTS), F32)], axis=0).astype(BF16)
    lists[...] = jnp.zeros_like(lists)
    for at, call in ((0, forward_call), (3, backward_call)):
        group = jnp.where(mine, call * 4 + row, -1)
        member = jnp.where(group_of == group, 1.0, 0.0)
        rank = jnp.dot(member.astype(BF16), up_to, preferred_element_type=F32)
        counts = jnp.sum(member, axis=1, keepdims=True)
        earlier = jnp.dot(before, member.astype(BF16), preferred_element_type=F32)
        starts = jnp.sum(earlier, axis=1, keepdims=True)
        goal = jnp.sum(member * (starts + rank), axis=0, keepdims=True).astype(jnp.int32) - 1
        moved = jnp.where(first == goal, 1.0, 0.0).astype(BF16)
        ordered = lax.dot_general(values, moved, (((1,), (1,)), ((), ())), preferred_element_type=F32)
        lists[at : at + 1, :] = jnp.sum(jnp.where(group_of == lane, counts, 0.0), axis=0, keepdims=True).astype(jnp.int32)
        lists[at + 1 : at + 2, :] = jnp.sum(jnp.where(group_of == lane, starts, 0.0), axis=0, keepdims=True).astype(jnp.int32)
        lists[at + 2 : at + 3, :] = (ordered[0:1] * 64.0 + ordered[1:2]).astype(jnp.int32)
    told = jnp.zeros(wide, jnp.int32)
    for i in range(6):
        told = jnp.where(slot == i, place[i], told)
    lists[6:7, :] = told


def make_lists(place, own, sib):
    return pl.pallas_call(
        list_kernel,
        out_shape=jax.ShapeDtypeStruct((8, 2 * SLOTS), jnp.int32),
        in_specs=[smem(), vmem(), vmem()],
        out_specs=vmem(),
    )(place, own, sib)


def place_of(lists):
    return [lists[6, i] for i in range(4)]


def copy_each(copies, action):
    for condition, copy in copies:
        call = getattr(copy, action)
        if condition is None:
            call()
        else:
            pl.when(condition)(call)


class Tiles:
    def __init__(self, lists, at, call, every, own, sib, held, sem):
        self.lists, self.at, self.call, self.every = lists, at, call, every
        self.own, self.sib, self.held, self.sem = own, sib, held, sem
        self.begin = lists[at + 1, call * 4]
        self.end = lists[at + 1, call * 4 + 3] + lists[at, call * 4 + 3]

    def bulk(self):
        copies = []
        for which, source in enumerate((self.own, self.sib)):
            for step in range(SLOTS // FETCH):
                first = step * FETCH
                copy = pltpu.make_async_copy(
                    source.at[pl.ds(first, FETCH)],
                    self.held.at[pl.ds(which * SLOTS + first, FETCH)],
                    self.sem.at[which * (SLOTS // FETCH) + step],
                )
                copies.append((first < self.lists[6, 4 + which], copy))
        return copies

    def each(self, action):
        def step(p, carry):
            slot = self.lists[self.at + 2, p] >> 6
            goal = self.held.at[p]

            @pl.when(slot < SLOTS)
            def _():
                getattr(pltpu.make_async_copy(self.own.at[jnp.minimum(slot, SLOTS - 1)], goal, self.sem.at[0]), action)()

            @pl.when(slot >= SLOTS)
            def _():
                getattr(pltpu.make_async_copy(self.sib.at[jnp.maximum(slot - SLOTS, 0)], goal, self.sem.at[0]), action)()

            return carry

        lax.fori_loop(self.begin, self.end, step, 0)

    def start(self):
        if self.every:
            copy_each(self.bulk(), "start")
        else:
            self.each("start")
        self.held[2 * SLOTS] = jnp.zeros((BLK, BLK), BF16)

    def wait(self):
        if self.every:
            copy_each(self.bulk(), "wait")
        else:
            self.each("wait")

    def rows(self):
        for row in range(4):
            group = self.call * 4 + row
            number, first = self.lists[self.at, group], self.lists[self.at + 1, group]

            def pick(it, number=number, first=first):
                lefts, spots = [], []
                for u in range(UNROLL):
                    p = it * UNROLL + u
                    entry = self.lists[self.at + 2, first + jnp.minimum(p, number - 1)]
                    place = entry >> 6 if self.every else first + p
                    lefts.append(self.held[jnp.where(p < number, place, 2 * SLOTS)])
                    spots.append(entry & 63)
                return jnp.concatenate(lefts, axis=1), spots

            yield row, lax.div(number + (UNROLL - 1), UNROLL), pick


def forward_kernel(call, lists, own, sib, *rest):
    chosen = FORWARD_CHUNKS[call]
    chunks, rest = rest[: len(chosen)], rest[len(chosen) :]
    if call:
        own_before, sib_before, weight_before, *rest = rest
    own_sums, sib_sums, weight_out, blocks, held, sem, tile_sem = rest
    core, x, z, y = place_of(lists)
    tiles = Tiles(lists, 0, call, False, own, sib, held, tile_sem)
    tiles.start()
    copies, arrived = [], []
    for n, chunk in zip(chosen, chunks):
        condition = None if n < 7 else core == (0 if n == 7 else 1)
        for i in range(chunk.shape[0]):
            if n < 7:
                spot = jnp.where(core == 0, GATHER_0[n][i], GATHER_1[n][i])
            else:
                spot = GATHER_0[n][i] if n == 7 else GATHER_1[n][i]
            copies.append((condition, pltpu.make_async_copy(chunk.at[i], blocks.at[spot], sem.at[len(copies)])))
            arrived.append((condition, spot))
    copy_each(copies, "start")
    copy_each(copies, "wait")
    tiles.wait()
    for row, steps, pick in tiles.rows():

        def step(it, total):
            left, spots = pick(it)
            rights = []
            for spot in spots:
                first = pl.multiple_of((spot & 1) * BLK, BLK)
                rights.append(blocks[spot >> 1, pl.ds(first, BLK), :])
            return total + jnp.dot(left, jnp.concatenate(rights, axis=0), preferred_element_type=F32)

        sums, at = (own_sums, row) if row < 2 else (sib_sums, row - 2)
        before = jnp.zeros((BLK, WIDTH), F32)
        if call:
            before = own_before[at] if row < 2 else sib_before[at]
        sums[at] = lax.fori_loop(0, steps, step, before)
    if call:
        weight_out[...] = weight_before[...]
    for condition, spot in arrived:

        def keep(spot=spot):
            column = (x - (spot >> 3)) & (NX - 1)
            level = (z - spot) & (NZ - 1)
            part = ((level >> 1) - y) & (NY - 1)
            weight_out[part, (level & 1) * NX + column] = blocks[spot, NODES:ROWS, :]

        if condition is None:
            keep()
        else:
            pl.when(condition)(keep)


def forward(call, lists, own, sib, chunks, before):
    chosen = [chunks[n] for n in FORWARD_CHUNKS[call]]
    return pl.pallas_call(
        functools.partial(forward_kernel, call),
        out_shape=(
            jax.ShapeDtypeStruct((2, BLK, WIDTH), F32),
            jax.ShapeDtypeStruct((2, BLK, WIDTH), F32),
            jax.ShapeDtypeStruct((NY, 2 * NX, W_ROWS, WIDTH), BF16),
        ),
        in_specs=[smem()] + [anywhere()] * (2 + len(chosen)) + [vmem()] * len(before),
        out_specs=(vmem(),) * 3,
        scratch_shapes=[
            pltpu.VMEM((NX * NZ, ROWS, WIDTH), BF16),
            pltpu.VMEM((2 * SLOTS + 1, BLK, BLK), BF16),
            pltpu.SemaphoreType.DMA((32,)),
            pltpu.SemaphoreType.DMA((2 * SLOTS // FETCH,)),
        ],
        compiler_params=pltpu.CompilerParams(vmem_limit_bytes=VMEM),
        cost_estimate=pl.CostEstimate(
            flops=2 * BLK * BLK * WIDTH * len(chosen) * 16, bytes_accessed=len(chosen) * MIB, transcendentals=0
        ),
    )(lists, own, sib, *chosen, *before)


def backward_kernel(call, lists, own, sib, scaled, other_scaled, weight_sums, chip_bias, *rest):
    chunks = SCATTER[call]
    outs, rest = rest[: len(chunks)], rest[len(chunks) :]
    total, held, tile_sem = rest
    core, x, z, y = place_of(lists)
    tiles = Tiles(lists, 3, call, call == 1, own, sib, held, tile_sem)
    tiles.start()

    def each_chunk(action):
        for out, chunk in zip(outs, chunks):
            if None in chunk:
                side = 1 if chunk[0] is None else 0

                @pl.when(core == side)
                def _(out=out, places=chunk[side]):
                    action(out, places)
            else:
                action(out, [[jnp.where(core == 0, p, q) for p, q in zip(*pair)] for pair in zip(*chunk)])

    def spot_of(dx, dz):
        return ((0 - dx) & (NX - 1)) * NZ + ((0 - dz) & (NZ - 1))

    def clear(out, places):
        for dx, dz in places:
            spot = spot_of(dx, dz)
            total[spot * 2] = jnp.zeros((BLK, WIDTH), F32)
            total[spot * 2 + 1] = jnp.zeros((BLK, WIDTH), F32)

    def emit(out, places):
        for i, (dx, dz) in enumerate(places):
            spot = spot_of(dx, dz)
            first = i * ROWS
            out[first : first + BLK, :] = total[spot * 2].astype(BF16)
            out[first + BLK : first + NODES, :] = total[spot * 2 + 1].astype(BF16)
            column = (x + dx) & (NX - 1)
            level = (z + dz) & (NZ - 1)
            part = ((level >> 1) - y) & (NY - 1)
            out[first + NODES : first + ROWS, :] = weight_sums[part, (level & 1) * NX + column]
        out[4 * ROWS : SUM_ROWS, :] = bias_block(rows_of(chip_bias[...]) if call == 0 else [])

    each_chunk(clear)
    tiles.wait()
    for row, steps, pick in tiles.rows():
        right = scaled[row] if row < 2 else other_scaled[row - 2]

        def step(it, carry):
            left, spots = pick(it)
            terms = lax.dot_general(left, right, (((0,), (0,)), ((), ())), preferred_element_type=F32)
            for u, spot in enumerate(spots):
                total[spot] += terms[u * BLK : (u + 1) * BLK]
            return carry

        lax.fori_loop(0, steps, step, 0)
    each_chunk(emit)


def backward(call, lists, own, sib, scaled, other_scaled, weight_sums, chip_bias):
    shapes = []
    for _ in SCATTER[call]:
        shapes.append(jax.ShapeDtypeStruct((SUM_ROWS, WIDTH), BF16))
    return pl.pallas_call(
        functools.partial(backward_kernel, call),
        out_shape=tuple(shapes),
        in_specs=[smem()] + [anywhere()] * 2 + [vmem()] * 4,
        out_specs=(vmem(),) * len(shapes),
        scratch_shapes=[
            pltpu.VMEM((2 * NX * NZ, BLK, WIDTH), F32),
            pltpu.VMEM((2 * SLOTS + 1, BLK, BLK), BF16),
            pltpu.SemaphoreType.DMA((2 * SLOTS // FETCH,)),
        ],
        compiler_params=pltpu.CompilerParams(vmem_limit_bytes=VMEM),
        cost_estimate=pl.CostEstimate(
            flops=2 * BLK * BLK * WIDTH * len(shapes) * 16, bytes_accessed=len(shapes) * MIB, transcendentals=0
        ),
    )(lists, own, sib, scaled, other_scaled, weight_sums, chip_bias)


def gather(block, core, lists, other_tiles, degree, call):
    p1 = shift(block, Z_UP, X_UP)
    p2 = shift(block, Z_DOWN, X_DOWN)
    p3 = shift(block, Z_UP_2, X_TWO)
    low, other_tiles = lax.optimization_barrier((jnp.stack([block, p1, p2, p3]), other_tiles))
    c1 = shift(low, X_UP, Z_UP)
    c2 = shift(low, X_DOWN, Z_DOWN)
    pa = shift(jnp.stack([low[1], low[3]]), Z_UP_2)
    pb = shift(jnp.stack([low[0], low[2]]), Z_DOWN_2)
    c1, c2, pa, pb, lists, degree = lax.optimization_barrier((c1, c2, pa, pb, lists, degree))
    high = jnp.concatenate([pa, pb], axis=0)
    early = lists, other_tiles
    c3 = shift(c1, X_UP, Z_UP)
    c4 = shift(jnp.where(core == 0, high, c2), X_DOWN, Z_DOWN)
    chunks = [low, c1, c2]
    sums = call(0, early, chunks, ())
    c3, c4, sums = lax.optimization_barrier((c3, c4, sums))
    chunks += [c3, c4, None, None, high]
    sums = call(1, early, chunks, sums)
    c5 = shift(jnp.where(core == 0, high, c3), X_UP, Z_UP)
    c6 = shift(c4, X_DOWN, Z_DOWN)
    c5, c6, sums = lax.optimization_barrier((c5, c6, sums))
    chunks[5:7] = c5, c6
    chunks += [shift(c5[:2], None, Z_UP), shift(c6[2:], None, Z_DOWN)]
    return degree, call(3, early, chunks, call(2, early, chunks, sums))


def add(*values):
    total = values[0].astype(F32)
    for value in values[1:]:
        total = total + value.astype(F32)
    return total


def rows_of(value):
    high = value.astype(BF16)
    middle = (value - high.astype(F32)).astype(BF16)
    low = (value - high.astype(F32) - middle.astype(F32)).astype(BF16)
    return [high.astype(F32), middle.astype(F32), low.astype(F32)]


def bias_block(rows):
    used = sum(row.shape[0] for row in rows)
    rows = rows + [jnp.zeros((BIAS_ROWS - used, WIDTH), F32)]
    return jnp.concatenate(rows, axis=0).astype(BF16)


def joined(block, first=0):
    rows = block.astype(F32)
    return rows[first : first + 1] + rows[first + 1 : first + 2] + rows[first + 2 : first + 3]


def in_order(values, place, held):
    count = len(values)
    for k, value in enumerate(values):
        held[k : k + 1, :] = value
    total = held[pl.ds(place & (count - 1), 1), :]
    for i in range(1, count):
        total = total + held[pl.ds((place - i) & (count - 1), 1), :]
    return total


def block_sum(i, *chunks):
    total = chunks[0][i * ROWS : (i + 1) * ROWS, :].astype(F32)
    for chunk in chunks[1:]:
        total = total + chunk[i * ROWS : (i + 1) * ROWS, :].astype(F32)
    return total


def tail_of(chunk):
    return chunk[4 * ROWS : SUM_ROWS, :]


def pair_kernel(lists, chip_bias, h0, ja1, ja2, jb1, pair_a, pair_b, line_bias, held):
    line = in_order([chip_bias[...], joined(tail_of(ja1)), joined(tail_of(jb1)), joined(tail_of(ja2))], lists[6, 1], held)
    line_bias[...] = line
    rows = bias_block(rows_of(line))
    for pair, first in ((pair_a, 0), (pair_b, 2)):
        for i in range(2):
            pair[i * ROWS : (i + 1) * ROWS, :] = block_sum(first + i, h0, jb1, ja2).astype(BF16)
        pair[2 * ROWS : 2 * ROWS + BIAS_ROWS, :] = rows


def message_kernel(line_bias, h1, jc1, jc2, ra, rb, m1, m2, m3, rest):
    own = rows_of(line_bias[...])
    rest[...] = block_sum(0, h1, jc1, jc2) + block_sum(0, rb)
    relayed = [chunk[2 * ROWS : 2 * ROWS + BIAS_ROWS, :].astype(F32)[0:3] for chunk in (ra, rb)]
    m1[0:ROWS, :] = (block_sum(1, h1, jc1, jc2) + block_sum(0, ra)).astype(BF16)
    m1[ROWS:, :] = bias_block(own + [relayed[0]])
    m2[0:ROWS, :] = (block_sum(2, h1, jc1, jc2) + block_sum(1, rb)).astype(BF16)
    m2[ROWS:, :] = bias_block(own + [relayed[1]])
    m3[0:ROWS, :] = (block_sum(3, h1, jc1, jc2) + block_sum(1, ra)).astype(BF16)
    m3[ROWS:, :] = bias_block(own + [relayed[0]])


def bias_kernel(lists, line_bias, r1, r2, r3, rb, bias, held):
    t1, t2, t3 = (chunk[ROWS:, :] for chunk in (r1, r2, r3))
    tb = rb[2 * ROWS :, :]
    values = [line_bias[...], joined(t1), joined(t3), joined(t1, 3), joined(t3, 3), joined(t2, 3), joined(tb), joined(t2)]
    bias[...] = in_order(values, lists[6, 2], held)


def last_kernel(rest, r1, r2, r3, scaled, feats_grad, weight_grad):
    total = rest[...] + block_sum(0, r1, r2, r3)
    feats_grad[...] = (scaled[...].astype(F32) + total[0:NODES]).astype(BF16)
    weight_grad[...] = total[NODES:ROWS]


def small_call(kernel, shapes, lists, operands, scratch):
    first = [] if lists is None else [lists]
    return pl.pallas_call(
        kernel,
        out_shape=tuple(jax.ShapeDtypeStruct(shape, dtype) for shape, dtype in shapes),
        in_specs=[smem()] * len(first) + [vmem()] * len(operands),
        out_specs=(vmem(),) * len(shapes),
        scratch_shapes=[pltpu.VMEM((8, WIDTH), F32)] * scratch,
        compiler_params=pltpu.CompilerParams(vmem_limit_bytes=16 * MIB),
    )(*first, *operands)


def scatter(parts, weight_sums, core, lists, chip_bias, scaled):
    first_up, x1, x2 = parts(0, weight_sums)
    zero = jnp.zeros((), BF16)
    j0 = shift(first_up, None, Z_UP)
    y1, y2, b1, b2, q1, q2, h0, h1 = parts(1, weight_sums)
    ja1 = shift(jnp.where(core == 0, x1, add(y1, j0).astype(BF16)), X_UP, Z_UP)
    ja2 = shift(jnp.where(core == 0, x2, y2), X_DOWN, Z_DOWN)
    ja1, ja2 = lax.optimization_barrier((ja1, ja2))
    jb1 = shift(add(b1, ja1).astype(BF16), X_UP, Z_UP)
    jb2 = shift(add(b2, jnp.where(core == 0, zero, ja2)).astype(BF16), X_DOWN, Z_DOWN)
    jb1, jb2 = lax.optimization_barrier((jb1, jb2))
    wide = (2 * ROWS + BIAS_ROWS, WIDTH)
    pair_a, pair_b, line_bias = small_call(
        pair_kernel, ((wide, BF16), (wide, BF16), ((1, WIDTH), F32)), lists, (chip_bias, h0, ja1, ja2, jb1), 1
    )
    jc1 = shift(add(q1, jnp.where(core == 0, zero, jb1)).astype(BF16), X_UP, Z_UP)
    jc2 = shift(add(q2, jb2).astype(BF16), X_DOWN, Z_DOWN)
    ra = shift(pair_a, Z_UP_2)
    rb = shift(pair_b, Z_DOWN_2)
    jc1, jc2, ra, rb = lax.optimization_barrier((jc1, jc2, ra, rb))
    size = (ROWS + BIAS_ROWS, WIDTH)
    m1, m2, m3, rest = small_call(
        message_kernel,
        ((size, BF16), (size, BF16), (size, BF16), ((ROWS, WIDTH), F32)),
        None,
        (line_bias, h1, jc1, jc2, ra, rb),
        0,
    )
    r1 = shift(m1, Z_UP, X_UP)
    r2 = shift(m2, Z_DOWN, X_DOWN)
    r3 = shift(m3, Z_UP_2, X_TWO)
    (bias,) = small_call(bias_kernel, (((1, WIDTH), F32),), lists, (line_bias, r1, r2, r3, rb), 1)
    from_core_0 = lax.ppermute(bias, "dom", [(i, i + 1) for i in range(0, NZ * NX * 2, 2)])
    feats_grad, weight_grad = small_call(
        last_kernel, (((NODES, WIDTH), BF16), ((W_ROWS, WIDTH), F32)), None, (rest, r1, r2, r3, scaled), 0
    )
    return feats_grad, weight_grad, jnp.where(core == 0, bias, from_core_0)


def silu_parts(hidden):
    gate_value = jax.nn.sigmoid(hidden)
    return (hidden * gate_value, gate_value * (1.0 + hidden * (1.0 - gate_value)))


def on_device(feats, weight, bias, tile_values, tile_rows, tile_cols, tile_live, cotangent):
    dom = lax.axis_index("dom")
    y = lax.axis_index("feat")
    core = dom % 2
    x = (dom // 2) % NX
    z = dom // (2 * NX)

    meta = jnp.stack([tile_rows, tile_cols, jnp.broadcast_to(tile_live, (SLOTS,))])
    other_meta = swap(meta, 1)
    place = jnp.stack([core, x, z, y, tile_live[0], other_meta[2, 0]]).astype(jnp.int32)
    lists = make_lists(place, meta, other_meta)

    own_live = jnp.arange(SLOTS, dtype=jnp.int32) < tile_live[0]
    row_sums = jnp.sum(tile_values, axis=2, dtype=F32)
    degree = 1.0 + jnp.concatenate(
        [
            jnp.sum(jnp.where((own_live & (tile_rows == row))[:, None], row_sums, 0.0), axis=0)
            for row in range(2)
        ]
    ).reshape(NODES, 1)

    other_tiles = swap(tile_values, 1)
    degree, (sums, other_sums, weight_lane) = gather(
        jnp.concatenate([feats, weight.T], axis=0),
        core,
        lists,
        other_tiles,
        degree,
        lambda call, early, chunks, before: forward(call, early[0], tile_values, early[1], chunks, before),
    )
    neighbour_sum = (sums + swap(other_sums, 1)).reshape(NODES, WIDTH)
    weight_other = swap(weight_lane, 1)
    mixed = ((feats.astype(F32) + neighbour_sum) / degree).astype(BF16)

    first = jnp.where(core == 0, weight_lane, weight_other)
    second = jnp.where(core == 0, weight_other, weight_lane)
    weight_t = jnp.stack([first, second], axis=2).reshape(NY, WIDTH, WIDTH)

    def hidden_part(dy):
        return lax.dot_general(mixed, weight_t[dy], (((1,), (1,)), ((), ())), preferred_element_type=F32)

    hidden = add(
        hidden_part(0),
        y_shift(hidden_part(1).astype(BF16), 1),
        y_shift(hidden_part(2).astype(BF16), 2),
        y_shift(hidden_part(3).astype(BF16), 3),
    ) + bias
    activated, slope = silu_parts(hidden)
    output = activated.astype(BF16)
    dz_full = cotangent.astype(F32) * slope
    dz_own = dz_full.astype(BF16)
    dz_parts = [dz_own] + [y_shift(dz_own, NY - dy) for dy in range(1, NY)]

    dmixed = sum(jnp.dot(dz_parts[dy], weight_t[dy], preferred_element_type=F32) for dy in range(NY))
    scaled = (dmixed / degree).astype(BF16)
    scaled_blocks = [value.reshape(2, BLK, WIDTH) for value in (scaled, swap(scaled, 1))]

    weight_part = jnp.stack(
        [
            lax.dot_general(dz_parts[dy], mixed, (((0,), (0,)), ((), ())), preferred_element_type=F32)
            for dy in range(NY)
        ]
    ).reshape(NY, 2 * NX, 2, W_ROWS, WIDTH)
    mine = jnp.where(core == 0, weight_part[:, :, 0], weight_part[:, :, 1])
    others = jnp.where(core == 0, weight_part[:, :, 1], weight_part[:, :, 0])
    bias_part = jnp.sum(dz_full, axis=0, keepdims=True)
    sent = jnp.concatenate([others.reshape(-1, WIDTH), jnp.pad(bias_part, ((0, 7), (0, 0)))], axis=0)
    got = swap(sent, 1)
    weight_sums = (mine + got[:-8].reshape(mine.shape)).astype(BF16)

    chip_bias = bias_part + got[-8:-7]

    def parts(call, weight_sums):
        return backward(call, lists, tile_values, other_tiles, *scaled_blocks, weight_sums, chip_bias)

    feats_grad, weight_sum, bias_grad = scatter(parts, weight_sums, core, lists, chip_bias, scaled)
    return (output, feats_grad, weight_sum.T, bias_grad.reshape(WIDTH))


def solution(mesh):
    return jax.shard_map(
        on_device,
        mesh=mesh,
        in_specs=(
            P("dom", "feat"),
            P("feat", "dom"),
            P("feat"),
            P("dom", None, None),
            P("dom"),
            P("dom"),
            P("dom"),
            P("dom", "feat"),
        ),
        out_specs=(P("dom", "feat"), P("dom", "feat"), P("feat", "dom"), P("feat")),
        check_vma=False,
    )
```

```python
import functools

import jax
import jax.numpy as jnp
from jax import lax
from jax.experimental import pallas as pl
from jax.experimental.pallas import tpu as pltpu
from jax.sharding import PartitionSpec as P

F32 = jnp.float32
BF16 = jnp.bfloat16
NZ, NX, NY = 8, 4, 4
BLK = 128
SLOTS = 128
WIDTH = 256
NODES = 2 * BLK
W_ROWS = 16
ROWS = NODES + W_ROWS
UNROLL = 8
FETCH = 16
BIAS_ROWS = 16
SUM_ROWS = 4 * ROWS + BIAS_ROWS
MIB = 1 << 20
VMEM = 54 * MIB

LOW, HIGH, ACROSS = (0, 1, 7, 2), (3, 4, 6, 5), (0, 1, 3, 2)
GATHER_0 = tuple(
    tuple(k * NZ + j for j in group)
    for k, group in ((0, LOW), (1, LOW), (3, LOW), (2, LOW), (3, HIGH), (1, HIGH), (2, HIGH), (0, HIGH))
)
GATHER_1 = tuple(tuple(k * NZ + j for k in ACROSS) for j in (0, 1, 7, 2, 6, 3, 5)) + (
    None,
    tuple(k * NZ + 4 for k in ACROSS[:2]),
    tuple(k * NZ + 4 for k in ACROSS[2:]),
)
FORWARD_CHUNKS = ((0, 1, 2), (3, 4, 7), (5, 6), (8, 9))
SCATTER = (
    (
        (None, tuple((dx, 4) for dx in ACROSS)),
        (tuple((2, dz) for dz in HIGH), None),
        (tuple((3, dz) for dz in HIGH), None),
    ),
    (
        (None, tuple((dx, 3) for dx in ACROSS)),
        (None, tuple((dx, 5) for dx in ACROSS)),
        (tuple((1, dz) for dz in HIGH), tuple((dx, 2) for dx in ACROSS)),
        (tuple((2, dz) for dz in LOW), tuple((dx, 6) for dx in ACROSS)),
        (tuple((1, dz) for dz in LOW), tuple((dx, 1) for dx in ACROSS)),
        (tuple((3, dz) for dz in LOW), tuple((dx, 7) for dx in ACROSS)),
        (tuple((0, dz) for dz in HIGH), None),
        (tuple((0, dz) for dz in LOW), tuple((dx, 0) for dx in ACROSS)),
    ),
)


def shift(value, core_0=None, core_1=None):
    pairs = []
    for z in range(NZ):
        for x in range(NX):
            for core, step in enumerate((core_0, core_1)):
                if step is not None:
                    target = ((z + step[0]) % NZ * NX + (x + step[1]) % NX) * 2 + core
                    pairs.append(((z * NX + x) * 2 + core, target))
    return lax.ppermute(value, "dom", pairs)


Z_UP, Z_DOWN, Z_UP_2, Z_DOWN_2 = (1, 0), (-1, 0), (2, 0), (-2, 0)
X_UP, X_DOWN, X_TWO = (0, 1), (0, -1), (0, 2)


def swap(value, bit):
    return lax.ppermute(value, "dom", [(i, i ^ bit) for i in range(NZ * NX * 2)])


def y_shift(value, dy):
    return lax.ppermute(value, "feat", [(y, (y + dy) % NY) for y in range(NY)])


def smem():
    return pl.BlockSpec(memory_space=pltpu.SMEM)


def vmem():
    return pl.BlockSpec(memory_space=pltpu.VMEM)


def anywhere():
    return pl.BlockSpec(memory_space=pl.ANY)


def list_kernel(place, own, sib, lists):
    core, x, z = place[0], place[1], place[2]
    wide = (1, 2 * SLOTS)
    column = jnp.concatenate([own[1:2], sib[1:2]], axis=1)
    row = jnp.concatenate([own[0:1], sib[0:1] + 2], axis=1)
    slot = lax.broadcasted_iota(jnp.int32, wide, 1)
    live = slot < jnp.where(slot < SLOTS, place[4], SLOTS + place[5])
    owner = column >> 1
    chip = owner >> 1
    k = (x - (chip & (NX - 1))) & (NX - 1)
    j = (z - (chip >> 2)) & (NZ - 1)
    spot = (k * NZ + j) * 2 + (column & 1)
    mine = live & ((owner & 1) == core)
    high, back = (j >= 3) & (j <= 6), (j >= 2) & (j <= 5)
    on_0 = jnp.where(high, jnp.where((k == 1) | (k == 2), 2, 1), jnp.where(k == 2, 1, 0))
    on_1 = jnp.where(j == 4, 3, jnp.where((j == 3) | (j == 5), 2, jnp.where((j == 2) | (j == 6), 1, 0)))
    forward_call = jnp.where(core == 0, on_0, on_1)
    backward_call = jnp.where(core == 0, jnp.where(back & ((k == 1) | (k == 2)), 0, 1), jnp.where(j == 4, 0, 1))
    square = (2 * SLOTS, 2 * SLOTS)
    first = lax.broadcasted_iota(jnp.int32, square, 0)
    second = lax.broadcasted_iota(jnp.int32, square, 1)
    up_to = jnp.where(first <= second, 1.0, 0.0).astype(BF16)
    group_of = lax.broadcasted_iota(jnp.int32, (16, 2 * SLOTS), 0)
    lane = lax.broadcasted_iota(jnp.int32, (16, 2 * SLOTS), 1)
    before = jnp.where(
        lax.broadcasted_iota(jnp.int32, (16, 16), 1) < lax.broadcasted_iota(jnp.int32, (16, 16), 0), 1.0, 0.0
    ).astype(BF16)
    values = jnp.concatenate([slot, spot], axis=0).astype(F32)
    values = jnp.concatenate([values, jnp.zeros((14, 2 * SLOTS), F32)], axis=0).astype(BF16)
    lists[...] = jnp.zeros_like(lists)
    for at, call in ((0, forward_call), (3, backward_call)):
        group = jnp.where(mine, call * 4 + row, -1)
        member = jnp.where(group_of == group, 1.0, 0.0)
        rank = jnp.dot(member.astype(BF16), up_to, preferred_element_type=F32)
        counts = jnp.sum(member, axis=1, keepdims=True)
        earlier = jnp.dot(before, member.astype(BF16), preferred_element_type=F32)
        starts = jnp.sum(earlier, axis=1, keepdims=True)
        goal = jnp.sum(member * (starts + rank), axis=0, keepdims=True).astype(jnp.int32) - 1
        moved = jnp.where(first == goal, 1.0, 0.0).astype(BF16)
        ordered = lax.dot_general(values, moved, (((1,), (1,)), ((), ())), preferred_element_type=F32)
        lists[at : at + 1, :] = jnp.sum(jnp.where(group_of == lane, counts, 0.0), axis=0, keepdims=True).astype(jnp.int32)
        lists[at + 1 : at + 2, :] = jnp.sum(jnp.where(group_of == lane, starts, 0.0), axis=0, keepdims=True).astype(jnp.int32)
        lists[at + 2 : at + 3, :] = (ordered[0:1] * 64.0 + ordered[1:2]).astype(jnp.int32)
    told = jnp.zeros(wide, jnp.int32)
    for i in range(6):
        told = jnp.where(slot == i, place[i], told)
    lists[6:7, :] = told


def make_lists(place, own, sib):
    return pl.pallas_call(
        list_kernel,
        out_shape=jax.ShapeDtypeStruct((8, 2 * SLOTS), jnp.int32),
        in_specs=[smem(), vmem(), vmem()],
        out_specs=vmem(),
    )(place, own, sib)


def place_of(lists):
    return [lists[6, i] for i in range(4)]


def copy_each(copies, action):
    for condition, copy in copies:
        call = getattr(copy, action)
        if condition is None:
            call()
        else:
            pl.when(condition)(call)


class Tiles:
    def __init__(self, lists, at, call, every, own, sib, held, sem):
        self.lists, self.at, self.call, self.every = lists, at, call, every
        self.own, self.sib, self.held, self.sem = own, sib, held, sem
        self.begin = lists[at + 1, call * 4]
        self.end = lists[at + 1, call * 4 + 3] + lists[at, call * 4 + 3]

    def bulk(self):
        copies = []
        for which, source in enumerate((self.own, self.sib)):
            for step in range(SLOTS // FETCH):
                first = step * FETCH
                copy = pltpu.make_async_copy(
                    source.at[pl.ds(first, FETCH)],
                    self.held.at[pl.ds(which * SLOTS + first, FETCH)],
                    self.sem.at[which * (SLOTS // FETCH) + step],
                )
                copies.append((first < self.lists[6, 4 + which], copy))
        return copies

    def each(self, action):
        def step(p, carry):
            slot = self.lists[self.at + 2, p] >> 6
            goal = self.held.at[p]

            @pl.when(slot < SLOTS)
            def _():
                getattr(pltpu.make_async_copy(self.own.at[jnp.minimum(slot, SLOTS - 1)], goal, self.sem.at[0]), action)()

            @pl.when(slot >= SLOTS)
            def _():
                getattr(pltpu.make_async_copy(self.sib.at[jnp.maximum(slot - SLOTS, 0)], goal, self.sem.at[0]), action)()

            return carry

        lax.fori_loop(self.begin, self.end, step, 0)

    def start(self):
        if self.every:
            copy_each(self.bulk(), "start")
        else:
            self.each("start")
        self.held[2 * SLOTS] = jnp.zeros((BLK, BLK), BF16)

    def wait(self):
        if self.every:
            copy_each(self.bulk(), "wait")
        else:
            self.each("wait")

    def rows(self):
        for row in range(4):
            group = self.call * 4 + row
            number, first = self.lists[self.at, group], self.lists[self.at + 1, group]

            def pick(it, number=number, first=first):
                lefts, spots = [], []
                for u in range(UNROLL):
                    p = it * UNROLL + u
                    entry = self.lists[self.at + 2, first + jnp.minimum(p, number - 1)]
                    place = entry >> 6 if self.every else first + p
                    lefts.append(self.held[jnp.where(p < number, place, 2 * SLOTS)])
                    spots.append(entry & 63)
                return jnp.concatenate(lefts, axis=1), spots

            yield row, lax.div(number + (UNROLL - 1), UNROLL), pick


def forward_kernel(call, lists, own, sib, *rest):
    chosen = FORWARD_CHUNKS[call]
    chunks, rest = rest[: len(chosen)], rest[len(chosen) :]
    if call:
        own_before, sib_before, weight_before, *rest = rest
    own_sums, sib_sums, weight_out, blocks, held, sem, tile_sem = rest
    core, x, z, y = place_of(lists)
    tiles = Tiles(lists, 0, call, False, own, sib, held, tile_sem)
    tiles.start()
    copies, arrived = [], []
    for n, chunk in zip(chosen, chunks):
        condition = None if n < 7 else core == (0 if n == 7 else 1)
        for i in range(chunk.shape[0]):
            if n < 7:
                spot = jnp.where(core == 0, GATHER_0[n][i], GATHER_1[n][i])
            else:
                spot = GATHER_0[n][i] if n == 7 else GATHER_1[n][i]
            copies.append((condition, pltpu.make_async_copy(chunk.at[i], blocks.at[spot], sem.at[len(copies)])))
            arrived.append((condition, spot))
    copy_each(copies, "start")
    copy_each(copies, "wait")
    tiles.wait()
    for row, steps, pick in tiles.rows():

        def step(it, total):
            left, spots = pick(it)
            rights = []
            for spot in spots:
                first = pl.multiple_of((spot & 1) * BLK, BLK)
                rights.append(blocks[spot >> 1, pl.ds(first, BLK), :])
            return total + jnp.dot(left, jnp.concatenate(rights, axis=0), preferred_element_type=F32)

        sums, at = (own_sums, row) if row < 2 else (sib_sums, row - 2)
        before = jnp.zeros((BLK, WIDTH), F32)
        if call:
            before = own_before[at] if row < 2 else sib_before[at]
        sums[at] = lax.fori_loop(0, steps, step, before)
    if call:
        weight_out[...] = weight_before[...]
    for condition, spot in arrived:

        def keep(spot=spot):
            column = (x - (spot >> 3)) & (NX - 1)
            level = (z - spot) & (NZ - 1)
            part = ((level >> 1) - y) & (NY - 1)
            weight_out[part, (level & 1) * NX + column] = blocks[spot, NODES:ROWS, :]

        if condition is None:
            keep()
        else:
            pl.when(condition)(keep)


def forward(call, lists, own, sib, chunks, before):
    chosen = [chunks[n] for n in FORWARD_CHUNKS[call]]
    return pl.pallas_call(
        functools.partial(forward_kernel, call),
        out_shape=(
            jax.ShapeDtypeStruct((2, BLK, WIDTH), F32),
            jax.ShapeDtypeStruct((2, BLK, WIDTH), F32),
            jax.ShapeDtypeStruct((NY, 2 * NX, W_ROWS, WIDTH), BF16),
        ),
        in_specs=[smem()] + [anywhere()] * (2 + len(chosen)) + [vmem()] * len(before),
        out_specs=(vmem(),) * 3,
        scratch_shapes=[
            pltpu.VMEM((NX * NZ, ROWS, WIDTH), BF16),
            pltpu.VMEM((2 * SLOTS + 1, BLK, BLK), BF16),
            pltpu.SemaphoreType.DMA((32,)),
            pltpu.SemaphoreType.DMA((2 * SLOTS // FETCH,)),
        ],
        compiler_params=pltpu.CompilerParams(vmem_limit_bytes=VMEM),
        cost_estimate=pl.CostEstimate(
            flops=2 * BLK * BLK * WIDTH * len(chosen) * 16, bytes_accessed=len(chosen) * MIB, transcendentals=0
        ),
    )(lists, own, sib, *chosen, *before)


def backward_kernel(call, lists, own, sib, scaled, other_scaled, weight_sums, chip_bias, *rest):
    chunks = SCATTER[call]
    outs, rest = rest[: len(chunks)], rest[len(chunks) :]
    total, held, tile_sem = rest
    core, x, z, y = place_of(lists)
    tiles = Tiles(lists, 3, call, call == 1, own, sib, held, tile_sem)
    tiles.start()

    def each_chunk(action):
        for out, chunk in zip(outs, chunks):
            if None in chunk:
                side = 1 if chunk[0] is None else 0

                @pl.when(core == side)
                def _(out=out, places=chunk[side]):
                    action(out, places)
            else:
                action(out, [[jnp.where(core == 0, p, q) for p, q in zip(*pair)] for pair in zip(*chunk)])

    def spot_of(dx, dz):
        return ((0 - dx) & (NX - 1)) * NZ + ((0 - dz) & (NZ - 1))

    def clear(out, places):
        for dx, dz in places:
            spot = spot_of(dx, dz)
            total[spot * 2] = jnp.zeros((BLK, WIDTH), F32)
            total[spot * 2 + 1] = jnp.zeros((BLK, WIDTH), F32)

    def emit(out, places):
        for i, (dx, dz) in enumerate(places):
            spot = spot_of(dx, dz)
            first = i * ROWS
            out[first : first + BLK, :] = total[spot * 2].astype(BF16)
            out[first + BLK : first + NODES, :] = total[spot * 2 + 1].astype(BF16)
            column = (x + dx) & (NX - 1)
            level = (z + dz) & (NZ - 1)
            part = ((level >> 1) - y) & (NY - 1)
            out[first + NODES : first + ROWS, :] = weight_sums[part, (level & 1) * NX + column]
        out[4 * ROWS : SUM_ROWS, :] = bias_block(rows_of(chip_bias[...]) if call == 0 else [])

    each_chunk(clear)
    tiles.wait()
    for row, steps, pick in tiles.rows():
        right = scaled[row] if row < 2 else other_scaled[row - 2]

        def step(it, carry):
            left, spots = pick(it)
            terms = lax.dot_general(left, right, (((0,), (0,)), ((), ())), preferred_element_type=F32)
            for u, spot in enumerate(spots):
                total[spot] += terms[u * BLK : (u + 1) * BLK]
            return carry

        lax.fori_loop(0, steps, step, 0)
    each_chunk(emit)


def backward(call, lists, own, sib, scaled, other_scaled, weight_sums, chip_bias):
    shapes = []
    for _ in SCATTER[call]:
        shapes.append(jax.ShapeDtypeStruct((SUM_ROWS, WIDTH), BF16))
    return pl.pallas_call(
        functools.partial(backward_kernel, call),
        out_shape=tuple(shapes),
        in_specs=[smem()] + [anywhere()] * 2 + [vmem()] * 4,
        out_specs=(vmem(),) * len(shapes),
        scratch_shapes=[
            pltpu.VMEM((2 * NX * NZ, BLK, WIDTH), F32),
            pltpu.VMEM((2 * SLOTS + 1, BLK, BLK), BF16),
            pltpu.SemaphoreType.DMA((2 * SLOTS // FETCH,)),
        ],
        compiler_params=pltpu.CompilerParams(vmem_limit_bytes=44 * MIB),
        cost_estimate=pl.CostEstimate(
            flops=2 * BLK * BLK * WIDTH * len(shapes) * 16, bytes_accessed=len(shapes) * MIB, transcendentals=0
        ),
    )(lists, own, sib, scaled, other_scaled, weight_sums, chip_bias)


def gather(block, core, lists, other_tiles, degree, call):
    p1 = shift(block, Z_UP, X_UP)
    p2 = shift(block, Z_DOWN, X_DOWN)
    p3 = shift(block, Z_UP_2, X_TWO)
    low, other_tiles = lax.optimization_barrier((jnp.stack([block, p1, p2, p3]), other_tiles))
    c1 = shift(low, X_UP, Z_UP)
    c2 = shift(low, X_DOWN, Z_DOWN)
    pa = shift(jnp.stack([low[1], low[3]]), Z_UP_2)
    pb = shift(jnp.stack([low[0], low[2]]), Z_DOWN_2)
    c1, c2, pa, pb, lists, degree = lax.optimization_barrier((c1, c2, pa, pb, lists, degree))
    high = jnp.concatenate([pa, pb], axis=0)
    early = lists, other_tiles
    c3 = shift(c1, X_UP, Z_UP)
    c4 = shift(jnp.where(core == 0, high, c2), X_DOWN, Z_DOWN)
    chunks = [low, c1, c2]
    sums = call(0, early, chunks, ())
    c3, c4, sums = lax.optimization_barrier((c3, c4, sums))
    chunks += [c3, c4, None, None, high]
    sums = call(1, early, chunks, sums)
    c5 = shift(jnp.where(core == 0, high, c3), X_UP, Z_UP)
    c6 = shift(c4, X_DOWN, Z_DOWN)
    c5, c6, sums = lax.optimization_barrier((c5, c6, sums))
    chunks[5:7] = c5, c6
    chunks += [shift(c5[:2], None, Z_UP), shift(c6[2:], None, Z_DOWN)]
    return degree, call(3, early, chunks, call(2, early, chunks, sums))


def add(*values):
    total = values[0].astype(F32)
    for value in values[1:]:
        total = total + value.astype(F32)
    return total


def rows_of(value):
    high = value.astype(BF16)
    middle = (value - high.astype(F32)).astype(BF16)
    low = (value - high.astype(F32) - middle.astype(F32)).astype(BF16)
    return [high.astype(F32), middle.astype(F32), low.astype(F32)]


def bias_block(rows):
    used = sum(row.shape[0] for row in rows)
    rows = rows + [jnp.zeros((BIAS_ROWS - used, WIDTH), F32)]
    return jnp.concatenate(rows, axis=0).astype(BF16)


def joined(block, first=0):
    rows = block.astype(F32)
    return rows[first : first + 1] + rows[first + 1 : first + 2] + rows[first + 2 : first + 3]


def in_order(values, place, held):
    count = len(values)
    for k, value in enumerate(values):
        held[k : k + 1, :] = value
    total = held[pl.ds(place & (count - 1), 1), :]
    for i in range(1, count):
        total = total + held[pl.ds((place - i) & (count - 1), 1), :]
    return total


def block_sum(i, *chunks):
    total = chunks[0][i * ROWS : (i + 1) * ROWS, :].astype(F32)
    for chunk in chunks[1:]:
        total = total + chunk[i * ROWS : (i + 1) * ROWS, :].astype(F32)
    return total


def tail_of(chunk):
    return chunk[4 * ROWS : SUM_ROWS, :]


def pair_kernel(lists, chip_bias, h0, ja1, ja2, jb1, pair_a, pair_b, line_bias, held):
    line = in_order([chip_bias[...], joined(tail_of(ja1)), joined(tail_of(jb1)), joined(tail_of(ja2))], lists[6, 1], held)
    line_bias[...] = line
    rows = bias_block(rows_of(line))
    for pair, first in ((pair_a, 0), (pair_b, 2)):
        for i in range(2):
            pair[i * ROWS : (i + 1) * ROWS, :] = block_sum(first + i, h0, jb1, ja2).astype(BF16)
        pair[2 * ROWS : 2 * ROWS + BIAS_ROWS, :] = rows


def message_kernel(line_bias, h1, jc1, jc2, ra, rb, m1, m2, m3, rest):
    own = rows_of(line_bias[...])
    rest[...] = block_sum(0, h1, jc1, jc2) + block_sum(0, rb)
    relayed = [chunk[2 * ROWS : 2 * ROWS + BIAS_ROWS, :].astype(F32)[0:3] for chunk in (ra, rb)]
    m1[0:ROWS, :] = (block_sum(1, h1, jc1, jc2) + block_sum(0, ra)).astype(BF16)
    m1[ROWS:, :] = bias_block(own + [relayed[0]])
    m2[0:ROWS, :] = (block_sum(2, h1, jc1, jc2) + block_sum(1, rb)).astype(BF16)
    m2[ROWS:, :] = bias_block(own + [relayed[1]])
    m3[0:ROWS, :] = (block_sum(3, h1, jc1, jc2) + block_sum(1, ra)).astype(BF16)
    m3[ROWS:, :] = bias_block(own + [relayed[0]])


def bias_kernel(lists, line_bias, r1, r2, r3, rb, bias, held):
    t1, t2, t3 = (chunk[ROWS:, :] for chunk in (r1, r2, r3))
    tb = rb[2 * ROWS :, :]
    values = [line_bias[...], joined(t1), joined(t3), joined(t1, 3), joined(t3, 3), joined(t2, 3), joined(tb), joined(t2)]
    bias[...] = in_order(values, lists[6, 2], held)


def last_kernel(rest, r1, r2, r3, scaled, feats_grad, weight_grad):
    total = rest[...] + block_sum(0, r1, r2, r3)
    feats_grad[...] = (scaled[...].astype(F32) + total[0:NODES]).astype(BF16)
    weight_grad[...] = total[NODES:ROWS]


def small_call(kernel, shapes, lists, operands, scratch):
    first = [] if lists is None else [lists]
    return pl.pallas_call(
        kernel,
        out_shape=tuple(jax.ShapeDtypeStruct(shape, dtype) for shape, dtype in shapes),
        in_specs=[smem()] * len(first) + [vmem()] * len(operands),
        out_specs=(vmem(),) * len(shapes),
        scratch_shapes=[pltpu.VMEM((8, WIDTH), F32)] * scratch,
        compiler_params=pltpu.CompilerParams(vmem_limit_bytes=16 * MIB),
    )(*first, *operands)


def scatter(parts, weight_sums, core, lists, chip_bias, scaled):
    first_up, x1, x2 = parts(0, weight_sums)
    zero = jnp.zeros((), BF16)
    j0 = shift(first_up, None, Z_UP)
    y1, y2, b1, b2, q1, q2, h0, h1 = parts(1, weight_sums)
    ja1 = shift(jnp.where(core == 0, x1, add(y1, j0).astype(BF16)), X_UP, Z_UP)
    ja2 = shift(jnp.where(core == 0, x2, y2), X_DOWN, Z_DOWN)
    ja1, ja2 = lax.optimization_barrier((ja1, ja2))
    jb1 = shift(add(b1, ja1).astype(BF16), X_UP, Z_UP)
    jb2 = shift(add(b2, jnp.where(core == 0, zero, ja2)).astype(BF16), X_DOWN, Z_DOWN)
    jb1, jb2 = lax.optimization_barrier((jb1, jb2))
    wide = (2 * ROWS + BIAS_ROWS, WIDTH)
    pair_a, pair_b, line_bias = small_call(
        pair_kernel, ((wide, BF16), (wide, BF16), ((1, WIDTH), F32)), lists, (chip_bias, h0, ja1, ja2, jb1), 1
    )
    jc1 = shift(add(q1, jnp.where(core == 0, zero, jb1)).astype(BF16), X_UP, Z_UP)
    jc2 = shift(add(q2, jb2).astype(BF16), X_DOWN, Z_DOWN)
    ra = shift(pair_a, Z_UP_2)
    rb = shift(pair_b, Z_DOWN_2)
    jc1, jc2, ra, rb = lax.optimization_barrier((jc1, jc2, ra, rb))
    size = (ROWS + BIAS_ROWS, WIDTH)
    m1, m2, m3, rest = small_call(
        message_kernel,
        ((size, BF16), (size, BF16), (size, BF16), ((ROWS, WIDTH), F32)),
        None,
        (line_bias, h1, jc1, jc2, ra, rb),
        0,
    )
    r1 = shift(m1, Z_UP, X_UP)
    r2 = shift(m2, Z_DOWN, X_DOWN)
    r3 = shift(m3, Z_UP_2, X_TWO)
    (bias,) = small_call(bias_kernel, (((1, WIDTH), F32),), lists, (line_bias, r1, r2, r3, rb), 1)
    from_core_0 = lax.ppermute(bias, "dom", [(i, i + 1) for i in range(0, NZ * NX * 2, 2)])
    feats_grad, weight_grad = small_call(
        last_kernel, (((NODES, WIDTH), BF16), ((W_ROWS, WIDTH), F32)), None, (rest, r1, r2, r3, scaled), 0
    )
    return feats_grad, weight_grad, jnp.where(core == 0, bias, from_core_0)


def silu_parts(hidden):
    gate_value = jax.nn.sigmoid(hidden)
    return (hidden * gate_value, gate_value * (1.0 + hidden * (1.0 - gate_value)))


def on_device(feats, weight, bias, tile_values, tile_rows, tile_cols, tile_live, cotangent):
    dom = lax.axis_index("dom")
    y = lax.axis_index("feat")
    core = dom % 2
    x = (dom // 2) % NX
    z = dom // (2 * NX)

    meta = jnp.stack([tile_rows, tile_cols, jnp.broadcast_to(tile_live, (SLOTS,))])
    other_meta = swap(meta, 1)
    place = jnp.stack([core, x, z, y, tile_live[0], other_meta[2, 0]]).astype(jnp.int32)
    lists = make_lists(place, meta, other_meta)

    own_live = jnp.arange(SLOTS, dtype=jnp.int32) < tile_live[0]
    row_sums = jnp.sum(tile_values, axis=2, dtype=F32)
    degree = 1.0 + jnp.concatenate(
        [
            jnp.sum(jnp.where((own_live & (tile_rows == row))[:, None], row_sums, 0.0), axis=0)
            for row in range(2)
        ]
    ).reshape(NODES, 1)

    other_tiles = swap(tile_values, 1)
    degree, (sums, other_sums, weight_lane) = gather(
        jnp.concatenate([feats, weight.T], axis=0),
        core,
        lists,
        other_tiles,
        degree,
        lambda call, early, chunks, before: forward(call, early[0], tile_values, early[1], chunks, before),
    )
    neighbour_sum = (sums + swap(other_sums, 1)).reshape(NODES, WIDTH)
    weight_other = swap(weight_lane, 1)
    mixed = ((feats.astype(F32) + neighbour_sum) / degree).astype(BF16)

    first = jnp.where(core == 0, weight_lane, weight_other)
    second = jnp.where(core == 0, weight_other, weight_lane)
    weight_t = jnp.stack([first, second], axis=2).reshape(NY, WIDTH, WIDTH)

    def hidden_part(dy):
        return lax.dot_general(mixed, weight_t[dy], (((1,), (1,)), ((), ())), preferred_element_type=F32)

    hidden = add(
        hidden_part(0),
        y_shift(hidden_part(1).astype(BF16), 1),
        y_shift(hidden_part(2).astype(BF16), 2),
        y_shift(hidden_part(3).astype(BF16), 3),
    ) + bias
    activated, slope = silu_parts(hidden)
    output = activated.astype(BF16)
    dz_full = cotangent.astype(F32) * slope
    dz_own = dz_full.astype(BF16)
    dz_parts = [dz_own] + [y_shift(dz_own, NY - dy) for dy in range(1, NY)]

    dmixed = sum(jnp.dot(dz_parts[dy], weight_t[dy], preferred_element_type=F32) for dy in range(NY))
    scaled = (dmixed / degree).astype(BF16)
    scaled_blocks = [value.reshape(2, BLK, WIDTH) for value in (scaled, swap(scaled, 1))]

    weight_part = jnp.stack(
        [
            lax.dot_general(dz_parts[dy], mixed, (((0,), (0,)), ((), ())), preferred_element_type=F32)
            for dy in range(NY)
        ]
    ).reshape(NY, 2 * NX, 2, W_ROWS, WIDTH)
    mine = jnp.where(core == 0, weight_part[:, :, 0], weight_part[:, :, 1])
    others = jnp.where(core == 0, weight_part[:, :, 1], weight_part[:, :, 0])
    bias_part = jnp.sum(dz_full, axis=0, keepdims=True)
    sent = jnp.concatenate([others.reshape(-1, WIDTH), jnp.pad(bias_part, ((0, 7), (0, 0)))], axis=0)
    got = swap(sent, 1)
    weight_sums = (mine + got[:-8].reshape(mine.shape)).astype(BF16)

    chip_bias = bias_part + got[-8:-7]

    def parts(call, weight_sums):
        return backward(call, lists, tile_values, other_tiles, *scaled_blocks, weight_sums, chip_bias)

    feats_grad, weight_sum, bias_grad = scatter(parts, weight_sums, core, lists, chip_bias, scaled)
    return (output, feats_grad, weight_sum.T, bias_grad.reshape(WIDTH))


def solution(mesh):
    return jax.shard_map(
        on_device,
        mesh=mesh,
        in_specs=(
            P("dom", "feat"),
            P("feat", "dom"),
            P("feat"),
            P("dom", None, None),
            P("dom"),
            P("dom"),
            P("dom"),
            P("dom", "feat"),
        ),
        out_specs=(P("dom", "feat"), P("dom", "feat"), P("feat", "dom"), P("feat")),
        check_vma=False,
    )
```
